32 devices in a mesh: dp: 8 (over z, y), tensor: 4 (over x, core).
Axes of the slice: x: 2, y: 2, z: 4, core: 2. Of those that a mesh axis runs over, the one named last changes fastest.
Arguments:
- block_input: bfloat16 [7680, 1536], P('dp'), may hold values from -6 to 6
- norm1_gain: float32 [1536], replicated, may hold values from 0.1 to 1.9
- query_weight: bfloat16 [1536, 1536], P(None, 'tensor'), may hold values from -0.15625 to 0.15625
- keyvalue_weight: bfloat16 [1536, 256], replicated, may hold values from -0.15625 to 0.15625
- out_weight: bfloat16 [1536, 1536], P('tensor'), may hold values from -0.625 to 0.625
- norm2_gain: float32 [1536], replicated, may hold values from 0.1 to 1.9
- gate_up_weight: bfloat16 [2, 1536, 4608], P(None, None, 'tensor'), may hold values from -0.15625 to 0.15625
- down_weight: bfloat16 [4608, 1536], P('tensor'), may hold values from -0.1875 to 0.1875
- cotangent: bfloat16 [7680, 1536], P('dp'), may hold values from -6 to 6
Outputs:
- block_output: bfloat16 [7680, 1536], P('dp')
- input_grad: bfloat16 [7680, 1536], P('dp')
- norm1_grad: float32 [1536], replicated
- query_grad: float32 [1536, 1536], P(None, 'tensor')
- keyvalue_grad: float32 [1536, 256], replicated
- out_grad: float32 [1536, 1536], P('tensor')
- norm2_grad: float32 [1536], replicated
- gate_up_grad: float32 [2, 1536, 4608], P(None, None, 'tensor')
- down_grad: float32 [4608, 1536], P('tensor')
The draws below stay inside these ranges and needn't reach their ends.
All inputs are finite; a program needn't handle non-finite values.
Results may differ from the reference program's by a relative error of at most 0.025.
Values may be sent and summed in bfloat16 or wider, within the bound.
No kernel may reach another device: no remote copies, remote signals or barrier semaphores. Data moves between devices by JAX's collectives and lax.ppermute only.
A program may use at most 192 MiB of HBM per device.

```python
import math
import jax
import jax.numpy as jnp
from jax import lax

D = 1536
HEADS = 12
HEAD_DIM = 128
FF = 4608
WINDOW = 1024
TOK_DEV = 960
TOKENS = 7680
N_DP = 8
N_TENSOR = 4


def spiked(values, stream_key, source, target, parts, factor):
    def block_of(dim):
        return (jnp.arange(values.shape[dim]) // (values.shape[dim] // parts)).reshape((-1,) + (1,) * (values.ndim - 1 - dim))

    first = jax.random.permutation(stream_key, parts)[block_of(target)]
    other_side = (block_of(target) + parts // 2) % parts
    return jnp.where((block_of(source) == first) | (block_of(source) == other_side), factor * values, values)


def shard_levels(rng, shape, shards, smallest, largest):
    level, own = 1.0, jax.random.fold_in(rng, 6)
    for dim, shards_of in shards:
        heights = jnp.exp(jax.random.uniform(jax.random.fold_in(own, dim), (shards_of,), jnp.float32, smallest / len(shards), largest / len(shards)))
        level = level * jnp.repeat(heights, shape[dim] // shards_of).reshape([-1 if axis == dim else 1 for axis in range(len(shape))])
    return level


def bell_draw(stream_key, dims, deviation, most, pieces=(), kind=jnp.bfloat16):
    array = deviation * jax.random.normal(stream_key, dims, jnp.float32)
    if pieces:
        array = array * shard_levels(stream_key, dims, pieces, -0.22, 0.18)
    return jnp.clip(array, -most, most).astype(kind)


def heavy_noise(rng, dims, spread, reach, shards, heavy, kind=jnp.bfloat16):
    values = spread * jax.random.normal(rng, dims, jnp.float32)
    if shards:
        values = values * shard_levels(rng, dims, shards, -0.22, 0.18)
    return jnp.clip(spiked(values, jax.random.fold_in(rng, 3), *heavy), -reach, reach).astype(kind)


def setup_inputs(seed: int = 0) -> dict:
    arg_keys = jax.random.split(jax.random.key(seed), 10)
    block_input = bell_draw(arg_keys[0], (TOKENS, D), 1.0, 6.0, ((0, 8),))
    norm1_gain = jnp.clip(1.0 + 0.18 * jax.random.normal(arg_keys[1], (D,), jnp.float32), 0.1, 1.9)
    query_weight = bell_draw(arg_keys[2], (D, HEADS * HEAD_DIM), D ** -0.5, 0.15625, ((1, 4),))
    keyvalue_weight = bell_draw(arg_keys[3], (D, 2 * HEAD_DIM), D ** -0.5, 0.15625)
    out_weight = bell_draw(arg_keys[4], (HEADS * HEAD_DIM, D), (HEADS * HEAD_DIM // 16) ** -0.5, 0.625, ((0, 4),))
    norm2_gain = jnp.clip(1.0 + 0.18 * jax.random.normal(arg_keys[5], (D,), jnp.float32), 0.1, 1.9)
    gate_up_weight = bell_draw(arg_keys[6], (2, D, FF), D ** -0.5, 0.15625, ((2, 4),))
    down_weight = bell_draw(arg_keys[7], (FF, D), (FF // 4) ** -0.5, 0.1875, ((0, 4),))
    cotangent = heavy_noise(arg_keys[8], (TOKENS, D), 1.0, 6.0, ((0, 8),), (0, 1, 8, 2.0))
    return dict(block_input=block_input, norm1_gain=norm1_gain, query_weight=query_weight, keyvalue_weight=keyvalue_weight, out_weight=out_weight, norm2_gain=norm2_gain, gate_up_weight=gate_up_weight, down_weight=down_weight, cotangent=cotangent)


HIGHEST = lax.Precision.HIGHEST
EPSILON = 1e-06
GELU_COEF = 0.7978845608028654

@jax.custom_vjp
def low(v):
    return lax.optimization_barrier(v.astype(jnp.bfloat16)).astype(jnp.float32)

@jax.custom_vjp
def low_back(v):
    return v

def low_keep(v):
    return (low(v), None)

def low_pass(kept, grad):
    return (grad,)

def back_keep(v):
    return (v, None)

def back_low(kept, grad):
    return (low(grad),)
low.defvjp(low_keep, low_pass)
low_back.defvjp(back_keep, back_low)

def rms_scale(field, gain):
    factor = lax.rsqrt(lax.optimization_barrier(jnp.mean(field * field, axis=-1, keepdims=True)) + EPSILON)
    return field * factor * gain

def gelu_tanh(field):
    return 0.5 * field * (1.0 + jnp.tanh(GELU_COEF * (field + 0.044715 * field * field * field)))

def rope_tables(length, width):
    half_width = width // 2
    position = jnp.arange(length, dtype=jnp.float32)[:, None]
    frequency = jnp.exp(jnp.arange(half_width, dtype=jnp.float32) * (-2.0 * math.log(10000.0) / width))
    angle = position * frequency[None, :]
    return (jnp.cos(angle), jnp.sin(angle))

def rotate(field, cosine, sine):
    half_width = field.shape[-1] // 2
    first_half = field[..., :half_width]
    second_half = field[..., half_width:]
    return jnp.concatenate([first_half * cosine - second_half * sine, second_half * cosine + first_half * sine], axis=-1)

def block_forward(inputs, gain_first, query_w, keyvalue_w, out_w, gain_second, gate_up_w, down_w):
    length = inputs.shape[0]
    per_group = HEADS // N_TENSOR
    ff_group = FF // N_TENSOR
    group_cols = per_group * HEAD_DIM
    cosine, sine = rope_tables(length, HEAD_DIM)
    cos_heads = cosine[:, None, :]
    sin_heads = sine[:, None, :]
    q_scale = 1.0 / math.sqrt(HEAD_DIM)
    row_pos = jnp.arange(length)[:, None]
    col_pos = jnp.arange(length)[None, :]
    allowed = (col_pos <= row_pos) & (row_pos - col_pos < WINDOW)
    normed1 = low(rms_scale(inputs, gain_first))
    attended = jnp.zeros_like(inputs)
    for group_index in range(N_TENSOR):
        q_cols = query_w[:, group_index * group_cols:(group_index + 1) * group_cols]
        queries = low_back(jnp.dot(normed1, q_cols, precision=HIGHEST)).reshape(length, per_group, HEAD_DIM)
        rot_q = low(rotate(queries, cos_heads, sin_heads) * q_scale)
        keyvalue = low_back(jnp.dot(normed1, keyvalue_w, precision=HIGHEST))
        rot_k = low(rotate(keyvalue[:, :HEAD_DIM], cosine, sine))
        values = low(keyvalue[:, HEAD_DIM:])
        scores = low_back(jnp.einsum('qhd,kd->hqk', rot_q, rot_k, precision=HIGHEST))
        scores = jnp.where(allowed[None], scores, -1e+30)
        row_max = lax.optimization_barrier(jnp.max(scores, axis=-1, keepdims=True))
        weights = jnp.exp(scores - row_max)
        probs = weights / lax.optimization_barrier(jnp.sum(weights, axis=-1, keepdims=True))
        head_out = jnp.einsum('hqk,kd->qhd', low(probs), values, precision=HIGHEST)
        head_out = low(low_back(head_out)).reshape(length, group_cols)
        o_rows = out_w[group_index * group_cols:(group_index + 1) * group_cols, :]
        attended = attended + low(jnp.dot(head_out, o_rows, precision=HIGHEST))
    residual = inputs + low_back(attended)
    normed2 = low(rms_scale(residual, gain_second))
    ffn_out = jnp.zeros_like(inputs)
    for group_index in range(N_TENSOR):
        lower_unit = group_index * ff_group
        upper_unit = lower_unit + ff_group
        gate_part = low_back(jnp.dot(normed2, gate_up_w[0][:, lower_unit:upper_unit], precision=HIGHEST))
        up_part = low_back(jnp.dot(normed2, gate_up_w[1][:, lower_unit:upper_unit], precision=HIGHEST))
        hidden = low(gelu_tanh(gate_part) * up_part)
        ffn_out = ffn_out + low(jnp.dot(hidden, down_w[lower_unit:upper_unit, :], precision=HIGHEST))
    return residual + low_back(ffn_out)

def reference(block_input, norm1_gain, query_weight, keyvalue_weight, out_weight, norm2_gain, gate_up_weight, down_weight, cotangent):
    params = (norm1_gain.astype(jnp.float32), query_weight.astype(jnp.float32), keyvalue_weight.astype(jnp.float32), out_weight.astype(jnp.float32), norm2_gain.astype(jnp.float32), gate_up_weight.astype(jnp.float32), down_weight.astype(jnp.float32))
    sequences = block_input.astype(jnp.float32).reshape(N_DP, TOK_DEV, D)
    cot_seqs = cotangent.astype(jnp.float32).reshape(N_DP, TOK_DEV, D)

    def sequence_step(totals, pair):
        seq_input, seq_cot = pair
        seq_out, pullback = jax.vjp(block_forward, seq_input, *params)
        gradients = pullback(seq_cot)
        totals = tuple((acc + new for acc, new in zip(totals, gradients[1:])))
        return (totals, (seq_out.astype(jnp.bfloat16), gradients[0].astype(jnp.bfloat16)))
    initial = tuple((jnp.zeros_like(param) for param in params))
    totals, (outputs, input_grads) = lax.scan(sequence_step, initial, (sequences, cot_seqs))
    return (outputs.reshape(TOKENS, D), input_grads.reshape(TOKENS, D), totals[0], totals[1], totals[2], totals[3], totals[4], totals[5], totals[6])
```

```python
import math

import jax
import jax.numpy as jnp
import numpy as np
from jax import lax
from jax.sharding import PartitionSpec as P

WINDOW = 1024
EPSILON = 1e-06
GELU_COEF = 0.7978845608028654
BF16 = jnp.bfloat16
F32 = jnp.float32

RING = (0, 2, 4, 6, 7, 5, 3, 1)


def product(left, right):
    return jnp.dot(left, right, preferred_element_type=F32)


def product_left_t(left, right):
    return lax.dot_general(left, right, (((0,), (0,)), ((), ())), preferred_element_type=F32)


def product_right_t(left, right):
    return lax.dot_general(left, right, (((1,), (1,)), ((), ())), preferred_element_type=F32)


def rope_tables(length, width):
    half_width = width // 2
    position = jnp.arange(length, dtype=F32)[:, None]
    frequency = jnp.exp(jnp.arange(half_width, dtype=F32) * (-2.0 * math.log(10000.0) / width))
    angle = position * frequency[None, :]
    return jnp.cos(angle), jnp.sin(angle)


def rotate(field, cosine, sine):
    half_width = field.shape[-1] // 2
    first_half = field[..., :half_width]
    second_half = field[..., half_width:]
    return jnp.concatenate(
        [first_half * cosine - second_half * sine, second_half * cosine + first_half * sine],
        axis=-1,
    )


def rotate_back(field, cosine, sine):
    return rotate(field, cosine, -sine)


def swap_core(field):
    return lax.ppermute(field, "tensor", [(i, i ^ 1) for i in range(4)])


def swap_x(field):
    return lax.ppermute(field, "tensor", [(i, i ^ 2) for i in range(4)])


def own_rows(field, core, half):
    return lax.dynamic_slice_in_dim(field, core * half, half, 0)


def both_halves(own, sibling, core):
    half = own.shape[0]
    out = jnp.zeros((2 * half,) + own.shape[1:], own.dtype)
    out = lax.dynamic_update_slice_in_dim(out, own, core * half, 0)
    return lax.dynamic_update_slice_in_dim(out, sibling, (1 - core) * half, 0)


class Ring:
    def __init__(self, forward):
        order = RING if forward else RING[::-1]
        self.perm = [(order[i], order[(i + 1) % 8]) for i in range(8)]
        place = np.zeros(8, np.int32)
        for i, device in enumerate(order):
            place[device] = i
        self.place = jnp.asarray(place)[lax.axis_index("dp")]

    def all_reduce(self, fields):
        rows = [field.shape[0] // 8 for field in fields]
        cuts = np.cumsum([0] + rows)

        def chunk(k):
            parts = [lax.dynamic_slice_in_dim(f, k * r, r, 0) for f, r in zip(fields, rows)]
            return parts[0] if len(parts) == 1 else jnp.concatenate(parts, 0)

        travelling = chunk((self.place + 7) % 8)
        for step in range(7):
            arrived = lax.ppermute(travelling, "dp", self.perm)
            mine = chunk((self.place + 14 - step) % 8)
            travelling = (arrived.astype(F32) + mine.astype(F32)).astype(BF16)
        outs = [jnp.zeros(f.shape, F32) for f in fields]

        def place_chunk(outs, piece, k):
            return [
                lax.dynamic_update_slice_in_dim(o, piece[a:b].astype(F32), k * r, 0)
                for o, r, a, b in zip(outs, rows, cuts[:-1], cuts[1:])
            ]

        outs = place_chunk(outs, travelling, self.place)
        for step in range(7):
            travelling = lax.ppermute(travelling, "dp", self.perm)
            outs = place_chunk(outs, travelling, (self.place + 7 - step) % 8)
        return outs


class Sum:
    def all_reduce(self, fields):
        return [lax.psum(field, "dp").astype(F32) for field in fields]


def small_sum(field, n_dp):
    if n_dp & (n_dp - 1):
        field = lax.psum(field, "dp")
    else:
        step = 1
        while step < n_dp:
            field = field + lax.ppermute(field, "dp", [(i, i ^ step) for i in range(n_dp)])
            step *= 2
    return field + swap_core(field)


def make_local(n_dp):
    def local(
        block_input,
        norm1_gain,
        query_weight,
        keyvalue_weight,
        out_weight,
        norm2_gain,
        gate_up_weight,
        down_weight,
        cotangent,
    ):
        length, width = block_input.shape
        half = length // 2
        head_dim = keyvalue_weight.shape[1] // 2
        heads = 2 * query_weight.shape[1] // head_dim
        q_scale = 1.0 / math.sqrt(head_dim)
        tensor = lax.axis_index("tensor")
        core = tensor % 2
        chip = tensor // 2
        clockwise, counter = (Ring(True), Ring(False)) if n_dp == 8 else (Sum(), Sum())

        query_chip = jnp.concatenate([query_weight, swap_core(query_weight)], 1)
        out_chip = jnp.concatenate([out_weight, swap_core(out_weight)], 0)

        input_full = block_input.astype(F32)
        factor1 = lax.rsqrt(jnp.mean(input_full * input_full, -1, keepdims=True) + EPSILON)
        normed1 = (input_full * factor1 * norm1_gain).astype(BF16)
        input_own = own_rows(block_input, core, half).astype(F32)
        factor1_own = own_rows(factor1, core, half)
        normed1_own = own_rows(normed1, core, half)
        cosine, sine = rope_tables(length, head_dim)
        cos_own = own_rows(cosine, core, half)[:, None, :]
        sin_own = own_rows(sine, core, half)[:, None, :]

        keyvalue = product(normed1, keyvalue_weight)
        rot_k = rotate(keyvalue[:, :head_dim], cosine, sine).astype(BF16)
        values = keyvalue[:, head_dim:].astype(BF16)
        queries = product(normed1_own, query_chip).reshape(half, heads, head_dim)
        rot_q = (rotate(queries, cos_own, sin_own) * q_scale).astype(BF16)

        row_pos = core * half + jnp.arange(half)[:, None]
        col_pos = jnp.arange(length)[None, :]
        allowed = (col_pos <= row_pos) & (row_pos - col_pos < WINDOW)
        scores = jnp.einsum("qhd,kd->hqk", rot_q, rot_k, preferred_element_type=F32)
        scores = jnp.where(allowed[None], scores, -1e30)
        weights = jnp.exp(scores - jnp.max(scores, axis=-1, keepdims=True))
        probs = weights / jnp.sum(weights, axis=-1, keepdims=True)
        probs_low = probs.astype(BF16)
        head_out = jnp.einsum("hqk,kd->qhd", probs_low, values, preferred_element_type=F32)
        head_out = head_out.astype(BF16).reshape(half, heads * head_dim)

        attn_part = product(head_out, out_chip).astype(BF16)
        attended = attn_part.astype(F32) + swap_x(attn_part).astype(F32)
        residual = input_own + attended
        factor2 = lax.rsqrt(jnp.mean(residual * residual, -1, keepdims=True) + EPSILON)
        normed2_own = (residual * factor2 * norm2_gain).astype(BF16)
        normed2 = both_halves(normed2_own, swap_core(normed2_own), core)

        gate_weight, up_weight = gate_up_weight[0], gate_up_weight[1]
        gate = product(normed2, gate_weight)
        up = product(normed2, up_weight)
        inner = jnp.tanh(GELU_COEF * (gate + 0.044715 * gate * gate * gate))
        gelu = 0.5 * gate * (1.0 + inner)
        slope = 0.5 * (1.0 + inner) + 0.5 * gate * (1.0 - inner * inner) * GELU_COEF * (
            1.0 + 3.0 * 0.044715 * gate * gate
        )
        hidden = (gelu * up).astype(BF16)
        down_grad = product_left_t(hidden, cotangent).astype(BF16)
        d_hidden = product_right_t(cotangent, down_weight)
        d_gate = (d_hidden * up * slope).astype(BF16)
        d_up = (d_hidden * gelu).astype(BF16)
        gate_grad = product_left_t(normed2, d_gate).astype(BF16)
        up_grad = product_left_t(normed2, d_up).astype(BF16)

        middle = width // 2
        (down_left,) = clockwise.all_reduce([down_grad[:, :middle]])
        (down_right,) = counter.all_reduce([down_grad[:, middle:]])
        (gate_sum,) = clockwise.all_reduce([gate_grad])
        (up_sum,) = counter.all_reduce([up_grad])
        down_sum = jnp.concatenate([down_left, down_right], 1)
        gate_up_sum = jnp.stack([gate_sum, up_sum])

        def chip_sum(part):
            mine = own_rows(part, core, half)
            other = own_rows(part, 1 - core, half).astype(BF16)
            on_chip = (mine + swap_core(other).astype(F32)).astype(BF16)
            return on_chip.astype(F32) + swap_x(on_chip).astype(F32)

        d_normed2 = chip_sum(product_right_t(d_gate, gate_weight) + product_right_t(d_up, up_weight))
        scaled = norm2_gain * d_normed2
        norm2_part = jnp.sum(d_normed2 * residual * factor2, axis=0)
        d_residual = (
            cotangent_own(cotangent, core, half)
            + factor2 * scaled
            - residual * factor2**3 * jnp.mean(scaled * residual, -1, keepdims=True)
        )
        d_res_low = d_residual.astype(BF16)
        out_part = product_left_t(head_out, d_res_low)
        own_cols = query_weight.shape[1]
        out_grad = (out_part[:own_cols] + swap_core(out_part[own_cols:].astype(BF16)).astype(F32)).astype(BF16)
        d_heads = product_right_t(d_res_low, out_chip).astype(BF16).reshape(half, heads, head_dim)

        d_probs = jnp.einsum("qhd,kd->hqk", d_heads, values, preferred_element_type=F32)
        delta = jnp.sum(probs * d_probs, axis=-1, keepdims=True)
        d_scores = (probs * (d_probs - delta)).astype(BF16)
        d_rot_q = jnp.einsum("hqk,kd->qhd", d_scores, rot_k, preferred_element_type=F32)
        d_rot_k = jnp.einsum("hqk,qhd->kd", d_scores, rot_q, preferred_element_type=F32)
        d_values = jnp.einsum("hqk,qhd->kd", probs_low, d_heads, preferred_element_type=F32)
        d_queries = rotate_back(d_rot_q * q_scale, cos_own, sin_own).astype(BF16)
        d_queries = d_queries.reshape(half, heads * head_dim)
        d_keyvalue = chip_sum(jnp.concatenate([rotate_back(d_rot_k, cosine, sine), d_values], 1)).astype(BF16)

        query_part = product_left_t(normed1_own, d_queries)
        query_grad = (
            query_part[:, :own_cols] + swap_core(query_part[:, own_cols:].astype(BF16)).astype(F32)
        ).astype(BF16)
        mine = lax.dynamic_slice_in_dim(d_keyvalue, chip * head_dim, head_dim, 1)
        kv_part = product_left_t(normed1_own, mine)
        kv_mine = own_rows(kv_part, core, middle)
        kv_other = own_rows(kv_part, 1 - core, middle).astype(BF16)
        kv_grad = (kv_mine + swap_core(kv_other).astype(F32)).astype(BF16)
        lanes = own_cols // head_dim
        kv_rows = middle // lanes
        kv_wide = jnp.concatenate([kv_grad[i * kv_rows : (i + 1) * kv_rows] for i in range(lanes)], 1)

        (out_sum,) = clockwise.all_reduce([out_grad])
        query_sum, kv_sum = counter.all_reduce([query_grad, kv_wide])

        d_normed1_part = product_right_t(d_queries, query_chip).astype(BF16)
        d_normed1 = (d_normed1_part.astype(F32) + swap_x(d_normed1_part).astype(F32)) + product_right_t(
            d_keyvalue, keyvalue_weight
        )
        scaled1 = norm1_gain * d_normed1
        norm1_part = jnp.sum(d_normed1 * input_own * factor1_own, axis=0)
        input_grad_own = (
            d_residual
            + factor1_own * scaled1
            - input_own * factor1_own**3 * jnp.mean(scaled1 * input_own, -1, keepdims=True)
        ).astype(BF16)
        input_grad = both_halves(input_grad_own, swap_core(input_grad_own), core)

        ffn_out = chip_sum(product(hidden, down_weight))
        output_own = (residual + ffn_out).astype(BF16)
        block_output = both_halves(output_own, swap_core(output_own), core)

        norm_sums = small_sum(jnp.stack([norm1_part, norm2_part]), n_dp)

        kv_tall = jnp.concatenate([kv_sum[:, i * head_dim : (i + 1) * head_dim] for i in range(lanes)], 0).astype(BF16)
        kv_column = both_halves(kv_tall, swap_core(kv_tall), core)
        kv_other_column = swap_x(kv_column)
        kv_out = jnp.zeros(keyvalue_weight.shape, BF16)
        kv_out = lax.dynamic_update_slice_in_dim(kv_out, kv_column, chip * head_dim, 1)
        kv_out = lax.dynamic_update_slice_in_dim(kv_out, kv_other_column, (1 - chip) * head_dim, 1)

        return (
            block_output,
            input_grad,
            norm_sums[0],
            query_sum,
            kv_out.astype(F32),
            out_sum,
            norm_sums[1],
            gate_up_sum,
            down_sum,
        )

    return local


def cotangent_own(cotangent, core, half):
    return own_rows(cotangent, core, half).astype(F32)


def solution(mesh):
    return jax.shard_map(
        make_local(mesh.shape["dp"]),
        mesh=mesh,
        in_specs=(
            P("dp", None),
            P(),
            P(None, "tensor"),
            P(),
            P("tensor", None),
            P(),
            P(None, None, "tensor"),
            P("tensor", None),
            P("dp", None),
        ),
        out_specs=(
            P("dp", None),
            P("dp", None),
            P(),
            P(None, "tensor"),
            P(),
            P("tensor", None),
            P(),
            P(None, None, "tensor"),
            P("tensor", None),
        ),
        check_vma=False,
    )
```

```python
import functools
import math

import jax
import jax.numpy as jnp
import numpy as np
from jax import lax
from jax.experimental import pallas as pl
from jax.experimental.pallas import tpu as pltpu
from jax.sharding import PartitionSpec as P

WINDOW = 1024
EPSILON = 1e-06
GELU_COEF = 0.7978845608028654
BF16 = jnp.bfloat16
F32 = jnp.float32
NN = (((1,), (0,)), ((), ()))
NT = (((1,), (1,)), ((), ()))
TN = (((0,), (0,)), ((), ()))

RING = (0, 2, 4, 6, 7, 5, 3, 1)

ANY = pl.BlockSpec(memory_space=pl.ANY)
SMEM = pl.BlockSpec(memory_space=pltpu.SMEM)
MIB = 2**20

ORDER = " ".join(
    (
        "project attend0 attend1 dhidden",
        "norm0 ffn0 norm1 ffn1",
        "down gate a up",
        "a dnsib a b",
        "dnown a b a",
        "a b a nback",
        "aback a b qg",
        "a kv b a",
        "kvpart outg a b",
        "dn1 a b a",
        "a b E fosib",
        "a b a foown",
        "a b a a",
        "b a input sums",
        "a b a out",
        "weave a b a",
        "a b a a",
        "a",
    )
).split()


def dot(left, right, dims=NN):
    return lax.dot_general(left, right, dims, preferred_element_type=F32)


def swap_core(field):
    return lax.ppermute(field, "tensor", [(i, i ^ 1) for i in range(4)])


def swap_x(field):
    return lax.ppermute(field, "tensor", [(i, i ^ 2) for i in range(4)])


def shape(dims, dtype):
    return jax.ShapeDtypeStruct(dims, dtype)


def whole(array):
    rank = len(array.shape)
    return pl.BlockSpec(array.shape, lambda *_: (0,) * rank)


class Chain:
    def __init__(self):
        self.links = []

    def call(self, body, outs, ins, in_specs, out_specs, grid=(), scalars=(), vmem=24, scratch=(), aliases=None):
        links, given = self.links, len(scalars) + len(ins)

        def run(*refs):
            body(*refs[:given], *refs[given + len(links) :])

        results = pl.pallas_call(
            run,
            out_shape=outs,
            grid_spec=pltpu.PrefetchScalarGridSpec(
                num_scalar_prefetch=len(scalars),
                grid=grid,
                in_specs=list(in_specs) + [ANY] * len(links),
                out_specs=out_specs,
                scratch_shapes=list(scratch),
            ),
            input_output_aliases=aliases or {},
            compiler_params=pltpu.CompilerParams(vmem_limit_bytes=vmem * MIB),
            cost_estimate=pl.CostEstimate(flops=0, bytes_accessed=0, transcendentals=0),
        )(*scalars, *ins, *links)
        self.links = [results[0]]
        return results

    def after(self, *values):
        tied = lax.optimization_barrier(values + tuple(self.links))
        self.links = list(tied[len(values) :])
        return tied[: len(values)]


def rope(field, table, sign=1.0):
    half = field.shape[1] // 2
    other = pltpu.roll(table, half, 1)
    first = lax.broadcasted_iota(jnp.int32, table.shape, 1) < half
    cosine = jnp.where(first, table, other)
    sine = jnp.where(first, -other, table) * sign
    return field * cosine + pltpu.roll(field, half, 1) * sine


def rms_factor(field):
    return lax.rsqrt(jnp.mean(field * field, axis=1, keepdims=True) + EPSILON)


def project_kernel(core, x, gain, weight, table, keys, values, own0, own1):
    block = pl.program_id(0)
    head_dim = keys.shape[1]
    field = x[...].astype(F32)
    normed = (field * rms_factor(field) * gain[...]).astype(BF16)
    both = dot(normed, weight[...])
    keys[...] = rope(both[:, :head_dim], table[...]).astype(BF16)
    values[...] = both[:, head_dim:].astype(BF16)

    @pl.when(core[0] == block)
    def _():
        own0[...] = normed

    @pl.when(3 - core[0] == block)
    def _():
        own1[...] = normed


def causal(rows, columns, first_row):
    row = lax.broadcasted_iota(jnp.int32, (rows, columns), 0) + first_row
    column = lax.broadcasted_iota(jnp.int32, (rows, columns), 1)
    allowed = column <= row
    if columns > WINDOW:
        allowed = allowed & (row - column < WINDOW)
    return allowed


def attend_kernel(
    numbers, scale, block, normed, keys, values, table, query_own, query_sib, out_own, out_sib,
    part, rot_q, head_out, log_total, query_w, out_w, arrived,
):
    quarter = normed.shape[0]
    head_dim = keys.shape[1]
    per_core = query_own.shape[1] // head_dim
    copies = [
        pltpu.make_async_copy(source, target, arrived.at[i])
        for i, (source, target) in enumerate(
            ((query_own, query_w.at[0]), (query_sib, query_w.at[1]), (out_own, out_w.at[0]), (out_sib, out_w.at[1]))
        )
    ]
    for copy in copies:
        copy.start()
    for side in range(2):
        copies[side].wait()
        queries = dot(normed[...], query_w[side])
        for head in range(per_core):
            columns = slice(head * head_dim, (head + 1) * head_dim)
            place = side * per_core + head
            rot_q[:, place * head_dim : (place + 1) * head_dim] = (
                rope(queries[:, columns], table[...]) * scale
            ).astype(BF16)
    for number in numbers:

        @pl.when(block[0] == number)
        def _():
            span = (number + 1) * quarter
            allowed = causal(quarter, span, number * quarter)
            for head in range(2 * per_core):
                columns = slice(head * head_dim, (head + 1) * head_dim)
                scores = dot(rot_q[:, columns], keys[:span, :], NT)
                scores = jnp.where(allowed, scores, -1e30)
                top = jnp.max(scores, axis=1, keepdims=True)
                weights = jnp.exp(scores - top)
                total = jnp.sum(weights, axis=1, keepdims=True)
                probs = (weights * (1.0 / total)).astype(BF16)
                head_out[:, columns] = dot(probs, values[:span, :]).astype(BF16)
                log_total[:, head : head + 1] = top + jnp.log(total)

    copies[2].wait()
    copies[3].wait()
    half = per_core * head_dim
    part[...] = (dot(head_out[:, :half], out_w[0]) + dot(head_out[:, half:], out_w[1])).astype(BF16)


def attend_back_kernel(
    scale, core, rot_q0, rot_q1, log0, log1, d_heads, keys, values, table,
    d_queries, kv_own, kv_sib, d_keys, d_values,
):
    quarter = rot_q0.shape[0]
    head_dim = keys.shape[1]
    heads = rot_q0.shape[1] // head_dim
    d_keys[...] = jnp.zeros_like(d_keys)
    d_values[...] = jnp.zeros_like(d_values)

    def rows_of(block):
        return pl.ds(pl.multiple_of(block * quarter, 16), quarter)

    for order, (rot_q, log_total) in enumerate(((rot_q0, log0), (rot_q1, log1))):
        block = core[0] if order == 0 else 3 - core[0]
        rows = slice(order * quarter, (order + 1) * quarter)
        for number in (0, 1) if order == 0 else (2, 3):

            @pl.when(block == number)
            def _():
                span = (number + 1) * quarter
                own_table = table[number * quarter : span, :]
                allowed = causal(quarter, span, number * quarter)
                for head in range(heads):
                    columns = slice(head * head_dim, (head + 1) * head_dim)
                    query = rot_q[:, columns]
                    d_out = d_heads[rows, columns]
                    scores = dot(query, keys[:span, :], NT) - log_total[:, head : head + 1]
                    probs = jnp.exp(jnp.where(allowed, scores, -1e30))
                    d_probs = dot(d_out, values[:span, :], NT)
                    delta = jnp.sum(probs * d_probs, axis=1, keepdims=True)
                    d_scores = (probs * (d_probs - delta)).astype(BF16)
                    d_query = dot(d_scores, keys[:span, :]) * scale
                    d_queries[rows, columns] = rope(d_query, own_table, -1.0).astype(BF16)
                    d_keys[:span, :] += dot(d_scores, query, TN)
                    d_values[:span, :] += dot(probs.astype(BF16), d_out, TN)

    d_keys[...] = rope(d_keys[...], table[...], -1.0)
    for order in range(2):
        rows = slice(order * quarter, (order + 1) * quarter)
        own = rows_of(core[0] if order == 0 else 3 - core[0])
        sib = rows_of(1 - core[0] if order == 0 else 2 + core[0])
        kv_own[rows, :head_dim] = d_keys[own, :]
        kv_own[rows, head_dim:] = d_values[own, :]
        kv_sib[rows, :head_dim] = d_keys[sib, :].astype(BF16)
        kv_sib[rows, head_dim:] = d_values[sib, :].astype(BF16)


def d_hidden_kernel(places, cotangent, weight, d_hidden, ordered):
    d_hidden[...] = dot(cotangent[...], weight[...], NT).astype(BF16)
    ordered[...] = cotangent[...]


def norm_kernel(block, x, part, from_x, gain, *rest):
    normed, residual = rest[-2:]
    value = x[...].astype(F32) + (part[...].astype(F32) + from_x[...].astype(F32))
    residual[...] = value
    normed[...] = (value * rms_factor(value) * gain[...]).astype(BF16)


def ffn_kernel(normed_own, normed_sib, weight, d_hidden, *rest):
    hidden, d_gate, d_up, normed_all = rest[-4:]
    quarter = normed_own.shape[0]

    @pl.when(pl.program_id(0) == 0)
    def _():
        normed_all[:quarter, :] = normed_own[...]
        normed_all[quarter:, :] = normed_sib[...]

    gate = dot(normed_all[...], weight[0])
    up = dot(normed_all[...], weight[1])
    square = gate * gate
    inner = jnp.tanh(GELU_COEF * gate * (1.0 + 0.044715 * square))
    half = 0.5 * (1.0 + inner)
    gelu = gate * half
    slope = half + 0.5 * gate * (1.0 - inner * inner) * (GELU_COEF * (1.0 + 3.0 * 0.044715 * square))
    back = d_hidden[...].astype(F32)
    hidden[...] = (gelu * up).astype(BF16)
    d_gate[...] = (back * up * slope).astype(BF16)
    d_up[...] = (back * gelu).astype(BF16)


def grad_kernel(left, right, out):
    out[...] = dot(left[...], right[...], TN).astype(BF16)


def rows_back_kernel(dims, count, *refs):
    lefts, rights, rest = refs[:count], refs[count : 2 * count], refs[2 * count :]
    out = rest[-1]
    total = None
    for left, right in zip(lefts, rights):
        rows = left[...].reshape(-1, left.shape[-1])
        matrix = right[...]
        term = dot(rows, matrix.reshape(matrix.shape[-2:]), dims)
        total = term if total is None else total + term
    if len(rest) == 2:
        total = total + rest[0][...].astype(F32)
    out[...] = total.astype(BF16)


def norm_back(field, gain, d_normed):
    factor = rms_factor(field)
    scaled = gain * d_normed
    d_gain = jnp.sum(d_normed * field * factor, axis=0, keepdims=True)
    return factor * scaled - field * (factor * factor * factor) * jnp.mean(scaled * field, axis=1, keepdims=True), d_gain


def norm2_back_kernel(
    residual, on_chip, from_x, cotangent, gain, out_own, out_sib, d_residual, d_res_low, d_heads, d_gain
):
    d_normed = on_chip[...].astype(F32) + from_x[...].astype(F32)
    change, part = norm_back(residual[...], gain[...], d_normed)
    total = cotangent[...].reshape(residual.shape).astype(F32) + change
    d_residual[...] = total
    low = total.astype(BF16)
    d_res_low[...] = low
    half = out_own.shape[0]
    d_heads[:, :half] = dot(low, out_own[...], NT).astype(BF16)
    d_heads[:, half:] = dot(low, out_sib[...], NT).astype(BF16)

    @pl.when(pl.program_id(0) == 0)
    def _():
        d_gain[...] = part

    @pl.when(pl.program_id(0) > 0)
    def _():
        d_gain[...] += part


def norm1_back_kernel(places, x, on_chip, from_x, d_kv, kv_weight, d_residual, gain, d_input, d_gain):
    d_normed = (on_chip[...].astype(F32) + from_x[...].astype(F32)) + dot(d_kv[...], kv_weight[...], NT)
    change, part = norm_back(x[...].astype(F32), gain[...], d_normed)
    d_input[...] = (d_residual[...] + change).astype(BF16)

    @pl.when(pl.program_id(0) == 0)
    def _():
        d_gain[...] = part

    @pl.when(pl.program_id(0) > 0)
    def _():
        d_gain[...] += part


def split_grad_kernel(columns, left0, left1, right, mine, other):
    quarter = left0.shape[0]
    top, bottom = right[:quarter, :], right[quarter:, :]
    mine[...] = dot(left0[:, :columns], top, TN) + dot(left1[:, :columns], bottom, TN)
    other[...] = (dot(left0[:, columns:], top, TN) + dot(left1[:, columns:], bottom, TN)).astype(BF16)


def query_grad_kernel(columns, left0, left1, right, mine, other):
    quarter = left0.shape[0]
    mine[...] = dot(left0[...], right[:quarter, :columns], TN) + dot(left1[...], right[quarter:, :columns], TN)
    other[...] = (
        dot(left0[...], right[:quarter, columns:], TN) + dot(left1[...], right[quarter:, columns:], TN)
    ).astype(BF16)


def weave_kernel(places, own, sibling, out):
    step = pl.program_id(0)

    @pl.when(step < 2)
    def _():
        out[...] = own[...]

    @pl.when(step >= 2)
    def _():
        out[...] = sibling[...]


def empty(dims, dtype):
    return pl.pallas_call(lambda out: None, out_shape=shape(dims, dtype), out_specs=ANY)()


class Flow:
    def __init__(self, forward, chain):
        order = RING if forward else RING[::-1]
        self.chain = chain
        self.perm = [(order[i], order[(i + 1) % 8]) for i in range(8)]
        place = np.zeros(8, np.int32)
        for i, device in enumerate(order):
            place[device] = i
        place = jnp.asarray(place)[lax.axis_index("dp")]
        self.numbers = [(place - i) & 7 for i in range(8)]

    def chunk(self, i):
        parts = [
            lax.dynamic_slice(f, (self.numbers[i % 8], 0, 0), (1,) + f.shape[1:], allow_negative_indices=False)[0]
            for f in self.fields
        ]
        return parts[0] if len(parts) == 1 else jnp.concatenate(parts, 0)

    def begin(self, fields, write):
        self.fields, self.write, self.step = fields, write, 0
        self.travelling = self.chunk(1)
        self.arrived = lax.ppermute(self.travelling, "dp", self.perm)

    def land(self):
        step = self.step
        self.step += 1
        if step < 7:
            mine = self.chunk(step + 2)
            self.travelling = (self.arrived.astype(F32) + mine.astype(F32)).astype(BF16)
        else:
            self.travelling = self.arrived

    def send(self):
        if self.step < 14:
            self.arrived = lax.ppermute(self.travelling, "dp", self.perm)
        if self.step >= 7:
            self.write(self.numbers[(self.step - 7) % 8], self.travelling)


class Pair:
    def __init__(self, chain):
        self.chain = chain
        self.flows = (Flow(True, chain), Flow(False, chain))
        self.left = 0

    def begin(self, way, *job):
        self.flows[way].begin(*job)
        self.left = 14

    def step(self):
        if self.left == 0:
            raise ValueError("ring idle")
        self.left -= 1
        arrived = self.chain.after(*[flow.arrived for flow in self.flows])
        for flow, value in zip(self.flows, arrived):
            flow.arrived = value
            flow.land()
        self.chain.links = self.chain.links[:1] + [flow.travelling for flow in self.flows]
        for flow in self.flows:
            flow.send()


class Whole:
    left = 0

    def __init__(self, chain):
        pass

    def begin(self, way, fields, write):
        sums = [lax.psum(f, "dp") for f in fields]
        for k in range(8):
            write(k, jnp.concatenate([s[k] for s in sums], 0))

    def step(self):
        pass


def small_sum(field, n_dp):
    if n_dp & (n_dp - 1):
        field = lax.psum(field, "dp")
    else:
        step = 1
        while step < n_dp:
            field = field + lax.ppermute(field, "dp", [(i, i ^ step) for i in range(n_dp)])
            step *= 2
    return field + swap_core(field)


class Block:
    def __init__(self, n_dp, args):
        (
            self.x, self.gain1, self.query_w, self.kv_w, self.out_w, self.gain2, self.gate_up_w, self.down_w, self.cot_in,
        ) = args
        self.gain1, self.gain2 = self.gain1[None], self.gain2[None]
        self.n_dp = n_dp
        self.length, self.width = self.x.shape
        self.quarter, self.half = self.length // 4, self.length // 2
        self.head_dim = self.kv_w.shape[1] // 2
        self.cols = self.query_w.shape[1]
        self.units = self.down_w.shape[0]
        self.middle = self.width // 2
        self.scale = 1.0 / math.sqrt(self.head_dim)
        tensor = lax.axis_index("tensor")
        self.core, self.chip = tensor & 1, tensor >> 1
        core = self.core
        self.own = jnp.stack([core, 3 - core])
        self.places = jnp.stack([core, 1 - core, 3 - core, 2 + core])
        self.weave_places = jnp.stack([core, 3 - core, 1 - core, 2 + core])
        self.chain = Chain()
        ring = Pair if n_dp == 8 else Whole
        self.ring_a, self.ring_b = ring(self.chain), ring(self.chain)
        half_dim = self.head_dim // 2
        angle = np.arange(self.length)[:, None] * 10000.0 ** (-2.0 * np.arange(half_dim)[None, :] / self.head_dim)
        self.table = jnp.asarray(np.concatenate([np.cos(angle), np.sin(angle)], 1), F32)
        self.query_sib = swap_core(self.query_w)
        self.out_sib = swap_core(self.out_w)
        self.down_sum = empty((8, self.units // 8, self.width), F32)
        self.gate_up_sum = empty((2, 8, self.width // 8, self.units), F32)
        self.out_sum = empty((8, self.cols // 8, self.width), F32)
        self.query_sum = empty((8, self.width // 8, self.cols), F32)

    def rows(self, table=None):
        if table is None:
            return pl.BlockSpec((self.quarter, self.width), lambda i, *_: (i, 0))
        return pl.BlockSpec((self.quarter, self.width), lambda i, places: (places[i], 0))

    def project(self):
        q, d, w = self.quarter, self.head_dim, self.width
        same = pl.BlockSpec((q, w), lambda i, _: (0, 0))
        narrow = pl.BlockSpec((q, d), lambda i, _: (i, 0))
        self.keys, self.values, own0, own1 = self.chain.call(
            project_kernel,
            [shape((4 * q, d), BF16)] * 2 + [shape((q, w), BF16)] * 2,
            [self.x, self.gain1, self.kv_w, self.table],
            [pl.BlockSpec((q, w), lambda i, _: (i, 0)), whole(self.gain1), whole(self.kv_w), narrow],
            [narrow, narrow, same, same],
            grid=(4,),
            scalars=[self.core[None]],
        )
        self.normed1 = (own0, own1)

    def attend(self, j):
        q, w, c = self.quarter, self.width, 2 * self.cols
        normed = self.normed1[j]
        table = pl.BlockSpec((q, self.head_dim), lambda i, block: (block[0], 0))
        return self.chain.call(
            functools.partial(attend_kernel, (0, 1) if j == 0 else (2, 3), self.scale),
            [shape((q, w), BF16), shape((q, c), BF16), shape((q, c), BF16), shape((q, 8), F32)],
            [normed, self.keys, self.values, self.table, self.query_w, self.query_sib, self.out_w, self.out_sib],
            [whole(normed), whole(self.keys), whole(self.values), table] + [ANY] * 4,
            [pl.BlockSpec(d, lambda *_: (0, 0)) for d in ((q, w), (q, c), (q, c), (q, 8))],
            grid=(1,),
            scalars=[self.own[j][None]],
            scratch=[
                pltpu.VMEM((2,) + self.query_w.shape, BF16),
                pltpu.VMEM((2,) + self.out_w.shape, BF16),
                pltpu.SemaphoreType.DMA((4,)),
            ],
        )

    def attend0(self):
        self.part0, self.rot_q0, self.head_out0, self.log0 = self.attend(0)
        self.from_x0 = swap_x(self.part0)

    def attend1(self):
        self.part1, self.rot_q1, self.head_out1, self.log1 = self.attend(1)
        self.from_x1 = swap_x(self.part1)

    def dhidden(self):
        self.d_hidden, self.cot = self.chain.call(
            d_hidden_kernel,
            [shape((self.length, self.units), BF16), shape((self.length, self.width), BF16)],
            [self.cot_in, self.down_w],
            [self.rows(1), whole(self.down_w)],
            [pl.BlockSpec((self.quarter, self.units), lambda i, _: (i, 0)), self.rows()],
            grid=(4,),
            scalars=[self.places],
        )

    def norm(self, j, part, from_x, before):
        block = pl.BlockSpec((self.quarter, self.width), lambda i, _: (0, 0))
        return self.chain.call(
            norm_kernel,
            [shape((self.quarter, self.width), BF16), shape((self.half, self.width), F32)],
            [self.x, part, from_x, self.gain2, *before],
            [self.rows(1), block, block, whole(self.gain2)] + [ANY] * len(before),
            [block, pl.BlockSpec((self.quarter, self.width), lambda i, _: (j, 0))],
            grid=(1,),
            scalars=[self.own[j][None]],
            aliases={5: 1} if before else None,
        )

    def norm0(self):
        self.normed2_0, self.residual = self.norm(0, self.part0, self.from_x0, ())
        self.sib2_0 = swap_core(self.normed2_0)

    def norm1(self):
        self.normed2_1, self.residual = self.norm(1, self.part1, self.from_x1, (self.residual,))
        self.sib2_1 = swap_core(self.normed2_1)

    def ffn(self, j, own, sibling, before):
        tile = self.units // 3
        here = pl.BlockSpec((self.half, tile), lambda i: (j, i))
        return self.chain.call(
            ffn_kernel,
            [shape((self.length, self.units), BF16)] * 3 + [shape((self.length, self.width), BF16)],
            [own, sibling, self.gate_up_w, self.d_hidden, *before],
            [whole(own), whole(sibling), pl.BlockSpec((2, self.width, tile), lambda i: (0, 0, i)), here]
            + [ANY] * len(before),
            [here] * 3 + [pl.BlockSpec((self.half, self.width), lambda i: (j, 0))],
            grid=(3,),
            aliases={4 + i: i for i in range(len(before))},
            vmem=32,
        )

    def ffn0(self):
        self.wide = self.ffn(0, self.normed2_0, self.sib2_0, ())

    def ffn1(self):
        self.hidden, self.d_gate, self.d_up, self.normed2 = self.ffn(1, self.normed2_1, self.sib2_1, self.wide)

    def grad(self, left, right, tiles, column=0, columns=None):
        columns = columns or right.shape[1]
        tile = left.shape[1] // tiles
        return self.chain.call(
            grad_kernel,
            [shape((left.shape[1], columns), BF16)],
            [left, right],
            [
                pl.BlockSpec((self.length, tile), lambda i: (0, i)),
                pl.BlockSpec((self.length, columns), lambda i: (0, column)),
            ],
            [pl.BlockSpec((tile, columns), lambda i: (i, 0))],
            grid=(tiles,),
            vmem=28,
        )[0]

    def eight(self, field):
        return field.reshape(8, field.shape[0] // 8, field.shape[1])

    def down(self):
        for way in range(2):
            grad = self.grad(self.hidden, self.cot, 3, way, self.middle)

            def write(k, piece, way=way):
                self.down_sum = self.place(self.down_sum, piece[None], (k, 0, way * self.middle))

            self.ring_a.begin(way, [self.eight(grad)], write)

    @staticmethod
    def place(target, piece, position):
        return lax.dynamic_update_slice(target, piece.astype(F32), position, allow_negative_indices=False)

    def gate_up(self, way, d_wide):
        grad = self.grad(self.normed2, d_wide, 3)

        def write(k, piece):
            self.gate_up_sum = self.place(self.gate_up_sum, piece[None, None], (way, k, 0, 0))

        self.ring_b.begin(way, [self.eight(grad)], write)

    def gate(self):
        self.gate_up(0, self.d_gate)

    def up(self):
        self.gate_up(1, self.d_up)

    def rows_back(self, side, lefts, rights, specs, dims, extra=()):
        tile = self.width // 4
        lefts = [left.reshape(2, 2, self.quarter, self.units) for left in lefts]
        column = pl.BlockSpec((self.half, tile), lambda i: (0, i))
        return self.chain.call(
            functools.partial(rows_back_kernel, dims, len(lefts)),
            [shape((self.half, self.width), BF16)],
            [*lefts, *rights, *extra],
            [pl.BlockSpec((2, 1, self.quarter, self.units), lambda i: (0, side, 0, 0))] * len(lefts)
            + specs
            + [column] * len(extra),
            [column],
            grid=(4,),
        )[0]

    def dn(self, side, extra=()):
        tile = self.width // 4
        specs = [pl.BlockSpec((1, tile, self.units), lambda i, n=n: (n, i, 0)) for n in range(2)]
        return self.rows_back(side, [self.d_gate, self.d_up], [self.gate_up_w] * 2, specs, NT, extra)

    def dnsib(self):
        self.dn_from = swap_core(self.dn(1))

    def dnown(self):
        self.dn_chip = self.dn(0, (self.dn_from,))
        self.dn_x = swap_x(self.dn_chip)

    def fo(self, side, extra=()):
        tile = self.width // 4
        specs = [pl.BlockSpec((self.units, tile), lambda i: (0, i))]
        return self.rows_back(side, [self.hidden], [self.down_w], specs, NN, extra)

    def fosib(self):
        self.fo_from = swap_core(self.fo(1))

    def foown(self):
        self.fo_chip = self.fo(0, (self.fo_from,))
        self.fo_x = swap_x(self.fo_chip)

    def nback(self):
        q, w, c = self.quarter, self.width, 2 * self.cols
        self.d_residual, self.d_res_low, self.d_heads, self.norm2_part = self.chain.call(
            norm2_back_kernel,
            [shape((self.half, w), F32), shape((self.half, w), BF16), shape((self.half, c), BF16), shape((1, w), F32)],
            [
                self.residual, self.dn_chip, self.dn_x, self.cot.reshape(2, 2, q, w), self.gain2, self.out_w, self.out_sib,
            ],
            [
                self.rows(), self.rows(), self.rows(), pl.BlockSpec((1, 1, q, w), lambda i: (i, 0, 0, 0)),
                whole(self.gain2), whole(self.out_w), whole(self.out_sib),
            ],
            [self.rows(), self.rows(), pl.BlockSpec((q, c), lambda i: (i, 0)), pl.BlockSpec((1, w), lambda i: (0, 0))],
            grid=(2,),
            vmem=32,
        )

    def aback(self):
        ins = [self.rot_q0, self.rot_q1, self.log0, self.log1, self.d_heads, self.keys, self.values, self.table]
        outs = [
            shape((self.half, 2 * self.cols), BF16),
            shape((self.half, 2 * self.head_dim), F32),
            shape((self.half, 2 * self.head_dim), BF16),
        ]
        self.d_queries, self.kv_own, kv_sib = self.chain.call(
            functools.partial(attend_back_kernel, self.scale),
            outs,
            ins,
            [whole(a) for a in ins],
            [whole(a) for a in outs],
            grid=(1,),
            scalars=[self.core[None]],
            scratch=[pltpu.VMEM((self.length, self.head_dim), F32)] * 2,
        )
        self.kv_from = swap_core(kv_sib)

    def outg(self):
        outs = [shape(self.out_w.shape, F32), shape(self.out_w.shape, BF16)]
        ins = [self.head_out0, self.head_out1, self.d_res_low]
        self.out_mine, other = self.chain.call(
            functools.partial(split_grad_kernel, self.cols),
            outs, ins, [whole(a) for a in ins], [whole(a) for a in outs], grid=(1,),
        )
        self.out_from = swap_core(other)

    def qg(self):
        outs = [shape(self.query_w.shape, F32), shape(self.query_w.shape, BF16)]
        ins = [*self.normed1, self.d_queries]
        self.query_mine, other = self.chain.call(
            functools.partial(query_grad_kernel, self.cols),
            outs, ins, [whole(a) for a in ins], [whole(a) for a in outs], grid=(1,),
        )
        self.query_from = swap_core(other)

    def dn1(self):
        tile = self.width // 4
        row = pl.BlockSpec((tile, self.cols), lambda i: (i, 0))
        (self.dn1_chip,) = self.chain.call(
            functools.partial(rows_back_kernel, NT, 2),
            [shape((self.half, self.width), BF16)],
            [self.d_queries, self.d_queries, self.query_w, self.query_sib],
            [pl.BlockSpec((self.half, self.cols), lambda i, n=n: (0, n)) for n in range(2)] + [row, row],
            [pl.BlockSpec((self.half, tile), lambda i: (0, i))],
            grid=(4,),
        )
        self.dn1_x = swap_x(self.dn1_chip)

    def kv(self):
        own, sent = self.chain.after(self.kv_own, self.kv_from)
        self.kv_chip = (own + sent.astype(F32)).astype(BF16)
        self.kv_x = swap_x(self.kv_chip)

    def kvpart(self):
        chip, from_x = self.chain.after(self.kv_chip, self.kv_x)
        self.d_kv = (chip.astype(F32) + from_x.astype(F32)).astype(BF16)
        mine = lax.dynamic_slice_in_dim(self.d_kv, self.chip * self.head_dim, self.head_dim, 1)
        normed1 = jnp.concatenate(self.normed1, 0)
        part = dot(normed1, mine, TN)
        mine = lax.dynamic_slice_in_dim(part, self.core * self.middle, self.middle, 0)
        other = lax.dynamic_slice_in_dim(part, (1 - self.core) * self.middle, self.middle, 0).astype(BF16)
        self.kv_grad = (mine + swap_core(other).astype(F32)).astype(BF16)

    def out(self):
        chip, from_x = self.chain.after(self.fo_chip, self.fo_x)
        self.output_own = (self.residual + (chip.astype(F32) + from_x.astype(F32))).astype(BF16)
        self.output_sib = swap_core(self.output_own)

    def input(self):
        q, w, d = self.quarter, self.width, 2 * self.head_dim
        self.input_own, self.norm1_part = self.chain.call(
            norm1_back_kernel,
            [shape((self.half, w), BF16), shape((1, w), F32)],
            [self.x, self.dn1_chip, self.dn1_x, self.d_kv, self.kv_w, self.d_residual, self.gain1],
            [
                self.rows(1), self.rows(), self.rows(), pl.BlockSpec((q, d), lambda i, _: (i, 0)),
                whole(self.kv_w), self.rows(), whole(self.gain1),
            ],
            [self.rows(), pl.BlockSpec((1, w), lambda i, _: (0, 0))],
            grid=(2,),
            scalars=[self.own],
        )
        self.input_sib = swap_core(self.input_own)

    def weave_rows(self, own, sibling):
        block = (self.quarter, self.width)
        return self.chain.call(
            weave_kernel,
            [shape((self.length, self.width), BF16)],
            [own, sibling],
            [
                pl.BlockSpec(block, lambda i, _: (jnp.minimum(i, 1), 0)),
                pl.BlockSpec(block, lambda i, _: (jnp.maximum(i - 2, 0), 0)),
            ],
            [pl.BlockSpec(block, lambda i, places: (places[i], 0))],
            grid=(4,),
            scalars=[self.weave_places],
        )[0]

    def weave(self):
        self.block_output = self.weave_rows(self.output_own, self.output_sib)
        self.input_grad = self.weave_rows(self.input_own, self.input_sib)

    def sums(self):
        (parts,) = self.chain.after(jnp.concatenate([self.norm1_part, self.norm2_part], 0))
        self.norm_sums = small_sum(parts, self.n_dp)

    def E(self):
        out_grad = (self.out_mine + self.out_from.astype(F32)).astype(BF16)
        query_grad = (self.query_mine + self.query_from.astype(F32)).astype(BF16)
        self.lanes = self.cols // self.head_dim
        kv_rows = self.middle // self.lanes
        kv_wide = jnp.concatenate([self.kv_grad[i * kv_rows : (i + 1) * kv_rows] for i in range(self.lanes)], 1)
        out_grad, query_grad, kv_wide = self.chain.after(out_grad, query_grad, kv_wide)
        self.kv_sum = empty((8, kv_rows // 8, self.cols), F32)

        def write_out(k, piece):
            self.out_sum = self.place(self.out_sum, piece[None], (k, 0, 0))

        def write_query(k, piece):
            rows = self.width // 8
            self.query_sum = self.place(self.query_sum, piece[None, :rows], (k, 0, 0))
            self.kv_sum = self.place(self.kv_sum, piece[None, rows:], (k, 0, 0))

        self.ring_a.begin(0, [self.eight(out_grad)], write_out)
        self.ring_a.begin(1, [self.eight(query_grad), self.eight(kv_wide)], write_query)

    def a(self):
        self.ring_a.step()

    def b(self):
        self.ring_b.step()

    def results(self):
        d = self.head_dim
        wide = self.kv_sum.reshape(-1, self.cols)
        tall = jnp.concatenate([wide[:, i * d : (i + 1) * d] for i in range(self.lanes)], 0).astype(BF16)
        halves = jnp.stack([tall, swap_core(tall)])
        column = jnp.where(self.core == 0, halves, halves[::-1]).reshape(self.width, d)
        columns = jnp.stack([column, swap_x(column)])
        columns = jnp.where(self.chip == 0, columns, columns[::-1])
        kv_grad = jnp.concatenate([columns[0], columns[1]], 1).astype(F32)
        return (
            self.block_output,
            self.input_grad,
            self.norm_sums[0],
            self.query_sum.reshape(self.width, self.cols),
            kv_grad,
            self.out_sum.reshape(self.cols, self.width),
            self.norm_sums[1],
            self.gate_up_sum.reshape(2, self.width, self.units),
            self.down_sum.reshape(self.units, self.width),
        )


def solution(mesh):
    n_dp = mesh.shape["dp"]

    def local(*args):
        block = Block(n_dp, args)
        for name in ORDER:
            getattr(block, name)()
        return block.results()

    return jax.shard_map(
        local,
        mesh=mesh,
        in_specs=(
            P("dp", None),
            P(),
            P(None, "tensor"),
            P(),
            P("tensor", None),
            P(),
            P(None, None, "tensor"),
            P("tensor", None),
            P("dp", None),
        ),
        out_specs=(
            P("dp", None),
            P("dp", None),
            P(),
            P(None, "tensor"),
            P(),
            P("tensor", None),
            P(),
            P(None, None, "tensor"),
            P("tensor", None),
        ),
        check_vma=False,
    )
```

```python
import functools
import math

import jax
import jax.numpy as jnp
import numpy as np
from jax import lax
from jax.experimental import pallas as pl
from jax.experimental.pallas import tpu as pltpu
from jax.sharding import PartitionSpec as P

WINDOW = 1024
EPSILON = 1e-06
GELU_COEF = 0.7978845608028654
BF16 = jnp.bfloat16
F32 = jnp.float32
NN = (((1,), (0,)), ((), ()))
NT = (((1,), (1,)), ((), ()))
TN = (((0,), (0,)), ((), ()))

RING = (0, 2, 4, 6, 7, 5, 3, 1)

ANY = pl.BlockSpec(memory_space=pl.ANY)
SMEM = pl.BlockSpec(memory_space=pltpu.SMEM)
VMEM = pl.BlockSpec(memory_space=pltpu.VMEM)
MIB = 2**20
COST = pl.CostEstimate(flops=0, bytes_accessed=0, transcendentals=0)

ORDER = " ".join(
    (
        "project attend0 attend1 dhidden0",
        "norm0 dhidden1 ffn0 dnsib0",
        "norm1 ffn1 wide dnown0",
        "down b a dnsib1",
        "a dnown1 b a",
        "nback0 a aback0 b",
        "a fosib1 nback1 a",
        "b aback1 fosib0 a",
        "kv b late kvpart",
        "a dn11 E b",
        "e e b a",
        "e input1 dn10 foown0",
        "e a b e",
        "input0 sums e a",
        "b sums1 sums2 e",
        "foown1 sums4 e b",
        "out0 e sumscore a",
        "e out1 sumschip b",
        "e weave putwide0 a",
        "b a e sumsend",
        "e b putdown e",
        "putlate b putwide1",
    )
).split()


def dot(left, right, dims=NN):
    return lax.dot_general(left, right, dims, preferred_element_type=F32)


def swap_core(field):
    return lax.ppermute(field, "tensor", [(i, i ^ 1) for i in range(4)])


def swap_x(field):
    return lax.ppermute(field, "tensor", [(i, i ^ 2) for i in range(4)])


def shape(dims, dtype):
    return jax.ShapeDtypeStruct(dims, dtype)


def whole(array):
    rank = len(array.shape)
    return pl.BlockSpec(array.shape, lambda *_: (0,) * rank)


class Chain:
    def __init__(self):
        self.token = None

    def call(self, body, outs, ins, in_specs, out_specs, grid=(1,), scalars=(), vmem=16, scratch=(), aliases=None, far=(),
        far_ins=(), near=(),
    ):
        tokens = [] if self.token is None else [self.token]
        given, made = len(scalars) + len(ins), len(outs)

        def run(*refs):
            refs = refs[:given] + refs[given + len(tokens) :]
            body(*refs[: given + made], *refs[given + made + 1 :])

        outs = [pltpu.HBM(o.shape, o.dtype) if i in far else o for i, o in enumerate(outs)]
        outs = [pltpu.VMEM(o.shape, o.dtype) if i in near else o for i, o in enumerate(outs)]
        ins = [pltpu.with_memory_space_constraint(a, pltpu.HBM) if i in far_ins else a for i, a in enumerate(ins)]
        *results, self.token = pl.pallas_call(
            run,
            out_shape=outs + [shape((8, 128), F32)],
            grid_spec=pltpu.PrefetchScalarGridSpec(
                num_scalar_prefetch=len(scalars),
                grid=grid,
                in_specs=list(in_specs) + [ANY] * len(tokens),
                out_specs=list(out_specs) + [ANY],
                scratch_shapes=list(scratch),
            ),
            input_output_aliases=aliases or {},
            compiler_params=pltpu.CompilerParams(vmem_limit_bytes=vmem * MIB),
            cost_estimate=COST,
        )(*scalars, *ins, *tokens)
        return results

    def direct(self, body, outs, ins, scalars=(), far_ins=(), far=(), vmem=16, scratch=()):
        tokens = [] if self.token is None else [self.token]
        given, made = len(scalars) + len(ins), len(outs)

        def run(*refs):
            refs = refs[:given] + refs[given + len(tokens) :]
            body(*refs[: given + made], *refs[given + made + 1 :])

        ins = [pltpu.with_memory_space_constraint(a, pltpu.HBM) if i in far_ins else a for i, a in enumerate(ins)]
        in_specs = [SMEM] * len(scalars) + [ANY if i in far_ins else VMEM for i in range(len(ins))]
        *results, self.token = pl.pallas_call(
            run,
            out_shape=[pltpu.HBM(o.shape, o.dtype) if i in far else o for i, o in enumerate(outs)]
            + [shape((8, 128), F32)],
            in_specs=in_specs + [ANY] * len(tokens),
            out_specs=[ANY if i in far else VMEM for i in range(made)] + [ANY],
            scratch_shapes=list(scratch),
            compiler_params=pltpu.CompilerParams(vmem_limit_bytes=vmem * MIB),
            cost_estimate=COST,
        )(*scalars, *ins, *tokens)
        return results

    def after(self, *values):
        *values, self.token = lax.optimization_barrier((*values, self.token))
        return values


def rope(field, table, sign=1.0):
    half = field.shape[1] // 2
    other = pltpu.roll(table, half, 1)
    first = lax.broadcasted_iota(jnp.int32, table.shape, 1) < half
    cosine = jnp.where(first, table, other)
    sine = jnp.where(first, -other, table) * sign
    return field * cosine + pltpu.roll(field, half, 1) * sine


def rms_factor(field):
    return lax.rsqrt(jnp.mean(field * field, axis=1, keepdims=True) + EPSILON)


def start_all(sources, targets, done, first=0):
    copies = [pltpu.make_async_copy(s, t, done.at[first + i]) for i, (s, t) in enumerate(zip(sources, targets))]
    for copy in copies:
        copy.start()
    return copies


def project_kernel(
    core, gain, x, weight, table, keys, values, own0, own1, table0, table1, x_rows, weight_all, table_all, done
):
    quarter = own0.shape[0]
    head_dim = keys.shape[1]

    def rows(block):
        return pl.ds(block * quarter, quarter)

    copies = start_all([x.at[rows(i)] for i in range(4)], [x_rows.at[rows(i)] for i in range(4)], done)
    copies += start_all((weight, table), (weight_all, table_all), done, 4)
    for block in range(4):
        here = rows(block)
        copies[block].wait()
        field = x_rows[here, :].astype(F32)
        normed = (field * rms_factor(field) * gain[...]).astype(BF16)
        if block == 0:
            copies[4].wait()
            copies[5].wait()
        both = dot(normed, weight_all[...])
        keys[here, :] = rope(both[:, :head_dim], table_all[here, :]).astype(BF16)
        values[here, :] = both[:, head_dim:].astype(BF16)
        number, own, angles = (core[0], own0, table0) if block < 2 else (3 - core[0], own1, table1)

        @pl.when(number == block)
        def _():
            own[...] = normed
            angles[...] = table_all[here, :]


def causal(rows, columns, first_row):
    row = lax.broadcasted_iota(jnp.int32, (rows, columns), 0) + first_row
    column = lax.broadcasted_iota(jnp.int32, (rows, columns), 1)
    allowed = column <= row
    if columns > WINDOW:
        allowed = allowed & (row - column < WINDOW)
    return allowed


def attend(numbers, scale, block, normed, keys, values, table, query_w, out_w, part, rot_q, head_out, log_total, arriving):
    quarter = normed.shape[0]
    head_dim = keys.shape[1]
    heads = out_w.shape[0] // head_dim
    for side in range(2):
        arriving[side].wait()
        queries = dot(normed[...], query_w[side])
        for head in range(heads // 2):
            columns = slice(head * head_dim, (head + 1) * head_dim)
            place = side * (heads // 2) + head
            rot_q[:, place * head_dim : (place + 1) * head_dim] = (
                rope(queries[:, columns], table[...]) * scale
            ).astype(BF16)
    for number in numbers:

        @pl.when(block[0] == number)
        def _():
            span = (number + 1) * quarter
            allowed = causal(quarter, span, number * quarter)
            for head in range(heads):
                columns = slice(head * head_dim, (head + 1) * head_dim)
                scores = dot(rot_q[:, columns], keys[:span, :], NT)
                scores = jnp.where(allowed, scores, -1e30)
                top = jnp.max(scores, axis=1, keepdims=True)
                weights = jnp.exp(scores - top)
                total = jnp.sum(weights, axis=1, keepdims=True)
                probs = (weights * (1.0 / total)).astype(BF16)
                head_out[:, columns] = dot(probs, values[:span, :]).astype(BF16)
                log_total[:, head : head + 1] = top + jnp.log(total)

    arriving[2].wait()
    arriving[3].wait()
    part[...] = dot(head_out[...], out_w[...]).astype(BF16)


def attend_kernel(
    numbers, scale, gather, block, places, normed, keys, values, table, query_own, query_sib, out_own, out_sib, *refs
):
    *refs, query_w, out_w, done = refs
    columns = out_own.shape[0]
    weights = start_all(
        (query_own, query_sib, out_own, out_sib),
        (query_w.at[0], query_w.at[1], out_w.at[pl.ds(0, columns)], out_w.at[pl.ds(columns, columns)]),
        done,
    )
    if gather:
        cotangent, gate_up, part, rot_q, head_out, log_total, far_normed, far_keys, far_values, cot0, cot1, near_gate_up = refs
        quarter = normed.shape[0]
        rows = [cotangent.at[pl.ds(pl.multiple_of(places[i] * quarter, 16), quarter)] for i in range(4)]
        halves = [cot.at[pl.ds(i * quarter, quarter)] for cot in (cot0, cot1) for i in range(2)]
        sources, targets = (keys, values, *rows, gate_up), (far_keys, far_values, *halves, near_gate_up)
    else:
        down, part, rot_q, head_out, log_total, far_normed, near_down = refs
        sources, targets = (down,), (near_down,)
    kept = start_all((normed, *sources), (far_normed, *targets), done, 4)
    attend(numbers, scale, block, normed, keys, values, table, query_w, out_w, part, rot_q, head_out, log_total, weights)
    for copy in kept:
        copy.wait()


def attend_back_kernel(scale, order, core, rot_q, log_total, d_heads, keys, values, table, *refs):
    if order == 0:
        d_queries, wide_keys, wide_values = refs
        wide_keys[...] = jnp.zeros_like(wide_keys)
        wide_values[...] = jnp.zeros_like(wide_values)
    else:
        before_keys, before_values, d_queries, kv_own, kv_sib, d_keys, d_values, wide_keys, wide_values = refs
        wide_keys[...] = before_keys[...]
        wide_values[...] = before_values[...]
    quarter = rot_q.shape[0]
    head_dim = keys.shape[1]
    block = core[0] if order == 0 else 3 - core[0]
    for number in (0, 1) if order == 0 else (2, 3):

        @pl.when(block == number)
        def _():
            span = (number + 1) * quarter
            own_table = table[number * quarter : span, :]
            allowed = causal(quarter, span, number * quarter)
            for head in range(rot_q.shape[1] // head_dim):
                columns = slice(head * head_dim, (head + 1) * head_dim)
                query = rot_q[:, columns]
                d_out = d_heads[:, columns]
                scores = dot(query, keys[:span, :], NT) - log_total[:, head : head + 1]
                probs = jnp.exp(jnp.where(allowed, scores, -1e30))
                d_probs = dot(d_out, values[:span, :], NT)
                delta = jnp.sum(probs * d_probs, axis=1, keepdims=True)
                d_scores = (probs * (d_probs - delta)).astype(BF16)
                d_query = dot(d_scores, keys[:span, :]) * scale
                d_queries[:, columns] = rope(d_query, own_table, -1.0).astype(BF16)
                wide_keys[:, :span] += dot(query, d_scores, TN)
                wide_values[:, :span] += dot(d_out, probs.astype(BF16), TN)

    if order == 0:
        return

    def rows_of(number):
        return pl.ds(pl.multiple_of(number * quarter, 16), quarter)

    d_keys[...] = rope(wide_keys[...].T, table[...], -1.0)
    d_values[...] = wide_values[...].T
    for place in range(2):
        rows = slice(place * quarter, (place + 1) * quarter)
        own = rows_of(core[0] if place == 0 else 3 - core[0])
        sib = rows_of(1 - core[0] if place == 0 else 2 + core[0])
        kv_own[rows, :head_dim] = d_keys[own, :]
        kv_own[rows, head_dim:] = d_values[own, :]
        kv_sib[rows, :head_dim] = d_keys[sib, :].astype(BF16)
        kv_sib[rows, head_dim:] = d_values[sib, :].astype(BF16)


def d_hidden_kernel(cotangent, weight, d_hidden):
    d_hidden[...] = dot(cotangent[...], weight[...], NT).astype(BF16)


def norm_kernel(block, x, part, from_x, gain, upper, lower, residual, x_rows, done):
    quarter = part.shape[0]
    here = x.at[pl.ds(pl.multiple_of(block[0] * quarter, 16), quarter)]
    (copy,) = start_all((here,), (x_rows,), done)
    total = part[...].astype(F32) + from_x[...].astype(F32)
    copy.wait()
    value = x_rows[...].astype(F32) + total
    residual[...] = value
    normed = (value * rms_factor(value) * gain[...]).astype(BF16)
    cut = upper.shape[0]
    upper[...] = normed[:cut, :]
    lower[...] = normed[cut:, :]


def ffn_kernel(own0, own1, sib0, sib1, weight, d_hidden, hidden, d_gate, d_up, normed):
    first = 0
    for rows in (own0, own1, sib0, sib1):
        normed[first : first + rows.shape[0], :] = rows[...]
        first += rows.shape[0]
    gate = dot(normed[...], weight[0])
    up = dot(normed[...], weight[1])
    square = gate * gate
    inner = jnp.tanh(GELU_COEF * gate * (1.0 + 0.044715 * square))
    bell = 0.5 * (1.0 + inner)
    gelu = gate * bell
    slope = bell + 0.5 * gate * (1.0 - inner * inner) * (GELU_COEF * (1.0 + 3.0 * 0.044715 * square))
    change = d_hidden[...].astype(F32)
    hidden[...] = (gelu * up).astype(BF16)
    d_gate[...] = (change * up * slope).astype(BF16)
    d_up[...] = (change * gelu).astype(BF16)


def down_grad_kernel(place, left0, left1, right0, right1, out):
    rows, tile = out.shape[1], out.shape[2] // 2
    for i in range(2):
        here = slice(i * tile, (i + 1) * tile)
        total = dot(left0[...], right0[:, here], TN) + dot(left1[...], right1[:, here], TN)
        for number in range(8):
            out[turned(place, number), :, here] = total[number * rows : (number + 1) * rows, :].astype(BF16)


def turned(places, number, side=0):
    return (places[side] - number) & 7


def wide_grad_kernel(tiles, place, left0, left1, gate0, gate1, up0, up1, out):
    rows, columns, chunks = out.shape[1], gate0.shape[1], 8 // tiles
    for side, (right0, right1) in enumerate(((gate0, gate1), (up0, up1))):
        for i in range(tiles):
            here = slice(i * chunks * rows, (i + 1) * chunks * rows)
            total = dot(left0[:, here], right0[...], TN) + dot(left1[:, here], right1[...], TN)
            for chunk in range(chunks):
                part = total[chunk * rows : (chunk + 1) * rows, :].astype(BF16)
                out[turned(place, i * chunks + chunk), :, side * columns : (side + 1) * columns] = part


def rows_kernel(side, tiles, dims, count, *refs):
    refs, joined = refs[:-count], refs[-count:]
    chunks = joined[0].shape[0] * 2 // refs[0].shape[0]
    lefts, weight = refs[: chunks * count], refs[chunks * count]
    *extra, out = refs[chunks * count + 1 :]
    quarter = out.shape[0] // chunks
    own = slice(side * quarter, (side + 1) * quarter)
    for i, target in enumerate(joined):
        for chunk in range(chunks):
            target[chunk * quarter : (chunk + 1) * quarter, :] = lefts[chunks * i + chunk][own, :]
    tile = out.shape[1] // tiles
    for t in range(tiles):
        here = slice(t * tile, (t + 1) * tile)
        total = None
        for i, left in enumerate(joined):
            right = weight[:, here] if dims == NN else weight[i, here, :]
            term = dot(left[...], right, dims)
            total = term if total is None else total + term
        if extra:
            total = total + extra[0][:, here].astype(F32)
        out[:, here] = total.astype(BF16)


def d_normed1_kernel(d_queries, own, sibling, out):
    half = own.shape[1]
    out[...] = (dot(d_queries[:, :half], own[...], NT) + dot(d_queries[:, half:], sibling[...], NT)).astype(BF16)


def norm_back(field, gain, d_normed):
    factor = rms_factor(field)
    scaled = gain * d_normed
    d_gain = jnp.sum(d_normed * field * factor, axis=0, keepdims=True)
    return factor * scaled - field * (factor * factor * factor) * jnp.mean(scaled * field, axis=1, keepdims=True), d_gain


def norm2_back_kernel(
    residual, on_chip, from_x, cotangent, gain, out_own, out_sib, d_residual, d_res_low, d_heads, d_gain
):
    d_normed = on_chip[...].astype(F32) + from_x[...].astype(F32)
    change, d_gain[...] = norm_back(residual[...], gain[...], d_normed)
    total = cotangent[...].astype(F32) + change
    d_residual[...] = total
    low = total.astype(BF16)
    d_res_low[...] = low
    half = out_own.shape[0]
    d_heads[:, :half] = dot(low, out_own[...], NT).astype(BF16)
    d_heads[:, half:] = dot(low, out_sib[...], NT).astype(BF16)


def norm1_back_kernel(block, x, on_chip, from_x, d_kv, d_residual, kv_weight, gain, d_input, d_gain):
    d_normed = (on_chip[...].astype(F32) + from_x[...].astype(F32)) + dot(d_kv[...], kv_weight[...], NT)
    change, d_gain[...] = norm_back(x[...].astype(F32), gain[...], d_normed)
    d_input[...] = (d_residual[...] + change).astype(BF16)


def late_grad_kernel(
    columns, place, normed0, normed1, d_queries0, d_queries1, head_out0, head_out1, d_res_low0, d_res_low1, mine, other
):
    rows = mine.shape[1]
    for side, out in enumerate((mine, other)):
        part = slice(side * columns, (side + 1) * columns)
        query = dot(normed0[...], d_queries0[:, part], TN) + dot(normed1[...], d_queries1[:, part], TN)
        outer = dot(head_out0[:, part], d_res_low0[...], TN) + dot(head_out1[:, part], d_res_low1[...], TN)
        folds = outer.shape[1] // columns
        short = rows // folds
        for number in range(8):
            spot = turned(place, number, side)
            out[spot, :, :columns] = query[number * rows : (number + 1) * rows, :].astype(out.dtype)
            for fold in range(folds):
                out[spot, fold * short : (fold + 1) * short, columns:] = outer[
                    number * short : (number + 1) * short, fold * columns : (fold + 1) * columns
                ].astype(out.dtype)


def weave_kernel(places, *refs):
    *refs, first, second, done = refs
    quarter = refs[0].shape[0]
    copies = []
    for i, source in enumerate(refs):
        target = (first, second)[i // 4]
        rows = pl.ds(pl.multiple_of(places[i % 4] * quarter, 16), quarter)
        copies += start_all((source,), (target.at[rows],), done, i)
    for copy in copies:
        copy.wait()


def assemble_kernel(first, old, count, place, *refs):
    pieces, refs = refs[:count], refs[count + old :]
    *targets, stage, done = refs
    rows, width = pieces[0].shape
    flying = [None, None]
    for i, piece in enumerate(pieces):
        slot = i % 2
        k = (place[0] - first - i) & 7
        for copy in flying[slot] or ():
            copy.wait()
        stage[slot] = piece[...].astype(F32)
        if len(targets) == 1 and targets[0].shape[0] == 2:
            half = width // 2
            moves = [(stage.at[slot, :, n * half : (n + 1) * half], targets[0].at[n, k]) for n in range(2)]
        elif len(targets) == 1:
            moves = [(stage.at[slot], targets[0].at[k])]
        else:
            half = width // 2
            folds = targets[1].shape[2] // half
            short = rows // folds
            moves = [(stage.at[slot, :, :half], targets[0].at[k])]
            moves += [
                (stage.at[slot, n * short : (n + 1) * short, half:], targets[1].at[k, :, n * half : (n + 1) * half])
                for n in range(folds)
            ]
        flying[slot] = [pltpu.make_async_copy(s, t, done.at[slot, n]) for n, (s, t) in enumerate(moves)]
        for copy in flying[slot]:
            copy.start()
    for copies in flying:
        for copy in copies or ():
            copy.wait()


def ring_orders():
    return [RING if tensor % 2 == 0 else RING[::-1] for tensor in range(4)]


def ring_pairs():
    return [
        (order[i] * 4 + tensor, order[(i + 1) % 8] * 4 + tensor) for tensor, order in enumerate(ring_orders()) for i in range(8)
    ]


def ring_places():
    places = np.zeros((8, 2, 2), np.int32)
    for core, order in enumerate((RING, RING[::-1])):
        for i, device in enumerate(order):
            places[device, core, 0] = places[device, 1 - core, 1] = i
    return places.reshape(8, 4)


class Ring:
    def __init__(self, chain, place):
        self.chain, self.place, self.left = chain, place, 0

    def begin(self, field):
        self.field, self.travelling, self.pieces, self.left = field, field[1], [], 14
        self.send()

    def send(self):
        self.arrived = lax.ppermute(self.travelling, ("dp", "tensor"), ring_pairs())

    def step(self):
        if self.left == 0:
            raise ValueError("ring idle")
        self.left -= 1
        number = 14 - self.left
        (self.travelling,) = self.chain.after(self.arrived)
        if number <= 7:
            mine = self.field[(number + 1) % 8].astype(F32)
            (self.travelling,) = self.chain.after((self.travelling.astype(F32) + mine).astype(BF16))
        if number >= 7:
            self.pieces.append(self.travelling)
        if self.left:
            self.send()

    def assemble(self, targets, first, last):
        pieces = self.pieces[first:last]
        old = [t for t in targets if isinstance(t, jax.Array)]
        return self.chain.call(
            functools.partial(assemble_kernel, first, len(old), len(pieces)),
            [shape(t.shape, F32) for t in targets],
            [*pieces, *old],
            [whole(p) for p in pieces] + [ANY] * len(old),
            [ANY] * len(targets),
            scalars=[self.place],
            scratch=[pltpu.VMEM((2,) + pieces[0].shape, F32), pltpu.SemaphoreType.DMA((2, 8))],
            aliases={1 + len(pieces) + i: i for i in range(len(old))},
            vmem=16,
        )


class Whole:
    def __init__(self, chain, place):
        self.chain, self.place = chain, place

    def begin(self, field):
        total = lax.psum(field, "dp")
        self.pieces = [total[i] for i in range(8)]

    def step(self):
        pass

    assemble = Ring.assemble


def over_dp(field, step, n_dp):
    return field.astype(F32) + lax.ppermute(field, "dp", [(i, i ^ step) for i in range(n_dp)]).astype(F32)


class Block:
    def __init__(self, n_dp, args):
        (
            self.x, self.gain1, self.query_w, self.kv_w, self.out_w, self.gain2, self.gate_up_w, self.down_w, self.cot_in,
        ) = args
        self.gain1, self.gain2 = self.gain1[None], self.gain2[None]
        self.n_dp = n_dp
        self.length, self.width = self.x.shape
        self.quarter, self.half = self.length // 4, self.length // 2
        self.head_dim = self.kv_w.shape[1] // 2
        self.cols = self.query_w.shape[1]
        self.units = self.down_w.shape[0]
        self.middle = self.width // 2
        self.scale = 1.0 / math.sqrt(self.head_dim)
        tensor = lax.axis_index("tensor")
        self.core, self.chip = tensor & 1, tensor >> 1
        core = self.core
        self.own = jnp.stack([core, 3 - core])
        self.places = jnp.stack([core, 1 - core, 3 - core, 2 + core])
        self.weave_places = jnp.stack([core, 3 - core, 1 - core, 2 + core])
        self.chain = Chain()
        if n_dp == 8:
            self.ring_place = lax.dynamic_slice(
                jnp.asarray(ring_places()), (lax.axis_index("dp"), 2 * core), (1, 2), allow_negative_indices=False
            )[0]
        else:
            self.ring_place = jnp.zeros(2, jnp.int32)
        ring = Ring if n_dp == 8 else Whole
        self.ring_a, self.ring_b, self.ring_e = (ring(self.chain, self.ring_place) for _ in range(3))
        half_dim = self.head_dim // 2
        angle = np.arange(self.length)[:, None] * 10000.0 ** (-2.0 * np.arange(half_dim)[None, :] / self.head_dim)
        self.table = jnp.asarray(np.concatenate([np.cos(angle), np.sin(angle)], 1), F32)
        self.query_sib = swap_core(self.query_w)
        self.out_sib = swap_core(self.out_w)
    def rows(self, table=None):
        if table is None:
            return pl.BlockSpec((self.quarter, self.width), lambda i, *_: (i, 0))
        return pl.BlockSpec((self.quarter, self.width), lambda i, places: (places[i], 0))

    def project(self):
        q, d, w, n = self.quarter, self.head_dim, self.width, self.length
        outs = [shape((n, d), BF16)] * 2 + [shape((q, w), BF16)] * 2 + [shape((q, d), F32)] * 2
        self.keys, self.values, own0, own1, table0, table1 = self.chain.direct(
            project_kernel,
            outs,
            [self.gain1, self.x, self.kv_w, self.table],
            scalars=[self.core[None]],
            far_ins=(1, 2, 3),
            scratch=[
                pltpu.VMEM(self.x.shape, BF16), pltpu.VMEM(self.kv_w.shape, BF16), pltpu.VMEM(self.table.shape, F32),
                pltpu.SemaphoreType.DMA((6,)),
            ],
        )
        self.normed1, self.own_tables, self.far_normed1 = (own0, own1), (table0, table1), []

    def attend(self, j):
        q, w, c = self.quarter, self.width, 2 * self.cols
        ins = [
            self.normed1[j], self.keys, self.values, self.own_tables[j],
            self.query_w, self.query_sib, self.out_w, self.out_sib,
        ]
        blocks = [shape((q, w), BF16), shape((q, c), BF16), shape((q, c), BF16), shape((q, 8), F32)]
        outs = [shape((q, w), BF16)]
        if j == 1:
            more, narrow, rows = [self.cot_in, self.gate_up_w], shape(self.keys.shape, BF16), shape((self.half, w), BF16)
            outs += [narrow, narrow, rows, rows, shape(self.gate_up_w.shape, BF16)]
        else:
            more = [self.down_w]
            outs += [shape(self.down_w.shape, BF16)]
        part, rot_q, head_out, log_total, far_normed, *rest = self.chain.call(
            functools.partial(attend_kernel, (0, 1) if j == 0 else (2, 3), self.scale, j == 1),
            blocks + outs,
            ins + more,
            [whole(a) for a in ins[:4]] + [ANY] * (4 + len(more)),
            [whole(b) for b in blocks] + [ANY] * len(outs),
            scalars=[self.own[j : j + 1], self.places],
            scratch=[
                pltpu.VMEM((2,) + self.query_w.shape, BF16),
                pltpu.VMEM((c, w), BF16),
                pltpu.SemaphoreType.DMA((12,)),
            ],
            far=range(1, 7) if j == 1 else range(1, 5),
            near=range(7, 10) if j == 1 else (5,),
            far_ins=range(4, 10),
            vmem=20,
        )
        self.far_normed1.append(far_normed)
        return part, rot_q, head_out, log_total, rest

    def attend0(self):
        self.part0, self.rot_q0, self.head_out0, self.log0, (self.near_down,) = self.attend(0)
        self.from_x0 = swap_x(self.part0)

    def attend1(self):
        self.part1, self.rot_q1, self.head_out1, self.log1, rest = self.attend(1)
        self.far_keys, self.far_values, cot0, cot1, self.near_gate_up = rest
        self.cot = (cot0, cot1)
        self.from_x1 = swap_x(self.part1)

    def dhidden(self, j):
        return self.chain.direct(
            d_hidden_kernel, [shape((self.half, self.units), BF16)], [self.cot[j], self.near_down]
        )[0]

    def dhidden0(self):
        self.d_hidden0 = self.dhidden(0)

    def dhidden1(self):
        self.d_hidden1 = self.dhidden(1)

    def norm(self, j, part, from_x):
        upper = (self.quarter // 32 + 1) * 16
        outs = [shape((rows, self.width), BF16) for rows in (upper, self.quarter - upper)]
        outs.append(shape((self.quarter, self.width), F32))
        upper, lower, residual = self.chain.direct(
            norm_kernel,
            outs,
            [self.x, part, from_x, self.gain2],
            scalars=[self.own[j : j + 1]],
            far_ins=(0,),
            scratch=[pltpu.VMEM((self.quarter, self.width), BF16), pltpu.SemaphoreType.DMA((1,))],
        )
        return [upper, lower, swap_core(upper), swap_core(lower)], residual

    def norm0(self):
        self.normed2_0, self.residual0 = self.norm(0, self.part0, self.from_x0)

    def norm1(self):
        self.normed2_1, self.residual1 = self.norm(1, self.part1, self.from_x1)

    def ffn(self, normed, d_hidden):
        return self.chain.direct(
            ffn_kernel,
            [shape((self.half, self.units), BF16)] * 3 + [shape((self.half, self.width), BF16)],
            [*normed, self.near_gate_up, d_hidden],
        )

    def ffn0(self):
        self.wide0 = self.ffn(self.normed2_0, self.d_hidden0)

    def ffn1(self):
        self.wide1 = self.ffn(self.normed2_1, self.d_hidden1)
        self.hidden, self.d_gate, self.d_up, self.normed2 = zip(self.wide0, self.wide1)

    def down(self):
        (grad,) = self.chain.direct(
            down_grad_kernel,
            [shape((8, self.units // 8, self.width), BF16)],
            [*self.hidden, *self.cot],
            scalars=[self.ring_place],
        )
        self.ring_a.begin(grad)

    def wide(self):
        (grad,) = self.chain.direct(
            functools.partial(wide_grad_kernel, 2),
            [shape((8, self.width // 8, 2 * self.units), BF16)],
            [*self.normed2, *self.d_gate, *self.d_up],
            scalars=[self.ring_place],
        )
        self.ring_b.begin(grad)

    def putdown(self):
        (self.down_sum,) = self.ring_a.assemble([shape((8, self.units // 8, self.width), F32)], 0, 8)

    def putwide0(self):
        (self.gate_up_sum,) = self.ring_b.assemble([shape((2, 8, self.width // 8, self.units), F32)], 0, 4)

    def putwide1(self):
        (self.gate_up_sum,) = self.ring_b.assemble([self.gate_up_sum], 4, 8)

    def putlate(self):
        self.query_sum, self.out_sum = self.ring_e.assemble(
            [shape((8, self.width // 8, self.cols), F32), shape((8, self.cols // 8, self.width), F32)], 0, 8
        )

    def rows_back(self, side, chunks, lefts, weight, dims, extra):
        rows, count = chunks * self.quarter, len(lefts) // chunks
        return self.chain.direct(
            functools.partial(rows_kernel, side, 3, dims, count),
            [shape((rows, self.width), BF16)],
            [*lefts, weight, *extra],
            scratch=[pltpu.VMEM((rows, self.units), BF16)] * count,
        )[0]

    def dn(self, side, wide, extra=()):
        return self.rows_back(side, 1, wide[1:3], self.near_gate_up, NT, extra)

    def dnsib0(self):
        self.dn_from0 = swap_core(self.dn(1, self.wide0))

    def dnown0(self):
        self.dn_chip0 = self.dn(0, self.wide0, (self.dn_from0,))
        self.dn_x0 = swap_x(self.dn_chip0)

    def dnsib1(self):
        self.dn_from1 = swap_core(self.dn(1, self.wide1))

    def dnown1(self):
        self.dn_chip1 = self.dn(0, self.wide1, (self.dn_from1,))
        self.dn_x1 = swap_x(self.dn_chip1)

    def fo(self, side, wide, extra=()):
        return self.rows_back(side, 1, wide[:1], self.near_down, NN, extra)

    def fosib0(self):
        self.fo_from0 = swap_core(self.fo(1, self.wide0))

    def fosib1(self):
        self.fo_from1 = swap_core(self.fo(1, self.wide1))

    def foown0(self):
        self.fo_chip0 = self.fo(0, self.wide0, (self.fo_from0,))
        self.fo_x0 = swap_x(self.fo_chip0)

    def foown1(self):
        self.fo_chip1 = self.fo(0, self.wide1, (self.fo_from1,))
        self.fo_x1 = swap_x(self.fo_chip1)

    def nback(self, residual, on_chip, from_x, cot):
        q, w, c = self.quarter, self.width, 2 * self.cols
        outs = [shape((q, w), F32), shape((q, w), BF16), shape((q, c), BF16), shape((1, w), F32)]
        ins = [residual, on_chip, from_x, cot, self.gain2, self.out_w, self.out_sib]
        specs = [whole(a) for a in ins]
        specs[3] = pl.BlockSpec((q, w), lambda i: (0, 0))
        return self.chain.call(norm2_back_kernel, outs, ins, specs, [whole(o) for o in outs], far=(0, 1))

    def nback0(self):
        self.d_residual0, self.d_res_low0, self.d_heads0, self.norm2_part0 = self.nback(
            self.residual0, self.dn_chip0, self.dn_x0, self.cot[0]
        )

    def nback1(self):
        self.d_residual1, self.d_res_low1, self.d_heads1, self.norm2_part1 = self.nback(
            self.residual1, self.dn_chip1, self.dn_x1, self.cot[1]
        )

    def aback0(self):
        ins = [self.rot_q0, self.log0, self.d_heads0, self.far_keys, self.far_values, self.table]
        wide = shape((self.head_dim, self.length), F32)
        outs = [shape((self.quarter, 2 * self.cols), BF16), wide, wide]
        self.d_queries0, self.wide_keys, self.wide_values = self.chain.call(
            functools.partial(attend_back_kernel, self.scale, 0),
            outs,
            ins,
            [whole(a) for a in ins],
            [whole(a) for a in outs],
            scalars=[self.core[None]],
            far=(0,),
        )

    def aback1(self):
        ins = [self.rot_q1, self.log1, self.d_heads1, self.far_keys, self.far_values, self.table]
        ins += [self.wide_keys, self.wide_values]
        outs = [
            shape((self.quarter, 2 * self.cols), BF16),
            shape((self.half, 2 * self.head_dim), F32),
            shape((self.half, 2 * self.head_dim), BF16),
        ]
        self.d_queries1, self.kv_own, kv_sib = self.chain.call(
            functools.partial(attend_back_kernel, self.scale, 1),
            outs,
            ins,
            [whole(a) for a in ins],
            [whole(a) for a in outs],
            scalars=[self.core[None]],
            scratch=[pltpu.VMEM((self.length, self.head_dim), F32)] * 2
            + [pltpu.VMEM((self.head_dim, self.length), F32)] * 2,
        )
        self.d_queries = (self.d_queries0, self.d_queries1)
        self.kv_from = swap_core(kv_sib)

    def late(self):
        self.late_mine, other = self.chain.direct(
            functools.partial(late_grad_kernel, self.cols),
            [shape((8, self.width // 8, 2 * self.cols), t) for t in (F32, BF16)],
            [
                *self.far_normed1, *self.d_queries, self.head_out0, self.head_out1, self.d_res_low0, self.d_res_low1,
            ],
            scalars=[self.ring_place],
        )
        self.late_from = swap_core(other)

    def dn1(self, d_queries):
        tile = pl.BlockSpec((self.width // 3, self.cols), lambda i: (i, 0))
        return self.chain.call(
            d_normed1_kernel,
            [shape((self.quarter, self.width), BF16)],
            [d_queries, self.query_w, self.query_sib],
            [whole(d_queries), tile, tile],
            [pl.BlockSpec((self.quarter, self.width // 3), lambda i: (0, i))],
            grid=(3,),
        )[0]

    def dn10(self):
        self.dn1_chip0 = self.dn1(self.d_queries0)
        self.dn1_x0 = swap_x(self.dn1_chip0)

    def dn11(self):
        self.dn1_chip1 = self.dn1(self.d_queries1)
        self.dn1_x1 = swap_x(self.dn1_chip1)

    def kv(self):
        own, sent = self.chain.after(self.kv_own, self.kv_from)
        self.kv_chip = (own + sent.astype(F32)).astype(BF16)
        self.kv_x = swap_x(self.kv_chip)

    def kvpart(self):
        chip, from_x = self.chain.after(self.kv_chip, self.kv_x)
        self.d_kv = (chip.astype(F32) + from_x.astype(F32)).astype(BF16)
        mine = lax.dynamic_slice_in_dim(self.d_kv, self.chip * self.head_dim, self.head_dim, 1)
        normed1 = jnp.concatenate(self.far_normed1, 0)
        part = dot(normed1, mine, TN)
        mine = lax.dynamic_slice_in_dim(part, self.core * self.middle, self.middle, 0)
        other = lax.dynamic_slice_in_dim(part, (1 - self.core) * self.middle, self.middle, 0).astype(BF16)
        self.kv_grad = (mine + swap_core(other).astype(F32)).astype(BF16)

    def out(self, residual, chip, from_x):
        chip, from_x = self.chain.after(chip, from_x)
        own = (residual + (chip.astype(F32) + from_x.astype(F32))).astype(BF16)
        return own, swap_core(own)

    def out0(self):
        self.output_own0, self.output_sib0 = self.out(self.residual0, self.fo_chip0, self.fo_x0)

    def out1(self):
        self.output_own1, self.output_sib1 = self.out(self.residual1, self.fo_chip1, self.fo_x1)

    def input(self, j, on_chip, from_x, d_residual):
        q, w, d = self.quarter, self.width, 2 * self.head_dim
        block = pl.BlockSpec((q, w), lambda i, _: (0, 0))
        own, part = self.chain.call(
            norm1_back_kernel,
            [shape((q, w), BF16), shape((1, w), F32)],
            [self.x, on_chip, from_x, self.d_kv, d_residual, self.kv_w, self.gain1],
            [
                self.rows(1), block, block, pl.BlockSpec((q, d), lambda i, _: (j, 0)), block, whole(self.kv_w),
                whole(self.gain1),
            ],
            [block, pl.BlockSpec((1, w), lambda i, _: (0, 0))],
            scalars=[self.own[j : j + 1]],
            far_ins=(0, 5),
        )
        return own, swap_core(own), part

    def input0(self):
        self.input_own0, self.input_sib0, self.norm1_part0 = self.input(0, self.dn1_chip0, self.dn1_x0, self.d_residual0)

    def input1(self):
        self.input_own1, self.input_sib1, self.norm1_part1 = self.input(1, self.dn1_chip1, self.dn1_x1, self.d_residual1)

    def weave(self):
        ins = [self.output_own0, self.output_own1, self.output_sib0, self.output_sib1]
        ins += [self.input_own0, self.input_own1, self.input_sib0, self.input_sib1]
        self.block_output, self.input_grad = self.chain.direct(
            weave_kernel,
            [shape((self.length, self.width), BF16)] * 2,
            ins,
            scalars=[self.weave_places],
            far=(0, 1),
            scratch=[pltpu.SemaphoreType.DMA((8,))],
        )

    def sums(self):
        d = self.head_dim
        gains = jnp.concatenate([self.norm1_part0 + self.norm1_part1, self.norm2_part0 + self.norm2_part1], 0).reshape(-1, d).astype(BF16)
        self.small = jnp.concatenate([self.kv_grad, gains], 0)
        if self.n_dp & (self.n_dp - 1):
            self.small = lax.psum(self.small, "dp")

    def small_step(self, step):
        if self.n_dp & (self.n_dp - 1):
            return
        while step < self.n_dp:
            (small,) = self.chain.after(self.small)
            self.small = over_dp(small, step, self.n_dp).astype(BF16)
            if step < 4:
                return
            step *= 2

    def sums1(self):
        self.small_step(1)

    def sums2(self):
        self.small_step(2)

    def sums4(self):
        self.small_step(4)

    def sumscore(self):
        (small,) = self.chain.after(self.small)
        self.from_core = swap_core(small)
        self.small = small

    def sumschip(self):
        d, rows = self.head_dim, self.middle
        mine, other = self.chain.after(self.small, self.from_core)
        total = mine[rows:].astype(F32) + other[rows:].astype(F32)
        self.norm_sums = total.reshape(2, self.width)
        halves = jnp.stack([mine[:rows], other[:rows]])
        self.kv_column = jnp.where(self.core == 0, halves, halves[::-1]).reshape(self.width, d)
        self.kv_other = swap_x(self.kv_column)

    def sumsend(self):
        mine, other = self.chain.after(self.kv_column, self.kv_other)
        columns = jnp.stack([mine, other])
        columns = jnp.where(self.chip == 0, columns, columns[::-1])
        self.kv_out = jnp.concatenate([columns[0], columns[1]], 1).astype(F32)

    def E(self):
        (grad,) = self.chain.after((self.late_mine + self.late_from.astype(F32)).astype(BF16))
        self.ring_e.begin(grad)

    def e(self):
        self.ring_e.step()

    def a(self):
        self.ring_a.step()

    def b(self):
        self.ring_b.step()

    def results(self):
        return (
            self.block_output,
            self.input_grad,
            self.norm_sums[0],
            self.query_sum.reshape(self.width, self.cols),
            self.kv_out,
            self.out_sum.reshape(self.cols, self.width),
            self.norm_sums[1],
            self.gate_up_sum.reshape(2, self.width, self.units),
            self.down_sum.reshape(self.units, self.width),
        )


def solution(mesh):
    n_dp = mesh.shape["dp"]

    def local(*args):
        block = Block(n_dp, args)
        for name in ORDER:
            getattr(block, name)()
        return block.results()

    return jax.shard_map(
        local,
        mesh=mesh,
        in_specs=(
            P("dp", None),
            P(),
            P(None, "tensor"),
            P(),
            P("tensor", None),
            P(),
            P(None, None, "tensor"),
            P("tensor", None),
            P("dp", None),
        ),
        out_specs=(
            P("dp", None),
            P("dp", None),
            P(),
            P(None, "tensor"),
            P(),
            P("tensor", None),
            P(),
            P(None, None, "tensor"),
            P("tensor", None),
        ),
        check_vma=False,
    )
```

```python
import functools
import math

import jax
import jax.numpy as jnp
import numpy as np
from jax import lax
from jax.experimental import pallas as pl
from jax.experimental.pallas import tpu as pltpu
from jax.sharding import PartitionSpec as P

WINDOW = 1024
EPSILON = 1e-06
GELU_COEF = 0.7978845608028654
BF16 = jnp.bfloat16
F32 = jnp.float32
NN = (((1,), (0,)), ((), ()))
NT = (((1,), (1,)), ((), ()))
TN = (((0,), (0,)), ((), ()))

RING = (0, 2, 4, 6, 7, 5, 3, 1)

ANY = pl.BlockSpec(memory_space=pl.ANY)
SMEM = pl.BlockSpec(memory_space=pltpu.SMEM)
VMEM = pl.BlockSpec(memory_space=pltpu.VMEM)
MIB = 2**20
COST = pl.CostEstimate(flops=0, bytes_accessed=0, transcendentals=0)

ORDER = " ".join(
    (
        "project attend0 attend1 dhidden0",
        "norm0 dhidden1 ffn0 dnsib0",
        "norm1 ffn1 wide dnown0",
        "down b a dnsib1",
        "a dnown1 b a",
        "nback0 a aback0 nback1",
        "b a aback1 a",
        "b late kv a",
        "b fosib1 fosib0 kvpart",
        "a dn11 E b",
        "e e b a",
        "e input1 dn10 foown0",
        "e a b e",
        "input0 sums e a",
        "b sums1 sums2 e",
        "foown1 sums4 e b",
        "out0 e sumscore a",
        "e out1 sumschip b",
        "e weave a b",
        "a e sumsend putdown",
        "e b putwide0 e",
        "putlate b putwide1",
    )
).split()


def dot(left, right, dims=NN):
    return lax.dot_general(left, right, dims, preferred_element_type=F32)


def swap_core(field):
    return lax.ppermute(field, "tensor", [(i, i ^ 1) for i in range(4)])


def swap_x(field):
    return lax.ppermute(field, "tensor", [(i, i ^ 2) for i in range(4)])


def shape(dims, dtype):
    return jax.ShapeDtypeStruct(dims, dtype)


def whole(array):
    rank = len(array.shape)
    return pl.BlockSpec(array.shape, lambda *_: (0,) * rank)


class Chain:
    def __init__(self):
        self.token = None

    def call(self, body, outs, ins, in_specs, out_specs, grid=(1,), scalars=(), vmem=16, scratch=(), aliases=None, far=(),
        far_ins=(), near=(),
    ):
        tokens = [] if self.token is None else [self.token]
        given, made = len(scalars) + len(ins), len(outs)

        def run(*refs):
            refs = refs[:given] + refs[given + len(tokens) :]
            body(*refs[: given + made], *refs[given + made + 1 :])

        outs = [pltpu.HBM(o.shape, o.dtype) if i in far else o for i, o in enumerate(outs)]
        outs = [pltpu.VMEM(o.shape, o.dtype) if i in near else o for i, o in enumerate(outs)]
        ins = [pltpu.with_memory_space_constraint(a, pltpu.HBM) if i in far_ins else a for i, a in enumerate(ins)]
        *results, self.token = pl.pallas_call(
            run,
            out_shape=outs + [shape((8, 128), F32)],
            grid_spec=pltpu.PrefetchScalarGridSpec(
                num_scalar_prefetch=len(scalars),
                grid=grid,
                in_specs=list(in_specs) + [ANY] * len(tokens),
                out_specs=list(out_specs) + [ANY],
                scratch_shapes=list(scratch),
            ),
            input_output_aliases=aliases or {},
            compiler_params=pltpu.CompilerParams(vmem_limit_bytes=vmem * MIB),
            cost_estimate=COST,
        )(*scalars, *ins, *tokens)
        return results

    def direct(self, body, outs, ins, scalars=(), far_ins=(), far=(), vmem=16, scratch=()):
        tokens = [] if self.token is None else [self.token]
        given, made = len(scalars) + len(ins), len(outs)

        def run(*refs):
            refs = refs[:given] + refs[given + len(tokens) :]
            body(*refs[: given + made], *refs[given + made + 1 :])

        ins = [pltpu.with_memory_space_constraint(a, pltpu.HBM) if i in far_ins else a for i, a in enumerate(ins)]
        in_specs = [SMEM] * len(scalars) + [ANY if i in far_ins else VMEM for i in range(len(ins))]
        *results, self.token = pl.pallas_call(
            run,
            out_shape=[pltpu.HBM(o.shape, o.dtype) if i in far else o for i, o in enumerate(outs)]
            + [shape((8, 128), F32)],
            in_specs=in_specs + [ANY] * len(tokens),
            out_specs=[ANY if i in far else VMEM for i in range(made)] + [ANY],
            scratch_shapes=list(scratch),
            compiler_params=pltpu.CompilerParams(vmem_limit_bytes=vmem * MIB),
            cost_estimate=COST,
        )(*scalars, *ins, *tokens)
        return results

    def after(self, *values):
        *values, self.token = lax.optimization_barrier((*values, self.token))
        return values


def rope(field, table, sign=1.0):
    half = field.shape[1] // 2
    other = pltpu.roll(table, half, 1)
    first = lax.broadcasted_iota(jnp.int32, table.shape, 1) < half
    cosine = jnp.where(first, table, other)
    sine = jnp.where(first, -other, table) * sign
    return field * cosine + pltpu.roll(field, half, 1) * sine


def rms_factor(field):
    return lax.rsqrt(jnp.mean(field * field, axis=1, keepdims=True) + EPSILON)


def start_all(sources, targets, done, first=0):
    copies = [pltpu.make_async_copy(s, t, done.at[first + i]) for i, (s, t) in enumerate(zip(sources, targets))]
    for copy in copies:
        copy.start()
    return copies


def project_kernel(
    core, gain, x, weight, table, keys, values, own0, own1, table0, table1, x_rows, weight_all, table_all, done
):
    quarter = own0.shape[0]
    head_dim = keys.shape[1]

    def rows(block):
        return pl.ds(block * quarter, quarter)

    copies = start_all([x.at[rows(i)] for i in range(4)], [x_rows.at[rows(i)] for i in range(4)], done)
    copies += start_all((weight, table), (weight_all, table_all), done, 4)
    for block in range(4):
        here = rows(block)
        copies[block].wait()
        field = x_rows[here, :].astype(F32)
        normed = (field * rms_factor(field) * gain[...]).astype(BF16)
        if block == 0:
            copies[4].wait()
            copies[5].wait()
        both = dot(normed, weight_all[...])
        keys[here, :] = rope(both[:, :head_dim], table_all[here, :]).astype(BF16)
        values[here, :] = both[:, head_dim:].astype(BF16)
        number, own, angles = (core[0], own0, table0) if block < 2 else (3 - core[0], own1, table1)

        @pl.when(number == block)
        def _():
            own[...] = normed
            angles[...] = table_all[here, :]


def causal(rows, columns, first_row):
    row = lax.broadcasted_iota(jnp.int32, (rows, columns), 0) + first_row
    column = lax.broadcasted_iota(jnp.int32, (rows, columns), 1)
    allowed = column <= row
    if columns > WINDOW:
        allowed = allowed & (row - column < WINDOW)
    return allowed


def attend(numbers, scale, block, normed, keys, values, table, query_w, out_w, part, rot_q, head_out, log_total, arriving):
    quarter = normed.shape[0]
    head_dim = keys.shape[1]
    heads = out_w.shape[0] // head_dim
    for side in range(2):
        arriving[side].wait()
        queries = dot(normed[...], query_w[side])
        for head in range(heads // 2):
            columns = slice(head * head_dim, (head + 1) * head_dim)
            place = side * (heads // 2) + head
            rot_q[:, place * head_dim : (place + 1) * head_dim] = (
                rope(queries[:, columns], table[...]) * scale
            ).astype(BF16)
    for number in numbers:

        @pl.when(block[0] == number)
        def _():
            span = (number + 1) * quarter
            allowed = causal(quarter, span, number * quarter)
            lane = lax.broadcasted_iota(jnp.int32, log_total.shape, 1)

            def two_heads(pair, _):
                for head in (2 * pair, 2 * pair + 1):
                    columns = pl.ds(pl.multiple_of(head * head_dim, head_dim), head_dim)
                    scores = dot(rot_q[:, columns], keys[:span, :], NT)
                    scores = jnp.where(allowed, scores, -1e30)
                    top = jnp.max(scores, axis=1, keepdims=True)
                    weights = jnp.exp(scores - top)
                    total = jnp.sum(weights, axis=1, keepdims=True)
                    probs = (weights * (1.0 / total)).astype(BF16)
                    head_out[:, columns] = dot(probs, values[:span, :]).astype(BF16)
                    log_total[...] = jnp.where(lane == head, top + jnp.log(total), log_total[...])
                return 0

            lax.fori_loop(0, heads // 2, two_heads, 0)

    arriving[2].wait()
    arriving[3].wait()
    part[...] = dot(head_out[...], out_w[...]).astype(BF16)


def attend_kernel(
    numbers, scale, gather, block, places, normed, keys, values, table, query_own, query_sib, out_own, out_sib, *refs
):
    *refs, query_w, out_w, done = refs
    columns = out_own.shape[0]
    weights = start_all(
        (query_own, query_sib, out_own, out_sib),
        (query_w.at[0], query_w.at[1], out_w.at[pl.ds(0, columns)], out_w.at[pl.ds(columns, columns)]),
        done,
    )
    if gather:
        cotangent, gate_up, part, rot_q, head_out, log_total, far_normed, far_keys, far_values, cot0, cot1, near_gate_up = refs
        quarter = normed.shape[0]
        rows = [cotangent.at[pl.ds(pl.multiple_of(places[i] * quarter, 16), quarter)] for i in range(4)]
        halves = [cot.at[pl.ds(i * quarter, quarter)] for cot in (cot0, cot1) for i in range(2)]
        sources, targets = (keys, values, *rows, gate_up), (far_keys, far_values, *halves, near_gate_up)
    else:
        down, part, rot_q, head_out, log_total, far_normed, near_down = refs
        sources, targets = (down,), (near_down,)
    kept = start_all((normed, *sources), (far_normed, *targets), done, 4)
    attend(numbers, scale, block, normed, keys, values, table, query_w, out_w, part, rot_q, head_out, log_total, weights)
    for copy in kept:
        copy.wait()


def attend_back_kernel(scale, order, core, rot_q, log_total, d_heads, keys, values, table, *refs):
    if order == 0:
        d_queries, wide_keys, wide_values = refs
        wide_keys[...] = jnp.zeros_like(wide_keys)
        wide_values[...] = jnp.zeros_like(wide_values)
    else:
        before_keys, before_values, d_queries, kv_own, kv_sib, d_keys, d_values, wide_keys, wide_values = refs
        wide_keys[...] = before_keys[...]
        wide_values[...] = before_values[...]
    quarter = rot_q.shape[0]
    head_dim = keys.shape[1]
    block = core[0] if order == 0 else 3 - core[0]
    for number in (0, 1) if order == 0 else (2, 3):

        @pl.when(block == number)
        def _():
            span = (number + 1) * quarter
            own_table = table[number * quarter : span, :]
            allowed = causal(quarter, span, number * quarter)
            for head in range(rot_q.shape[1] // head_dim):
                columns = slice(head * head_dim, (head + 1) * head_dim)
                query = rot_q[:, columns]
                d_out = d_heads[:, columns]
                scores = dot(query, keys[:span, :], NT) - log_total[:, head : head + 1]
                probs = jnp.exp(jnp.where(allowed, scores, -1e30))
                d_probs = dot(d_out, values[:span, :], NT)
                delta = jnp.sum(probs * d_probs, axis=1, keepdims=True)
                d_scores = (probs * (d_probs - delta)).astype(BF16)
                d_query = dot(d_scores, keys[:span, :]) * scale
                d_queries[:, columns] = rope(d_query, own_table, -1.0).astype(BF16)
                wide_keys[:, :span] += dot(query, d_scores, TN)
                wide_values[:, :span] += dot(d_out, probs.astype(BF16), TN)

    if order == 0:
        return

    def rows_of(number):
        return pl.ds(pl.multiple_of(number * quarter, 16), quarter)

    d_keys[...] = rope(wide_keys[...].T, table[...], -1.0)
    d_values[...] = wide_values[...].T
    for place in range(2):
        rows = slice(place * quarter, (place + 1) * quarter)
        own = rows_of(core[0] if place == 0 else 3 - core[0])
        sib = rows_of(1 - core[0] if place == 0 else 2 + core[0])
        kv_own[rows, :head_dim] = d_keys[own, :]
        kv_own[rows, head_dim:] = d_values[own, :]
        kv_sib[rows, :head_dim] = d_keys[sib, :].astype(BF16)
        kv_sib[rows, head_dim:] = d_values[sib, :].astype(BF16)


def d_hidden_kernel(cotangent, weight, d_hidden):
    d_hidden[...] = dot(cotangent[...], weight[...], NT).astype(BF16)


def norm_kernel(block, x, part, from_x, gain, upper, lower, residual, x_rows, done):
    quarter = part.shape[0]
    here = x.at[pl.ds(pl.multiple_of(block[0] * quarter, 16), quarter)]
    (copy,) = start_all((here,), (x_rows,), done)
    total = part[...].astype(F32) + from_x[...].astype(F32)
    copy.wait()
    value = x_rows[...].astype(F32) + total
    residual[...] = value
    normed = (value * rms_factor(value) * gain[...]).astype(BF16)
    cut = upper.shape[0]
    upper[...] = normed[:cut, :]
    lower[...] = normed[cut:, :]


def ffn_kernel(own0, own1, sib0, sib1, weight, d_hidden, hidden, d_gate, d_up, normed):
    first = 0
    for rows in (own0, own1, sib0, sib1):
        normed[first : first + rows.shape[0], :] = rows[...]
        first += rows.shape[0]
    gate = dot(normed[...], weight[0])
    up = dot(normed[...], weight[1])
    square = gate * gate
    inner = jnp.tanh(GELU_COEF * gate * (1.0 + 0.044715 * square))
    bell = 0.5 * (1.0 + inner)
    gelu = gate * bell
    slope = bell + 0.5 * gate * (1.0 - inner * inner) * (GELU_COEF * (1.0 + 3.0 * 0.044715 * square))
    change = d_hidden[...].astype(F32)
    hidden[...] = (gelu * up).astype(BF16)
    d_gate[...] = (change * up * slope).astype(BF16)
    d_up[...] = (change * gelu).astype(BF16)


def down_grad_kernel(place, left0, left1, right0, right1, out):
    rows, tile = out.shape[1], out.shape[2] // 2
    for i in range(2):
        here = slice(i * tile, (i + 1) * tile)
        total = dot(left0[...], right0[:, here], TN) + dot(left1[...], right1[:, here], TN)
        for number in range(8):
            out[turned(place, number), :, here] = total[number * rows : (number + 1) * rows, :].astype(BF16)


def turned(places, number, side=0):
    return (places[side] - number) & 7


def wide_grad_kernel(tiles, place, left0, left1, gate0, gate1, up0, up1, out):
    rows, columns, chunks = out.shape[1], gate0.shape[1], 8 // tiles
    for side, (right0, right1) in enumerate(((gate0, gate1), (up0, up1))):
        for i in range(tiles):
            here = slice(i * chunks * rows, (i + 1) * chunks * rows)
            total = dot(left0[:, here], right0[...], TN) + dot(left1[:, here], right1[...], TN)
            for chunk in range(chunks):
                part = total[chunk * rows : (chunk + 1) * rows, :].astype(BF16)
                out[turned(place, i * chunks + chunk), :, side * columns : (side + 1) * columns] = part


def rows_kernel(side, tiles, dims, count, *refs):
    refs, joined = refs[:-count], refs[-count:]
    chunks = joined[0].shape[0] * 2 // refs[0].shape[0]
    lefts, weight = refs[: chunks * count], refs[chunks * count]
    *extra, out = refs[chunks * count + 1 :]
    quarter = out.shape[0] // chunks
    own = slice(side * quarter, (side + 1) * quarter)
    for i, target in enumerate(joined):
        for chunk in range(chunks):
            target[chunk * quarter : (chunk + 1) * quarter, :] = lefts[chunks * i + chunk][own, :]
    tile = out.shape[1] // tiles
    for t in range(tiles):
        here = slice(t * tile, (t + 1) * tile)
        total = None
        for i, left in enumerate(joined):
            right = weight[:, here] if dims == NN else weight[i, here, :]
            term = dot(left[...], right, dims)
            total = term if total is None else total + term
        if extra:
            total = total + extra[0][:, here].astype(F32)
        out[:, here] = total.astype(BF16)


def d_normed1_kernel(d_queries, own, sibling, out):
    half = own.shape[1]
    out[...] = (dot(d_queries[:, :half], own[...], NT) + dot(d_queries[:, half:], sibling[...], NT)).astype(BF16)


def norm_back(field, gain, d_normed):
    factor = rms_factor(field)
    scaled = gain * d_normed
    d_gain = jnp.sum(d_normed * field * factor, axis=0, keepdims=True)
    return factor * scaled - field * (factor * factor * factor) * jnp.mean(scaled * field, axis=1, keepdims=True), d_gain


def norm2_back_kernel(
    residual, on_chip, from_x, cotangent, gain, out_own, out_sib, d_residual, d_res_low, d_heads, d_gain
):
    d_normed = on_chip[...].astype(F32) + from_x[...].astype(F32)
    change, d_gain[...] = norm_back(residual[...], gain[...], d_normed)
    total = cotangent[...].astype(F32) + change
    d_residual[...] = total
    low = total.astype(BF16)
    d_res_low[...] = low
    half = out_own.shape[0]
    d_heads[:, :half] = dot(low, out_own[...], NT).astype(BF16)
    d_heads[:, half:] = dot(low, out_sib[...], NT).astype(BF16)


def norm1_back_kernel(block, x, on_chip, from_x, d_kv, d_residual, kv_weight, gain, d_input, d_gain):
    d_normed = (on_chip[...].astype(F32) + from_x[...].astype(F32)) + dot(d_kv[...], kv_weight[...], NT)
    change, d_gain[...] = norm_back(x[...].astype(F32), gain[...], d_normed)
    d_input[...] = (d_residual[...] + change).astype(BF16)


def late_grad_kernel(
    columns, place, normed0, normed1, d_queries0, d_queries1, head_out0, head_out1, d_res_low0, d_res_low1, mine, other
):
    rows = mine.shape[1]
    for side, out in enumerate((mine, other)):
        part = slice(side * columns, (side + 1) * columns)
        query = dot(normed0[...], d_queries0[:, part], TN) + dot(normed1[...], d_queries1[:, part], TN)
        outer = dot(head_out0[:, part], d_res_low0[...], TN) + dot(head_out1[:, part], d_res_low1[...], TN)
        folds = outer.shape[1] // columns
        short = rows // folds
        for number in range(8):
            spot = turned(place, number, side)
            out[spot, :, :columns] = query[number * rows : (number + 1) * rows, :].astype(out.dtype)
            for fold in range(folds):
                out[spot, fold * short : (fold + 1) * short, columns:] = outer[
                    number * short : (number + 1) * short, fold * columns : (fold + 1) * columns
                ].astype(out.dtype)


def weave_kernel(places, *refs):
    *refs, first, second, done = refs
    quarter = refs[0].shape[0]
    copies = []
    for i, source in enumerate(refs):
        target = (first, second)[i // 4]
        rows = pl.ds(pl.multiple_of(places[i % 4] * quarter, 16), quarter)
        copies += start_all((source,), (target.at[rows],), done, i)
    for copy in copies:
        copy.wait()


def assemble_kernel(first, old, count, place, *refs):
    pieces, refs = refs[:count], refs[count + old :]
    *targets, stage, done = refs
    rows, width = pieces[0].shape
    flying = [None, None]
    for i, piece in enumerate(pieces):
        slot = i % 2
        k = (place[0] - first - i) & 7
        for copy in flying[slot] or ():
            copy.wait()
        stage[slot] = piece[...].astype(F32)
        if len(targets) == 1 and targets[0].shape[0] == 2:
            half = width // 2
            moves = [(stage.at[slot, :, n * half : (n + 1) * half], targets[0].at[n, k]) for n in range(2)]
        elif len(targets) == 1:
            moves = [(stage.at[slot], targets[0].at[k])]
        else:
            half = width // 2
            folds = targets[1].shape[2] // half
            short = rows // folds
            moves = [(stage.at[slot, :, :half], targets[0].at[k])]
            moves += [
                (stage.at[slot, n * short : (n + 1) * short, half:], targets[1].at[k, :, n * half : (n + 1) * half])
                for n in range(folds)
            ]
        flying[slot] = [pltpu.make_async_copy(s, t, done.at[slot, n]) for n, (s, t) in enumerate(moves)]
        for copy in flying[slot]:
            copy.start()
    for copies in flying:
        for copy in copies or ():
            copy.wait()


def ring_orders():
    return [RING if tensor % 2 == 0 else RING[::-1] for tensor in range(4)]


def ring_pairs():
    return [
        (order[i] * 4 + tensor, order[(i + 1) % 8] * 4 + tensor) for tensor, order in enumerate(ring_orders()) for i in range(8)
    ]


class Ring:
    def __init__(self, chain, place):
        self.chain, self.place, self.left = chain, place, 0

    def begin(self, field):
        self.field, self.travelling, self.pieces, self.left = field, field[1], [], 14
        self.send()

    def send(self):
        self.arrived = lax.ppermute(self.travelling, ("dp", "tensor"), ring_pairs())

    def step(self):
        if self.left == 0:
            raise ValueError("ring idle")
        self.left -= 1
        number = 14 - self.left
        (self.travelling,) = self.chain.after(self.arrived)
        if number <= 7:
            mine = self.field[(number + 1) % 8].astype(F32)
            (self.travelling,) = self.chain.after((self.travelling.astype(F32) + mine).astype(BF16))
        if number >= 7:
            self.pieces.append(self.travelling)
        if self.left:
            self.send()

    def assemble(self, targets, first, last):
        pieces = self.pieces[first:last]
        old = [t for t in targets if isinstance(t, jax.Array)]
        return self.chain.call(
            functools.partial(assemble_kernel, first, len(old), len(pieces)),
            [shape(t.shape, F32) for t in targets],
            [*pieces, *old],
            [whole(p) for p in pieces] + [ANY] * len(old),
            [ANY] * len(targets),
            scalars=[self.place],
            scratch=[pltpu.VMEM((2,) + pieces[0].shape, F32), pltpu.SemaphoreType.DMA((2, 8))],
            aliases={1 + len(pieces) + i: i for i in range(len(old))},
            vmem=16,
        )


class Whole:
    def __init__(self, chain, place):
        self.chain, self.place = chain, place

    def begin(self, field):
        total = lax.psum(field, "dp")
        self.pieces = [total[i] for i in range(8)]

    def step(self):
        pass

    assemble = Ring.assemble


def over_dp(field, step, n_dp):
    return field.astype(F32) + lax.ppermute(field, "dp", [(i, i ^ step) for i in range(n_dp)]).astype(F32)


class Block:
    def __init__(self, n_dp, args):
        (
            self.x, self.gain1, self.query_w, self.kv_w, self.out_w, self.gain2, self.gate_up_w, self.down_w, self.cot_in,
        ) = args
        self.gain1, self.gain2 = self.gain1[None], self.gain2[None]
        self.n_dp = n_dp
        self.length, self.width = self.x.shape
        self.quarter, self.half = self.length // 4, self.length // 2
        self.head_dim = self.kv_w.shape[1] // 2
        self.cols = self.query_w.shape[1]
        self.units = self.down_w.shape[0]
        self.middle = self.width // 2
        self.scale = 1.0 / math.sqrt(self.head_dim)
        tensor = lax.axis_index("tensor")
        self.core, self.chip = tensor & 1, tensor >> 1
        core = self.core
        self.own = jnp.stack([core, 3 - core])
        self.places = jnp.stack([core, 1 - core, 3 - core, 2 + core])
        self.weave_places = jnp.stack([core, 3 - core, 1 - core, 2 + core])
        self.chain = Chain()
        if n_dp == 8:
            dp = lax.axis_index("dp")
            z, y = dp >> 1, dp & 1
            forward = z + y * (7 - 2 * z)
            place = forward + core * (7 - 2 * forward)
            self.ring_place = jnp.stack([place, 7 - place])
        else:
            self.ring_place = jnp.zeros(2, jnp.int32)
        ring = Ring if n_dp == 8 else Whole
        self.ring_a, self.ring_b, self.ring_e = (ring(self.chain, self.ring_place) for _ in range(3))
        half_dim = self.head_dim // 2
        angle = np.arange(self.length)[:, None] * 10000.0 ** (-2.0 * np.arange(half_dim)[None, :] / self.head_dim)
        self.table = jnp.asarray(np.concatenate([np.cos(angle), np.sin(angle)], 1), F32)
        self.query_sib = swap_core(self.query_w)
        self.out_sib = swap_core(self.out_w)
    def rows(self, table=None):
        if table is None:
            return pl.BlockSpec((self.quarter, self.width), lambda i, *_: (i, 0))
        return pl.BlockSpec((self.quarter, self.width), lambda i, places: (places[i], 0))

    def project(self):
        q, d, w, n = self.quarter, self.head_dim, self.width, self.length
        outs = [shape((n, d), BF16)] * 2 + [shape((q, w), BF16)] * 2 + [shape((q, d), F32)] * 2
        self.keys, self.values, own0, own1, table0, table1 = self.chain.direct(
            project_kernel,
            outs,
            [self.gain1, self.x, self.kv_w, self.table],
            scalars=[self.core[None]],
            far_ins=(1, 2, 3),
            scratch=[
                pltpu.VMEM(self.x.shape, BF16), pltpu.VMEM(self.kv_w.shape, BF16), pltpu.VMEM(self.table.shape, F32),
                pltpu.SemaphoreType.DMA((6,)),
            ],
        )
        self.normed1, self.own_tables, self.far_normed1 = (own0, own1), (table0, table1), []

    def attend(self, j):
        q, w, c = self.quarter, self.width, 2 * self.cols
        ins = [
            self.normed1[j], self.keys, self.values, self.own_tables[j],
            self.query_w, self.query_sib, self.out_w, self.out_sib,
        ]
        blocks = [shape((q, w), BF16), shape((q, c), BF16), shape((q, c), BF16), shape((q, 8), F32)]
        outs = [shape((q, w), BF16)]
        if j == 1:
            more, narrow, rows = [self.cot_in, self.gate_up_w], shape(self.keys.shape, BF16), shape((self.half, w), BF16)
            outs += [narrow, narrow, rows, rows, shape(self.gate_up_w.shape, BF16)]
        else:
            more = [self.down_w]
            outs += [shape(self.down_w.shape, BF16)]
        part, rot_q, head_out, log_total, far_normed, *rest = self.chain.call(
            functools.partial(attend_kernel, (0, 1) if j == 0 else (2, 3), self.scale, j == 1),
            blocks + outs,
            ins + more,
            [whole(a) for a in ins[:4]] + [ANY] * (4 + len(more)),
            [whole(b) for b in blocks] + [ANY] * len(outs),
            scalars=[self.own[j : j + 1], self.places],
            scratch=[
                pltpu.VMEM((2,) + self.query_w.shape, BF16),
                pltpu.VMEM((c, w), BF16),
                pltpu.SemaphoreType.DMA((12,)),
            ],
            far=range(1, 7) if j == 1 else range(1, 5),
            near=range(7, 10) if j == 1 else (5,),
            far_ins=range(4, 10),
            vmem=20,
        )
        self.far_normed1.append(far_normed)
        return part, rot_q, head_out, log_total, rest

    def attend0(self):
        self.part0, self.rot_q0, self.head_out0, self.log0, (self.near_down,) = self.attend(0)
        self.from_x0 = swap_x(self.part0)

    def attend1(self):
        self.part1, self.rot_q1, self.head_out1, self.log1, rest = self.attend(1)
        self.far_keys, self.far_values, cot0, cot1, self.near_gate_up = rest
        self.cot = (cot0, cot1)
        self.from_x1 = swap_x(self.part1)

    def dhidden(self, j):
        return self.chain.direct(
            d_hidden_kernel, [shape((self.half, self.units), BF16)], [self.cot[j], self.near_down]
        )[0]

    def dhidden0(self):
        self.d_hidden0 = self.dhidden(0)

    def dhidden1(self):
        self.d_hidden1 = self.dhidden(1)

    def norm(self, j, part, from_x):
        upper = (self.quarter // 32 + 1) * 16
        outs = [shape((rows, self.width), BF16) for rows in (upper, self.quarter - upper)]
        outs.append(shape((self.quarter, self.width), F32))
        upper, lower, residual = self.chain.direct(
            norm_kernel,
            outs,
            [self.x, part, from_x, self.gain2],
            scalars=[self.own[j : j + 1]],
            far_ins=(0,),
            scratch=[pltpu.VMEM((self.quarter, self.width), BF16), pltpu.SemaphoreType.DMA((1,))],
        )
        return [upper, lower, swap_core(upper), swap_core(lower)], residual

    def norm0(self):
        self.normed2_0, self.residual0 = self.norm(0, self.part0, self.from_x0)

    def norm1(self):
        self.normed2_1, self.residual1 = self.norm(1, self.part1, self.from_x1)

    def ffn(self, normed, d_hidden):
        return self.chain.direct(
            ffn_kernel,
            [shape((self.half, self.units), BF16)] * 3 + [shape((self.half, self.width), BF16)],
            [*normed, self.near_gate_up, d_hidden],
        )

    def ffn0(self):
        self.wide0 = self.ffn(self.normed2_0, self.d_hidden0)

    def ffn1(self):
        self.wide1 = self.ffn(self.normed2_1, self.d_hidden1)
        self.hidden, self.d_gate, self.d_up, self.normed2 = zip(self.wide0, self.wide1)

    def down(self):
        (grad,) = self.chain.direct(
            down_grad_kernel,
            [shape((8, self.units // 8, self.width), BF16)],
            [*self.hidden, *self.cot],
            scalars=[self.ring_place],
        )
        self.ring_a.begin(grad)

    def wide(self):
        (grad,) = self.chain.direct(
            functools.partial(wide_grad_kernel, 2),
            [shape((8, self.width // 8, 2 * self.units), BF16)],
            [*self.normed2, *self.d_gate, *self.d_up],
            scalars=[self.ring_place],
        )
        self.ring_b.begin(grad)

    def putdown(self):
        (self.down_sum,) = self.ring_a.assemble([shape((8, self.units // 8, self.width), F32)], 0, 8)

    def putwide0(self):
        (self.gate_up_sum,) = self.ring_b.assemble([shape((2, 8, self.width // 8, self.units), F32)], 0, 6)

    def putwide1(self):
        (self.gate_up_sum,) = self.ring_b.assemble([self.gate_up_sum], 6, 8)

    def putlate(self):
        self.query_sum, self.out_sum = self.ring_e.assemble(
            [shape((8, self.width // 8, self.cols), F32), shape((8, self.cols // 8, self.width), F32)], 0, 8
        )

    def rows_back(self, side, chunks, lefts, weight, dims, extra):
        rows, count = chunks * self.quarter, len(lefts) // chunks
        return self.chain.direct(
            functools.partial(rows_kernel, side, 3, dims, count),
            [shape((rows, self.width), BF16)],
            [*lefts, weight, *extra],
            scratch=[pltpu.VMEM((rows, self.units), BF16)] * count,
        )[0]

    def dn(self, side, wide, extra=()):
        return self.rows_back(side, 1, wide[1:3], self.near_gate_up, NT, extra)

    def dnsib0(self):
        self.dn_from0 = swap_core(self.dn(1, self.wide0))

    def dnown0(self):
        self.dn_chip0 = self.dn(0, self.wide0, (self.dn_from0,))
        self.dn_x0 = swap_x(self.dn_chip0)

    def dnsib1(self):
        self.dn_from1 = swap_core(self.dn(1, self.wide1))

    def dnown1(self):
        self.dn_chip1 = self.dn(0, self.wide1, (self.dn_from1,))
        self.dn_x1 = swap_x(self.dn_chip1)

    def fo(self, side, wide, extra=()):
        return self.rows_back(side, 1, wide[:1], self.near_down, NN, extra)

    def fosib0(self):
        self.fo_from0 = swap_core(self.fo(1, self.wide0))

    def fosib1(self):
        self.fo_from1 = swap_core(self.fo(1, self.wide1))

    def foown0(self):
        self.fo_chip0 = self.fo(0, self.wide0, (self.fo_from0,))
        self.fo_x0 = swap_x(self.fo_chip0)

    def foown1(self):
        self.fo_chip1 = self.fo(0, self.wide1, (self.fo_from1,))
        self.fo_x1 = swap_x(self.fo_chip1)

    def nback(self, residual, on_chip, from_x, cot):
        q, w, c = self.quarter, self.width, 2 * self.cols
        outs = [shape((q, w), F32), shape((q, w), BF16), shape((q, c), BF16), shape((1, w), F32)]
        ins = [residual, on_chip, from_x, cot, self.gain2, self.out_w, self.out_sib]
        specs = [whole(a) for a in ins]
        specs[3] = pl.BlockSpec((q, w), lambda i: (0, 0))
        return self.chain.call(norm2_back_kernel, outs, ins, specs, [whole(o) for o in outs], far=(0, 1))

    def nback0(self):
        self.d_residual0, self.d_res_low0, self.d_heads0, self.norm2_part0 = self.nback(
            self.residual0, self.dn_chip0, self.dn_x0, self.cot[0]
        )

    def nback1(self):
        self.d_residual1, self.d_res_low1, self.d_heads1, self.norm2_part1 = self.nback(
            self.residual1, self.dn_chip1, self.dn_x1, self.cot[1]
        )

    def aback0(self):
        ins = [self.rot_q0, self.log0, self.d_heads0, self.far_keys, self.far_values, self.table]
        wide = shape((self.head_dim, self.length), F32)
        outs = [shape((self.quarter, 2 * self.cols), BF16), wide, wide]
        self.d_queries0, self.wide_keys, self.wide_values = self.chain.call(
            functools.partial(attend_back_kernel, self.scale, 0),
            outs,
            ins,
            [whole(a) for a in ins],
            [whole(a) for a in outs],
            scalars=[self.core[None]],
            far=(0,),
        )

    def aback1(self):
        ins = [self.rot_q1, self.log1, self.d_heads1, self.far_keys, self.far_values, self.table]
        ins += [self.wide_keys, self.wide_values]
        outs = [
            shape((self.quarter, 2 * self.cols), BF16),
            shape((self.half, 2 * self.head_dim), F32),
            shape((self.half, 2 * self.head_dim), BF16),
        ]
        self.d_queries1, self.kv_own, kv_sib = self.chain.call(
            functools.partial(attend_back_kernel, self.scale, 1),
            outs,
            ins,
            [whole(a) for a in ins],
            [whole(a) for a in outs],
            scalars=[self.core[None]],
            scratch=[pltpu.VMEM((self.length, self.head_dim), F32)] * 2
            + [pltpu.VMEM((self.head_dim, self.length), F32)] * 2,
        )
        self.d_queries = (self.d_queries0, self.d_queries1)
        self.kv_from = swap_core(kv_sib)

    def late(self):
        self.late_mine, other = self.chain.direct(
            functools.partial(late_grad_kernel, self.cols),
            [shape((8, self.width // 8, 2 * self.cols), t) for t in (F32, BF16)],
            [
                *self.far_normed1, *self.d_queries, self.head_out0, self.head_out1, self.d_res_low0, self.d_res_low1,
            ],
            scalars=[self.ring_place],
        )
        self.late_from = swap_core(other)

    def dn1(self, d_queries):
        tile = pl.BlockSpec((self.width // 3, self.cols), lambda i: (i, 0))
        return self.chain.call(
            d_normed1_kernel,
            [shape((self.quarter, self.width), BF16)],
            [d_queries, self.query_w, self.query_sib],
            [whole(d_queries), tile, tile],
            [pl.BlockSpec((self.quarter, self.width // 3), lambda i: (0, i))],
            grid=(3,),
        )[0]

    def dn10(self):
        self.dn1_chip0 = self.dn1(self.d_queries0)
        self.dn1_x0 = swap_x(self.dn1_chip0)

    def dn11(self):
        self.dn1_chip1 = self.dn1(self.d_queries1)
        self.dn1_x1 = swap_x(self.dn1_chip1)

    def kv(self):
        own, sent = self.chain.after(self.kv_own, self.kv_from)
        self.kv_chip = (own + sent.astype(F32)).astype(BF16)
        self.kv_x = swap_x(self.kv_chip)

    def kvpart(self):
        chip, from_x = self.chain.after(self.kv_chip, self.kv_x)
        self.d_kv = (chip.astype(F32) + from_x.astype(F32)).astype(BF16)
        mine = lax.dynamic_slice_in_dim(self.d_kv, self.chip * self.head_dim, self.head_dim, 1)
        normed1 = jnp.concatenate(self.far_normed1, 0)
        part = dot(normed1, mine, TN)
        mine = lax.dynamic_slice_in_dim(part, self.core * self.middle, self.middle, 0)
        other = lax.dynamic_slice_in_dim(part, (1 - self.core) * self.middle, self.middle, 0).astype(BF16)
        self.kv_grad = (mine + swap_core(other).astype(F32)).astype(BF16)

    def out(self, residual, chip, from_x):
        chip, from_x = self.chain.after(chip, from_x)
        own = (residual + (chip.astype(F32) + from_x.astype(F32))).astype(BF16)
        return own, swap_core(own)

    def out0(self):
        self.output_own0, self.output_sib0 = self.out(self.residual0, self.fo_chip0, self.fo_x0)

    def out1(self):
        self.output_own1, self.output_sib1 = self.out(self.residual1, self.fo_chip1, self.fo_x1)

    def input(self, j, on_chip, from_x, d_residual):
        q, w, d = self.quarter, self.width, 2 * self.head_dim
        block = pl.BlockSpec((q, w), lambda i, _: (0, 0))
        own, part = self.chain.call(
            norm1_back_kernel,
            [shape((q, w), BF16), shape((1, w), F32)],
            [self.x, on_chip, from_x, self.d_kv, d_residual, self.kv_w, self.gain1],
            [
                self.rows(1), block, block, pl.BlockSpec((q, d), lambda i, _: (j, 0)), block, whole(self.kv_w),
                whole(self.gain1),
            ],
            [block, pl.BlockSpec((1, w), lambda i, _: (0, 0))],
            scalars=[self.own[j : j + 1]],
            far_ins=(0, 5),
        )
        return own, swap_core(own), part

    def input0(self):
        self.input_own0, self.input_sib0, self.norm1_part0 = self.input(0, self.dn1_chip0, self.dn1_x0, self.d_residual0)

    def input1(self):
        self.input_own1, self.input_sib1, self.norm1_part1 = self.input(1, self.dn1_chip1, self.dn1_x1, self.d_residual1)

    def weave(self):
        ins = [self.output_own0, self.output_own1, self.output_sib0, self.output_sib1]
        ins += [self.input_own0, self.input_own1, self.input_sib0, self.input_sib1]
        self.block_output, self.input_grad = self.chain.direct(
            weave_kernel,
            [shape((self.length, self.width), BF16)] * 2,
            ins,
            scalars=[self.weave_places],
            far=(0, 1),
            scratch=[pltpu.SemaphoreType.DMA((8,))],
        )

    def sums(self):
        d = self.head_dim
        gains = jnp.concatenate([self.norm1_part0 + self.norm1_part1, self.norm2_part0 + self.norm2_part1], 0).reshape(-1, d).astype(BF16)
        self.small = jnp.concatenate([self.kv_grad, gains], 0)
        if self.n_dp & (self.n_dp - 1):
            self.small = lax.psum(self.small, "dp")

    def small_step(self, step):
        if self.n_dp & (self.n_dp - 1):
            return
        while step < self.n_dp:
            (small,) = self.chain.after(self.small)
            self.small = over_dp(small, step, self.n_dp).astype(BF16)
            if step < 4:
                return
            step *= 2

    def sums1(self):
        self.small_step(1)

    def sums2(self):
        self.small_step(2)

    def sums4(self):
        self.small_step(4)

    def sumscore(self):
        (small,) = self.chain.after(self.small)
        self.from_core = swap_core(small)
        self.small = small

    def sumschip(self):
        d, rows = self.head_dim, self.middle
        mine, other = self.chain.after(self.small, self.from_core)
        total = mine[rows:].astype(F32) + other[rows:].astype(F32)
        self.norm_sums = total.reshape(2, self.width)
        halves = jnp.stack([mine[:rows], other[:rows]])
        self.kv_column = jnp.where(self.core == 0, halves, halves[::-1]).reshape(self.width, d)
        self.kv_other = swap_x(self.kv_column)

    def sumsend(self):
        mine, other = self.chain.after(self.kv_column, self.kv_other)
        columns = jnp.stack([mine, other])
        columns = jnp.where(self.chip == 0, columns, columns[::-1])
        self.kv_out = jnp.concatenate([columns[0], columns[1]], 1).astype(F32)

    def E(self):
        (grad,) = self.chain.after((self.late_mine + self.late_from.astype(F32)).astype(BF16))
        self.ring_e.begin(grad)

    def e(self):
        self.ring_e.step()

    def a(self):
        self.ring_a.step()

    def b(self):
        self.ring_b.step()

    def results(self):
        return (
            self.block_output,
            self.input_grad,
            self.norm_sums[0],
            self.query_sum.reshape(self.width, self.cols),
            self.kv_out,
            self.out_sum.reshape(self.cols, self.width),
            self.norm_sums[1],
            self.gate_up_sum.reshape(2, self.width, self.units),
            self.down_sum.reshape(self.units, self.width),
        )


def solution(mesh):
    n_dp = mesh.shape["dp"]

    def local(*args):
        block = Block(n_dp, args)
        for name in ORDER:
            getattr(block, name)()
        return block.results()

    return jax.shard_map(
        local,
        mesh=mesh,
        in_specs=(
            P("dp", None),
            P(),
            P(None, "tensor"),
            P(),
            P("tensor", None),
            P(),
            P(None, None, "tensor"),
            P("tensor", None),
            P("dp", None),
        ),
        out_specs=(
            P("dp", None),
            P("dp", None),
            P(),
            P(None, "tensor"),
            P(),
            P("tensor", None),
            P(),
            P(None, None, "tensor"),
            P("tensor", None),
        ),
        check_vma=False,
    )
```

```python
import functools
import math

import jax
import jax.numpy as jnp
import numpy as np
from jax import lax
from jax.experimental import pallas as pl
from jax.experimental.pallas import tpu as pltpu
from jax.sharding import PartitionSpec as P

WINDOW = 1024
EPSILON = 1e-06
GELU_COEF = 0.7978845608028654
BF16 = jnp.bfloat16
F32 = jnp.float32
NN = (((1,), (0,)), ((), ()))
NT = (((1,), (1,)), ((), ()))
TN = (((0,), (0,)), ((), ()))

RING = (0, 2, 4, 6, 7, 5, 3, 1)

ANY = pl.BlockSpec(memory_space=pl.ANY)
SMEM = pl.BlockSpec(memory_space=pltpu.SMEM)
VMEM = pl.BlockSpec(memory_space=pltpu.VMEM)
MIB = 2**20
COST = pl.CostEstimate(flops=0, bytes_accessed=0, transcendentals=0)

ORDER = " ".join(
    (
        "project attend0 attend1 dhidden0",
        "norm0 dhidden1 ffn0 dnsib0",
        "norm1 ffn1 wide dnown0",
        "down b a dnsib1",
        "a dnown1 b a",
        "nback0 a aback0 nback1",
        "b a aback1 a",
        "late b kv a",
        "fosib1 fosib0 b kvpart",
        "a dn11 E b",
        "e dn10 e b",
        "a e input1 foown0",
        "e a putdown0 b",
        "e input0 sums sums1",
        "e a b sums2",
        "e foown1 e sums4",
        "b out0 putwide0 e",
        "a sumscore e out1",
        "b sumschip e weave",
        "a b a e",
        "sumsend putdown1 e b",
        "putwide1 putlate0 e putlate1",
        "b putwide2",
    )
).split()


def dot(left, right, dims=NN):
    return lax.dot_general(left, right, dims, preferred_element_type=F32)


def swap_core(field):
    return lax.ppermute(field, "tensor", [(i, i ^ 1) for i in range(4)])


def swap_x(field):
    return lax.ppermute(field, "tensor", [(i, i ^ 2) for i in range(4)])


def shape(dims, dtype):
    return jax.ShapeDtypeStruct(dims, dtype)


def whole(array):
    rank = len(array.shape)
    return pl.BlockSpec(array.shape, lambda *_: (0,) * rank)


class Chain:
    def __init__(self):
        self.token = None

    def call(self, body, outs, ins, in_specs, out_specs, grid=(1,), scalars=(), vmem=16, scratch=(), aliases=None, far=(),
        far_ins=(), near=(),
    ):
        tokens = [] if self.token is None else [self.token]
        given, made = len(scalars) + len(ins), len(outs)

        def run(*refs):
            refs = refs[:given] + refs[given + len(tokens) :]
            body(*refs[: given + made], *refs[given + made + 1 :])

        outs = [pltpu.HBM(o.shape, o.dtype) if i in far else o for i, o in enumerate(outs)]
        outs = [pltpu.VMEM(o.shape, o.dtype) if i in near else o for i, o in enumerate(outs)]
        ins = [pltpu.with_memory_space_constraint(a, pltpu.HBM) if i in far_ins else a for i, a in enumerate(ins)]
        *results, self.token = pl.pallas_call(
            run,
            out_shape=outs + [shape((8, 128), F32)],
            grid_spec=pltpu.PrefetchScalarGridSpec(
                num_scalar_prefetch=len(scalars),
                grid=grid,
                in_specs=list(in_specs) + [ANY] * len(tokens),
                out_specs=list(out_specs) + [ANY],
                scratch_shapes=list(scratch),
            ),
            input_output_aliases=aliases or {},
            compiler_params=pltpu.CompilerParams(vmem_limit_bytes=vmem * MIB),
            cost_estimate=COST,
        )(*scalars, *ins, *tokens)
        return results

    def direct(self, body, outs, ins, scalars=(), far_ins=(), far=(), vmem=16, scratch=()):
        tokens = [] if self.token is None else [self.token]
        given, made = len(scalars) + len(ins), len(outs)

        def run(*refs):
            refs = refs[:given] + refs[given + len(tokens) :]
            body(*refs[: given + made], *refs[given + made + 1 :])

        ins = [pltpu.with_memory_space_constraint(a, pltpu.HBM) if i in far_ins else a for i, a in enumerate(ins)]
        in_specs = [SMEM] * len(scalars) + [ANY if i in far_ins else VMEM for i in range(len(ins))]
        *results, self.token = pl.pallas_call(
            run,
            out_shape=[pltpu.HBM(o.shape, o.dtype) if i in far else o for i, o in enumerate(outs)]
            + [shape((8, 128), F32)],
            in_specs=in_specs + [ANY] * len(tokens),
            out_specs=[ANY if i in far else VMEM for i in range(made)] + [ANY],
            scratch_shapes=list(scratch),
            compiler_params=pltpu.CompilerParams(vmem_limit_bytes=vmem * MIB),
            cost_estimate=COST,
        )(*scalars, *ins, *tokens)
        return results

    def after(self, *values):
        *values, self.token = lax.optimization_barrier((*values, self.token))
        return values


def rope(field, table, sign=1.0):
    half = field.shape[1] // 2
    other = pltpu.roll(table, half, 1)
    first = lax.broadcasted_iota(jnp.int32, table.shape, 1) < half
    cosine = jnp.where(first, table, other)
    sine = jnp.where(first, -other, table) * sign
    return field * cosine + pltpu.roll(field, half, 1) * sine


def rms_factor(field):
    return lax.rsqrt(jnp.mean(field * field, axis=1, keepdims=True) + EPSILON)


def start_all(sources, targets, done, first=0):
    copies = [pltpu.make_async_copy(s, t, done.at[first + i]) for i, (s, t) in enumerate(zip(sources, targets))]
    for copy in copies:
        copy.start()
    return copies


def project_kernel(
    core, gain, x, weight, table, keys, values, own0, own1, table0, table1, x_rows, weight_all, table_all, done
):
    quarter = own0.shape[0]
    head_dim = keys.shape[1]

    def rows(block):
        return pl.ds(block * quarter, quarter)

    copies = start_all([x.at[rows(i)] for i in range(4)], [x_rows.at[rows(i)] for i in range(4)], done)
    copies += start_all((weight, table), (weight_all, table_all), done, 4)
    for block in range(4):
        here = rows(block)
        copies[block].wait()
        field = x_rows[here, :].astype(F32)
        normed = (field * rms_factor(field) * gain[...]).astype(BF16)
        if block == 0:
            copies[4].wait()
            copies[5].wait()
        both = dot(normed, weight_all[...])
        keys[here, :] = rope(both[:, :head_dim], table_all[here, :]).astype(BF16)
        values[here, :] = both[:, head_dim:].astype(BF16)
        number, own, angles = (core[0], own0, table0) if block < 2 else (3 - core[0], own1, table1)

        @pl.when(number == block)
        def _():
            own[...] = normed
            angles[...] = table_all[here, :]


def causal(rows, columns, first_row):
    row = lax.broadcasted_iota(jnp.int32, (rows, columns), 0) + first_row
    column = lax.broadcasted_iota(jnp.int32, (rows, columns), 1)
    allowed = column <= row
    if columns > WINDOW:
        allowed = allowed & (row - column < WINDOW)
    return allowed


def attend(numbers, scale, block, normed, keys, values, table, query_w, out_w, part, rot_q, head_out, log_total, arriving):
    quarter = normed.shape[0]
    head_dim = keys.shape[1]
    heads = out_w.shape[0] // head_dim
    for side in range(2):
        arriving[side].wait()
        queries = dot(normed[...], query_w[side])
        for head in range(heads // 2):
            columns = slice(head * head_dim, (head + 1) * head_dim)
            place = side * (heads // 2) + head
            rot_q[:, place * head_dim : (place + 1) * head_dim] = (
                rope(queries[:, columns], table[...]) * scale
            ).astype(BF16)
    for number in numbers:

        @pl.when(block[0] == number)
        def _():
            span = (number + 1) * quarter
            allowed = causal(quarter, span, number * quarter)
            lane = lax.broadcasted_iota(jnp.int32, log_total.shape, 1)

            def two_heads(pair, _):
                for head in (2 * pair, 2 * pair + 1):
                    columns = pl.ds(pl.multiple_of(head * head_dim, head_dim), head_dim)
                    scores = dot(rot_q[:, columns], keys[:span, :], NT)
                    scores = jnp.where(allowed, scores, -1e30)
                    top = jnp.max(scores, axis=1, keepdims=True)
                    weights = jnp.exp(scores - top)
                    total = jnp.sum(weights, axis=1, keepdims=True)
                    probs = (weights * (1.0 / total)).astype(BF16)
                    head_out[:, columns] = dot(probs, values[:span, :]).astype(BF16)
                    log_total[...] = jnp.where(lane == head, top + jnp.log(total), log_total[...])
                return 0

            lax.fori_loop(0, heads // 2, two_heads, 0)

    arriving[2].wait()
    arriving[3].wait()
    part[...] = dot(head_out[...], out_w[...]).astype(BF16)


def attend_kernel(
    numbers, scale, gather, block, places, normed, keys, values, table, query_own, query_sib, out_own, out_sib, *refs
):
    *refs, query_w, out_w, done = refs
    columns = out_own.shape[0]
    weights = start_all(
        (query_own, query_sib, out_own, out_sib),
        (query_w.at[0], query_w.at[1], out_w.at[pl.ds(0, columns)], out_w.at[pl.ds(columns, columns)]),
        done,
    )
    if gather:
        cotangent, gate_up, part, rot_q, head_out, log_total, far_normed, far_keys, far_values, cot0, cot1, near_gate_up = refs
        quarter = normed.shape[0]
        rows = [cotangent.at[pl.ds(pl.multiple_of(places[i] * quarter, 16), quarter)] for i in range(4)]
        halves = [cot.at[pl.ds(i * quarter, quarter)] for cot in (cot0, cot1) for i in range(2)]
        sources, targets = (keys, values, *rows, gate_up), (far_keys, far_values, *halves, near_gate_up)
    else:
        down, part, rot_q, head_out, log_total, far_normed, near_down = refs
        sources, targets = (down,), (near_down,)
    kept = start_all((normed, *sources), (far_normed, *targets), done, 4)
    attend(numbers, scale, block, normed, keys, values, table, query_w, out_w, part, rot_q, head_out, log_total, weights)
    for copy in kept:
        copy.wait()


def attend_back_kernel(scale, order, core, rot_q, log_total, d_heads, keys, values, table, *refs):
    if order == 0:
        d_queries, wide_keys, wide_values = refs
        wide_keys[...] = jnp.zeros_like(wide_keys)
        wide_values[...] = jnp.zeros_like(wide_values)
    else:
        before_keys, before_values, d_queries, kv_own, kv_sib, d_keys, d_values, wide_keys, wide_values = refs
        wide_keys[...] = before_keys[...]
        wide_values[...] = before_values[...]
    quarter = rot_q.shape[0]
    head_dim = keys.shape[1]
    block = core[0] if order == 0 else 3 - core[0]
    for number in (0, 1) if order == 0 else (2, 3):

        @pl.when(block == number)
        def _():
            span = (number + 1) * quarter
            own_table = table[number * quarter : span, :]
            allowed = causal(quarter, span, number * quarter)
            for head in range(rot_q.shape[1] // head_dim):
                columns = slice(head * head_dim, (head + 1) * head_dim)
                query = rot_q[:, columns]
                d_out = d_heads[:, columns]
                scores = dot(query, keys[:span, :], NT) - log_total[:, head : head + 1]
                probs = jnp.exp(jnp.where(allowed, scores, -1e30))
                d_probs = dot(d_out, values[:span, :], NT)
                delta = jnp.sum(probs * d_probs, axis=1, keepdims=True)
                d_scores = (probs * (d_probs - delta)).astype(BF16)
                d_query = dot(d_scores, keys[:span, :]) * scale
                d_queries[:, columns] = rope(d_query, own_table, -1.0).astype(BF16)
                wide_keys[:, :span] += dot(query, d_scores, TN)
                wide_values[:, :span] += dot(d_out, probs.astype(BF16), TN)

    if order == 0:
        return

    def rows_of(number):
        return pl.ds(pl.multiple_of(number * quarter, 16), quarter)

    d_keys[...] = rope(wide_keys[...].T, table[...], -1.0)
    d_values[...] = wide_values[...].T
    for place in range(2):
        rows = slice(place * quarter, (place + 1) * quarter)
        own = rows_of(core[0] if place == 0 else 3 - core[0])
        sib = rows_of(1 - core[0] if place == 0 else 2 + core[0])
        kv_own[rows, :head_dim] = d_keys[own, :]
        kv_own[rows, head_dim:] = d_values[own, :]
        kv_sib[rows, :head_dim] = d_keys[sib, :].astype(BF16)
        kv_sib[rows, head_dim:] = d_values[sib, :].astype(BF16)


def d_hidden_kernel(cotangent, weight, d_hidden):
    d_hidden[...] = dot(cotangent[...], weight[...], NT).astype(BF16)


def norm_kernel(block, x, part, from_x, gain, upper, lower, residual, x_rows, done):
    quarter = part.shape[0]
    here = x.at[pl.ds(pl.multiple_of(block[0] * quarter, 16), quarter)]
    (copy,) = start_all((here,), (x_rows,), done)
    total = part[...].astype(F32) + from_x[...].astype(F32)
    copy.wait()
    value = x_rows[...].astype(F32) + total
    residual[...] = value
    normed = (value * rms_factor(value) * gain[...]).astype(BF16)
    cut = upper.shape[0]
    upper[...] = normed[:cut, :]
    lower[...] = normed[cut:, :]


def ffn_kernel(own0, own1, sib0, sib1, weight, d_hidden, hidden, d_gate, d_up, normed):
    first = 0
    for rows in (own0, own1, sib0, sib1):
        normed[first : first + rows.shape[0], :] = rows[...]
        first += rows.shape[0]
    gate = dot(normed[...], weight[0])
    up = dot(normed[...], weight[1])
    square = gate * gate
    inner = jnp.tanh(GELU_COEF * gate * (1.0 + 0.044715 * square))
    bell = 0.5 * (1.0 + inner)
    gelu = gate * bell
    slope = bell + 0.5 * gate * (1.0 - inner * inner) * (GELU_COEF * (1.0 + 3.0 * 0.044715 * square))
    change = d_hidden[...].astype(F32)
    hidden[...] = (gelu * up).astype(BF16)
    d_gate[...] = (change * up * slope).astype(BF16)
    d_up[...] = (change * gelu).astype(BF16)


def down_grad_kernel(place, left0, left1, right0, right1, out):
    rows, tile = out.shape[1], out.shape[2] // 2
    for i in range(2):
        here = slice(i * tile, (i + 1) * tile)
        total = dot(left0[...], right0[:, here], TN) + dot(left1[...], right1[:, here], TN)
        for number in range(8):
            out[turned(place, number), :, here] = total[number * rows : (number + 1) * rows, :].astype(BF16)


def turned(places, number, side=0):
    return (places[side] - number) & 7


def wide_grad_kernel(tiles, place, left0, left1, gate0, gate1, up0, up1, out):
    rows, columns, chunks = out.shape[1], gate0.shape[1], 8 // tiles
    for side, (right0, right1) in enumerate(((gate0, gate1), (up0, up1))):
        for i in range(tiles):
            here = slice(i * chunks * rows, (i + 1) * chunks * rows)
            total = dot(left0[:, here], right0[...], TN) + dot(left1[:, here], right1[...], TN)
            for chunk in range(chunks):
                part = total[chunk * rows : (chunk + 1) * rows, :].astype(BF16)
                out[turned(place, i * chunks + chunk), :, side * columns : (side + 1) * columns] = part


def rows_kernel(side, tiles, dims, count, *refs):
    refs, joined = refs[:-count], refs[-count:]
    chunks = joined[0].shape[0] * 2 // refs[0].shape[0]
    lefts, weight = refs[: chunks * count], refs[chunks * count]
    *extra, out = refs[chunks * count + 1 :]
    quarter = out.shape[0] // chunks
    own = slice(side * quarter, (side + 1) * quarter)
    for i, target in enumerate(joined):
        for chunk in range(chunks):
            target[chunk * quarter : (chunk + 1) * quarter, :] = lefts[chunks * i + chunk][own, :]
    tile = out.shape[1] // tiles
    for t in range(tiles):
        here = slice(t * tile, (t + 1) * tile)
        total = None
        for i, left in enumerate(joined):
            right = weight[:, here] if dims == NN else weight[i, here, :]
            term = dot(left[...], right, dims)
            total = term if total is None else total + term
        if extra:
            total = total + extra[0][:, here].astype(F32)
        out[:, here] = total.astype(BF16)


def d_normed1_kernel(d_queries, own, sibling, out):
    half = own.shape[1]
    out[...] = (dot(d_queries[:, :half], own[...], NT) + dot(d_queries[:, half:], sibling[...], NT)).astype(BF16)


def norm_back(field, gain, d_normed):
    factor = rms_factor(field)
    scaled = gain * d_normed
    d_gain = jnp.sum(d_normed * field * factor, axis=0, keepdims=True)
    return factor * scaled - field * (factor * factor * factor) * jnp.mean(scaled * field, axis=1, keepdims=True), d_gain


def norm2_back_kernel(
    residual, on_chip, from_x, cotangent, gain, out_own, out_sib, d_residual, d_res_low, d_heads, d_gain
):
    d_normed = on_chip[...].astype(F32) + from_x[...].astype(F32)
    change, d_gain[...] = norm_back(residual[...], gain[...], d_normed)
    total = cotangent[...].astype(F32) + change
    d_residual[...] = total
    low = total.astype(BF16)
    d_res_low[...] = low
    half = out_own.shape[0]
    d_heads[:, :half] = dot(low, out_own[...], NT).astype(BF16)
    d_heads[:, half:] = dot(low, out_sib[...], NT).astype(BF16)


def norm1_back_kernel(block, x, on_chip, from_x, d_kv, d_residual, kv_weight, gain, d_input, d_gain):
    d_normed = (on_chip[...].astype(F32) + from_x[...].astype(F32)) + dot(d_kv[...], kv_weight[...], NT)
    change, d_gain[...] = norm_back(x[...].astype(F32), gain[...], d_normed)
    d_input[...] = (d_residual[...] + change).astype(BF16)


def late_grad_kernel(
    columns, place, normed0, normed1, d_queries0, d_queries1, head_out0, head_out1, d_res_low0, d_res_low1, mine, other
):
    rows = mine.shape[1]
    for side, out in enumerate((mine, other)):
        part = slice(side * columns, (side + 1) * columns)
        query = dot(normed0[...], d_queries0[:, part], TN) + dot(normed1[...], d_queries1[:, part], TN)
        outer = dot(head_out0[:, part], d_res_low0[...], TN) + dot(head_out1[:, part], d_res_low1[...], TN)
        folds = outer.shape[1] // columns
        short = rows // folds
        for number in range(8):
            spot = turned(place, number, side)
            out[spot, :, :columns] = query[number * rows : (number + 1) * rows, :].astype(out.dtype)
            for fold in range(folds):
                out[spot, fold * short : (fold + 1) * short, columns:] = outer[
                    number * short : (number + 1) * short, fold * columns : (fold + 1) * columns
                ].astype(out.dtype)


def weave_kernel(places, *refs):
    *refs, first, second, done = refs
    quarter = refs[0].shape[0]
    copies = []
    for i, source in enumerate(refs):
        target = (first, second)[i // 4]
        rows = pl.ds(pl.multiple_of(places[i % 4] * quarter, 16), quarter)
        copies += start_all((source,), (target.at[rows],), done, i)
    for copy in copies:
        copy.wait()


def assemble_kernel(first, old, count, place, *refs):
    pieces, refs = refs[:count], refs[count + old :]
    *targets, stage, done = refs
    rows, width = pieces[0].shape
    flying = [None, None]
    for i, piece in enumerate(pieces):
        slot = i % 2
        k = (place[0] - first - i) & 7
        for copy in flying[slot] or ():
            copy.wait()
        stage[slot] = piece[...].astype(F32)
        if len(targets) == 1 and targets[0].shape[0] == 2:
            half = width // 2
            moves = [(stage.at[slot, :, n * half : (n + 1) * half], targets[0].at[n, k]) for n in range(2)]
        elif len(targets) == 1:
            moves = [(stage.at[slot], targets[0].at[k])]
        else:
            half = width // 2
            folds = targets[1].shape[2] // half
            short = rows // folds
            moves = [(stage.at[slot, :, :half], targets[0].at[k])]
            moves += [
                (stage.at[slot, n * short : (n + 1) * short, half:], targets[1].at[k, :, n * half : (n + 1) * half])
                for n in range(folds)
            ]
        flying[slot] = [pltpu.make_async_copy(s, t, done.at[slot, n]) for n, (s, t) in enumerate(moves)]
        for copy in flying[slot]:
            copy.start()
    for copies in flying:
        for copy in copies or ():
            copy.wait()


def ring_orders():
    return [RING if tensor % 2 == 0 else RING[::-1] for tensor in range(4)]


def ring_pairs():
    return [
        (order[i] * 4 + tensor, order[(i + 1) % 8] * 4 + tensor) for tensor, order in enumerate(ring_orders()) for i in range(8)
    ]


class Ring:
    def __init__(self, chain, place):
        self.chain, self.place, self.left = chain, place, 0

    def begin(self, field):
        self.field, self.travelling, self.pieces, self.left = field, field[1], [], 14
        self.send()

    def send(self):
        self.arrived = lax.ppermute(self.travelling, ("dp", "tensor"), ring_pairs())

    def step(self):
        if self.left == 0:
            raise ValueError("ring idle")
        self.left -= 1
        number = 14 - self.left
        (self.travelling,) = self.chain.after(self.arrived)
        if number <= 7:
            mine = self.field[(number + 1) % 8].astype(F32)
            (self.travelling,) = self.chain.after((self.travelling.astype(F32) + mine).astype(BF16))
        if number >= 7:
            self.pieces.append(self.travelling)
        if self.left:
            self.send()

    def assemble(self, targets, first, last):
        pieces = self.pieces[first:last]
        old = [t for t in targets if isinstance(t, jax.Array)]
        return self.chain.call(
            functools.partial(assemble_kernel, first, len(old), len(pieces)),
            [shape(t.shape, F32) for t in targets],
            [*pieces, *old],
            [whole(p) for p in pieces] + [ANY] * len(old),
            [ANY] * len(targets),
            scalars=[self.place],
            scratch=[pltpu.VMEM((2,) + pieces[0].shape, F32), pltpu.SemaphoreType.DMA((2, 8))],
            aliases={1 + len(pieces) + i: i for i in range(len(old))},
            vmem=16,
        )


class Whole:
    def __init__(self, chain, place):
        self.chain, self.place = chain, place

    def begin(self, field):
        total = lax.psum(field, "dp")
        self.pieces = [total[i] for i in range(8)]

    def step(self):
        pass

    assemble = Ring.assemble


def over_dp(field, step, n_dp):
    return field.astype(F32) + lax.ppermute(field, "dp", [(i, i ^ step) for i in range(n_dp)]).astype(F32)


class Block:
    def __init__(self, n_dp, args):
        (
            self.x, self.gain1, self.query_w, self.kv_w, self.out_w, self.gain2, self.gate_up_w, self.down_w, self.cot_in,
        ) = args
        self.gain1, self.gain2 = self.gain1[None], self.gain2[None]
        self.n_dp = n_dp
        self.length, self.width = self.x.shape
        self.quarter, self.half = self.length // 4, self.length // 2
        self.head_dim = self.kv_w.shape[1] // 2
        self.cols = self.query_w.shape[1]
        self.units = self.down_w.shape[0]
        self.middle = self.width // 2
        self.scale = 1.0 / math.sqrt(self.head_dim)
        tensor = lax.axis_index("tensor")
        self.core, self.chip = tensor & 1, tensor >> 1
        core = self.core
        self.own = jnp.stack([core, 3 - core])
        self.places = jnp.stack([core, 1 - core, 3 - core, 2 + core])
        self.weave_places = jnp.stack([core, 3 - core, 1 - core, 2 + core])
        self.chain = Chain()
        if n_dp == 8:
            dp = lax.axis_index("dp")
            z, y = dp >> 1, dp & 1
            forward = z + y * (7 - 2 * z)
            place = forward + core * (7 - 2 * forward)
            self.ring_place = jnp.stack([place, 7 - place])
        else:
            self.ring_place = jnp.zeros(2, jnp.int32)
        ring = Ring if n_dp == 8 else Whole
        self.ring_a, self.ring_b, self.ring_e = (ring(self.chain, self.ring_place) for _ in range(3))
        half_dim = self.head_dim // 2
        angle = np.arange(self.length)[:, None] * 10000.0 ** (-2.0 * np.arange(half_dim)[None, :] / self.head_dim)
        self.table = jnp.asarray(np.concatenate([np.cos(angle), np.sin(angle)], 1), F32)
        self.query_sib = swap_core(self.query_w)
        self.out_sib = swap_core(self.out_w)
    def rows(self, table=None):
        if table is None:
            return pl.BlockSpec((self.quarter, self.width), lambda i, *_: (i, 0))
        return pl.BlockSpec((self.quarter, self.width), lambda i, places: (places[i], 0))

    def project(self):
        q, d, w, n = self.quarter, self.head_dim, self.width, self.length
        outs = [shape((n, d), BF16)] * 2 + [shape((q, w), BF16)] * 2 + [shape((q, d), F32)] * 2
        self.keys, self.values, own0, own1, table0, table1 = self.chain.direct(
            project_kernel,
            outs,
            [self.gain1, self.x, self.kv_w, self.table],
            scalars=[self.core[None]],
            far_ins=(1, 2, 3),
            scratch=[
                pltpu.VMEM(self.x.shape, BF16), pltpu.VMEM(self.kv_w.shape, BF16), pltpu.VMEM(self.table.shape, F32),
                pltpu.SemaphoreType.DMA((6,)),
            ],
        )
        self.normed1, self.own_tables, self.far_normed1 = (own0, own1), (table0, table1), []

    def attend(self, j):
        q, w, c = self.quarter, self.width, 2 * self.cols
        ins = [
            self.normed1[j], self.keys, self.values, self.own_tables[j],
            self.query_w, self.query_sib, self.out_w, self.out_sib,
        ]
        blocks = [shape((q, w), BF16), shape((q, c), BF16), shape((q, c), BF16), shape((q, 8), F32)]
        outs = [shape((q, w), BF16)]
        if j == 1:
            more, narrow, rows = [self.cot_in, self.gate_up_w], shape(self.keys.shape, BF16), shape((self.half, w), BF16)
            outs += [narrow, narrow, rows, rows, shape(self.gate_up_w.shape, BF16)]
        else:
            more = [self.down_w]
            outs += [shape(self.down_w.shape, BF16)]
        part, rot_q, head_out, log_total, far_normed, *rest = self.chain.call(
            functools.partial(attend_kernel, (0, 1) if j == 0 else (2, 3), self.scale, j == 1),
            blocks + outs,
            ins + more,
            [whole(a) for a in ins[:4]] + [ANY] * (4 + len(more)),
            [whole(b) for b in blocks] + [ANY] * len(outs),
            scalars=[self.own[j : j + 1], self.places],
            scratch=[
                pltpu.VMEM((2,) + self.query_w.shape, BF16),
                pltpu.VMEM((c, w), BF16),
                pltpu.SemaphoreType.DMA((12,)),
            ],
            far=range(1, 7) if j == 1 else range(1, 5),
            near=range(7, 10) if j == 1 else (5,),
            far_ins=range(4, 10),
            vmem=20,
        )
        self.far_normed1.append(far_normed)
        return part, rot_q, head_out, log_total, rest

    def attend0(self):
        self.part0, self.rot_q0, self.head_out0, self.log0, (self.near_down,) = self.attend(0)
        self.from_x0 = swap_x(self.part0)

    def attend1(self):
        self.part1, self.rot_q1, self.head_out1, self.log1, rest = self.attend(1)
        self.far_keys, self.far_values, cot0, cot1, self.near_gate_up = rest
        self.cot = (cot0, cot1)
        self.from_x1 = swap_x(self.part1)

    def dhidden(self, j):
        return self.chain.direct(
            d_hidden_kernel, [shape((self.half, self.units), BF16)], [self.cot[j], self.near_down]
        )[0]

    def dhidden0(self):
        self.d_hidden0 = self.dhidden(0)

    def dhidden1(self):
        self.d_hidden1 = self.dhidden(1)

    def norm(self, j, part, from_x):
        upper = (self.quarter // 32 + 1) * 16
        outs = [shape((rows, self.width), BF16) for rows in (upper, self.quarter - upper)]
        outs.append(shape((self.quarter, self.width), F32))
        upper, lower, residual = self.chain.direct(
            norm_kernel,
            outs,
            [self.x, part, from_x, self.gain2],
            scalars=[self.own[j : j + 1]],
            far_ins=(0,),
            scratch=[pltpu.VMEM((self.quarter, self.width), BF16), pltpu.SemaphoreType.DMA((1,))],
        )
        return [upper, lower, swap_core(upper), swap_core(lower)], residual

    def norm0(self):
        self.normed2_0, self.residual0 = self.norm(0, self.part0, self.from_x0)

    def norm1(self):
        self.normed2_1, self.residual1 = self.norm(1, self.part1, self.from_x1)

    def ffn(self, normed, d_hidden):
        return self.chain.direct(
            ffn_kernel,
            [shape((self.half, self.units), BF16)] * 3 + [shape((self.half, self.width), BF16)],
            [*normed, self.near_gate_up, d_hidden],
        )

    def ffn0(self):
        self.wide0 = self.ffn(self.normed2_0, self.d_hidden0)

    def ffn1(self):
        self.wide1 = self.ffn(self.normed2_1, self.d_hidden1)
        self.hidden, self.d_gate, self.d_up, self.normed2 = zip(self.wide0, self.wide1)

    def down(self):
        (grad,) = self.chain.direct(
            down_grad_kernel,
            [shape((8, self.units // 8, self.width), BF16)],
            [*self.hidden, *self.cot],
            scalars=[self.ring_place],
        )
        self.ring_a.begin(grad)

    def wide(self):
        (grad,) = self.chain.direct(
            functools.partial(wide_grad_kernel, 2),
            [shape((8, self.width // 8, 2 * self.units), BF16)],
            [*self.normed2, *self.d_gate, *self.d_up],
            scalars=[self.ring_place],
        )
        self.ring_b.begin(grad)

    def put_down(self, first, last):
        target = shape((8, self.units // 8, self.width), F32) if first == 0 else self.down_sum
        (self.down_sum,) = self.ring_a.assemble([target], first, last)

    def putdown0(self):
        self.put_down(0, 4)

    def putdown1(self):
        self.put_down(4, 8)

    def put_wide(self, first, last):
        target = shape((2, 8, self.width // 8, self.units), F32) if first == 0 else self.gate_up_sum
        (self.gate_up_sum,) = self.ring_b.assemble([target], first, last)

    def putwide0(self):
        self.put_wide(0, 4)

    def putwide1(self):
        self.put_wide(4, 7)

    def putwide2(self):
        self.put_wide(7, 8)

    def put_late(self, first, last):
        targets = [shape((8, self.width // 8, self.cols), F32), shape((8, self.cols // 8, self.width), F32)]
        if first:
            targets = [self.query_sum, self.out_sum]
        self.query_sum, self.out_sum = self.ring_e.assemble(targets, first, last)

    def putlate0(self):
        self.put_late(0, 6)

    def putlate1(self):
        self.put_late(6, 8)

    def rows_back(self, side, chunks, lefts, weight, dims, extra):
        rows, count = chunks * self.quarter, len(lefts) // chunks
        return self.chain.direct(
            functools.partial(rows_kernel, side, 3, dims, count),
            [shape((rows, self.width), BF16)],
            [*lefts, weight, *extra],
            scratch=[pltpu.VMEM((rows, self.units), BF16)] * count,
        )[0]

    def dn(self, side, wide, extra=()):
        return self.rows_back(side, 1, wide[1:3], self.near_gate_up, NT, extra)

    def dnsib0(self):
        self.dn_from0 = swap_core(self.dn(1, self.wide0))

    def dnown0(self):
        self.dn_chip0 = self.dn(0, self.wide0, (self.dn_from0,))
        self.dn_x0 = swap_x(self.dn_chip0)

    def dnsib1(self):
        self.dn_from1 = swap_core(self.dn(1, self.wide1))

    def dnown1(self):
        self.dn_chip1 = self.dn(0, self.wide1, (self.dn_from1,))
        self.dn_x1 = swap_x(self.dn_chip1)

    def fo(self, side, wide, extra=()):
        return self.rows_back(side, 1, wide[:1], self.near_down, NN, extra)

    def fosib0(self):
        self.fo_from0 = swap_core(self.fo(1, self.wide0))

    def fosib1(self):
        self.fo_from1 = swap_core(self.fo(1, self.wide1))

    def foown0(self):
        self.fo_chip0 = self.fo(0, self.wide0, (self.fo_from0,))
        self.fo_x0 = swap_x(self.fo_chip0)

    def foown1(self):
        self.fo_chip1 = self.fo(0, self.wide1, (self.fo_from1,))
        self.fo_x1 = swap_x(self.fo_chip1)

    def nback(self, residual, on_chip, from_x, cot):
        q, w, c = self.quarter, self.width, 2 * self.cols
        outs = [shape((q, w), F32), shape((q, w), BF16), shape((q, c), BF16), shape((1, w), F32)]
        ins = [residual, on_chip, from_x, cot, self.gain2, self.out_w, self.out_sib]
        specs = [whole(a) for a in ins]
        specs[3] = pl.BlockSpec((q, w), lambda i: (0, 0))
        return self.chain.call(norm2_back_kernel, outs, ins, specs, [whole(o) for o in outs], far=(0, 1))

    def nback0(self):
        self.d_residual0, self.d_res_low0, self.d_heads0, self.norm2_part0 = self.nback(
            self.residual0, self.dn_chip0, self.dn_x0, self.cot[0]
        )

    def nback1(self):
        self.d_residual1, self.d_res_low1, self.d_heads1, self.norm2_part1 = self.nback(
            self.residual1, self.dn_chip1, self.dn_x1, self.cot[1]
        )

    def aback0(self):
        ins = [self.rot_q0, self.log0, self.d_heads0, self.far_keys, self.far_values, self.table]
        wide = shape((self.head_dim, self.length), F32)
        outs = [shape((self.quarter, 2 * self.cols), BF16), wide, wide]
        self.d_queries0, self.wide_keys, self.wide_values = self.chain.call(
            functools.partial(attend_back_kernel, self.scale, 0),
            outs,
            ins,
            [whole(a) for a in ins],
            [whole(a) for a in outs],
            scalars=[self.core[None]],
            far=(0,),
        )

    def aback1(self):
        ins = [self.rot_q1, self.log1, self.d_heads1, self.far_keys, self.far_values, self.table]
        ins += [self.wide_keys, self.wide_values]
        outs = [
            shape((self.quarter, 2 * self.cols), BF16),
            shape((self.half, 2 * self.head_dim), F32),
            shape((self.half, 2 * self.head_dim), BF16),
        ]
        self.d_queries1, self.kv_own, kv_sib = self.chain.call(
            functools.partial(attend_back_kernel, self.scale, 1),
            outs,
            ins,
            [whole(a) for a in ins],
            [whole(a) for a in outs],
            scalars=[self.core[None]],
            scratch=[pltpu.VMEM((self.length, self.head_dim), F32)] * 2
            + [pltpu.VMEM((self.head_dim, self.length), F32)] * 2,
        )
        self.d_queries = (self.d_queries0, self.d_queries1)
        self.kv_from = swap_core(kv_sib)

    def late(self):
        self.late_mine, other = self.chain.direct(
            functools.partial(late_grad_kernel, self.cols),
            [shape((8, self.width // 8, 2 * self.cols), t) for t in (F32, BF16)],
            [
                *self.far_normed1, *self.d_queries, self.head_out0, self.head_out1, self.d_res_low0, self.d_res_low1,
            ],
            scalars=[self.ring_place],
        )
        self.late_from = swap_core(other)

    def dn1(self, d_queries):
        tile = pl.BlockSpec((self.width // 3, self.cols), lambda i: (i, 0))
        return self.chain.call(
            d_normed1_kernel,
            [shape((self.quarter, self.width), BF16)],
            [d_queries, self.query_w, self.query_sib],
            [whole(d_queries), tile, tile],
            [pl.BlockSpec((self.quarter, self.width // 3), lambda i: (0, i))],
            grid=(3,),
        )[0]

    def dn10(self):
        self.dn1_chip0 = self.dn1(self.d_queries0)
        self.dn1_x0 = swap_x(self.dn1_chip0)

    def dn11(self):
        self.dn1_chip1 = self.dn1(self.d_queries1)
        self.dn1_x1 = swap_x(self.dn1_chip1)

    def kv(self):
        own, sent = self.chain.after(self.kv_own, self.kv_from)
        self.kv_chip = (own + sent.astype(F32)).astype(BF16)
        self.kv_x = swap_x(self.kv_chip)

    def kvpart(self):
        chip, from_x = self.chain.after(self.kv_chip, self.kv_x)
        self.d_kv = (chip.astype(F32) + from_x.astype(F32)).astype(BF16)
        mine = lax.dynamic_slice_in_dim(self.d_kv, self.chip * self.head_dim, self.head_dim, 1)
        normed1 = jnp.concatenate(self.far_normed1, 0)
        part = dot(normed1, mine, TN)
        mine = lax.dynamic_slice_in_dim(part, self.core * self.middle, self.middle, 0)
        other = lax.dynamic_slice_in_dim(part, (1 - self.core) * self.middle, self.middle, 0).astype(BF16)
        self.kv_grad = (mine + swap_core(other).astype(F32)).astype(BF16)

    def out(self, residual, chip, from_x):
        chip, from_x = self.chain.after(chip, from_x)
        own = (residual + (chip.astype(F32) + from_x.astype(F32))).astype(BF16)
        return own, swap_core(own)

    def out0(self):
        self.output_own0, self.output_sib0 = self.out(self.residual0, self.fo_chip0, self.fo_x0)

    def out1(self):
        self.output_own1, self.output_sib1 = self.out(self.residual1, self.fo_chip1, self.fo_x1)

    def input(self, j, on_chip, from_x, d_residual):
        q, w, d = self.quarter, self.width, 2 * self.head_dim
        block = pl.BlockSpec((q, w), lambda i, _: (0, 0))
        own, part = self.chain.call(
            norm1_back_kernel,
            [shape((q, w), BF16), shape((1, w), F32)],
            [self.x, on_chip, from_x, self.d_kv, d_residual, self.kv_w, self.gain1],
            [
                self.rows(1), block, block, pl.BlockSpec((q, d), lambda i, _: (j, 0)), block, whole(self.kv_w),
                whole(self.gain1),
            ],
            [block, pl.BlockSpec((1, w), lambda i, _: (0, 0))],
            scalars=[self.own[j : j + 1]],
            far_ins=(0, 5),
        )
        return own, swap_core(own), part

    def input0(self):
        self.input_own0, self.input_sib0, self.norm1_part0 = self.input(0, self.dn1_chip0, self.dn1_x0, self.d_residual0)

    def input1(self):
        self.input_own1, self.input_sib1, self.norm1_part1 = self.input(1, self.dn1_chip1, self.dn1_x1, self.d_residual1)

    def weave(self):
        ins = [self.output_own0, self.output_own1, self.output_sib0, self.output_sib1]
        ins += [self.input_own0, self.input_own1, self.input_sib0, self.input_sib1]
        self.block_output, self.input_grad = self.chain.direct(
            weave_kernel,
            [shape((self.length, self.width), BF16)] * 2,
            ins,
            scalars=[self.weave_places],
            far=(0, 1),
            scratch=[pltpu.SemaphoreType.DMA((8,))],
        )

    def sums(self):
        d = self.head_dim
        gains = jnp.concatenate([self.norm1_part0 + self.norm1_part1, self.norm2_part0 + self.norm2_part1], 0).reshape(-1, d).astype(BF16)
        self.small = jnp.concatenate([self.kv_grad, gains], 0)
        if self.n_dp & (self.n_dp - 1):
            self.small = lax.psum(self.small, "dp")

    def small_step(self, step):
        if self.n_dp & (self.n_dp - 1):
            return
        while step < self.n_dp:
            (small,) = self.chain.after(self.small)
            self.small = over_dp(small, step, self.n_dp).astype(BF16)
            if step < 4:
                return
            step *= 2

    def sums1(self):
        self.small_step(1)

    def sums2(self):
        self.small_step(2)

    def sums4(self):
        self.small_step(4)

    def sumscore(self):
        (small,) = self.chain.after(self.small)
        self.from_core = swap_core(small)
        self.small = small

    def sumschip(self):
        d, rows = self.head_dim, self.middle
        mine, other = self.chain.after(self.small, self.from_core)
        total = mine[rows:].astype(F32) + other[rows:].astype(F32)
        self.norm_sums = total.reshape(2, self.width)
        halves = jnp.stack([mine[:rows], other[:rows]])
        self.kv_column = jnp.where(self.core == 0, halves, halves[::-1]).reshape(self.width, d)
        self.kv_other = swap_x(self.kv_column)

    def sumsend(self):
        mine, other = self.chain.after(self.kv_column, self.kv_other)
        columns = jnp.stack([mine, other])
        columns = jnp.where(self.chip == 0, columns, columns[::-1])
        self.kv_out = jnp.concatenate([columns[0], columns[1]], 1).astype(F32)

    def E(self):
        (grad,) = self.chain.after((self.late_mine + self.late_from.astype(F32)).astype(BF16))
        self.ring_e.begin(grad)

    def e(self):
        self.ring_e.step()

    def a(self):
        self.ring_a.step()

    def b(self):
        self.ring_b.step()

    def results(self):
        return (
            self.block_output,
            self.input_grad,
            self.norm_sums[0],
            self.query_sum.reshape(self.width, self.cols),
            self.kv_out,
            self.out_sum.reshape(self.cols, self.width),
            self.norm_sums[1],
            self.gate_up_sum.reshape(2, self.width, self.units),
            self.down_sum.reshape(self.units, self.width),
        )


def solution(mesh):
    n_dp = mesh.shape["dp"]

    def local(*args):
        block = Block(n_dp, args)
        for name in ORDER:
            getattr(block, name)()
        return block.results()

    return jax.shard_map(
        local,
        mesh=mesh,
        in_specs=(
            P("dp", None),
            P(),
            P(None, "tensor"),
            P(),
            P("tensor", None),
            P(),
            P(None, None, "tensor"),
            P("tensor", None),
            P("dp", None),
        ),
        out_specs=(
            P("dp", None),
            P("dp", None),
            P(),
            P(None, "tensor"),
            P(),
            P("tensor", None),
            P(),
            P(None, None, "tensor"),
            P("tensor", None),
        ),
        check_vma=False,
    )
```

```python
import functools
import math

import jax
import jax.numpy as jnp
import numpy as np
from jax import lax
from jax.experimental import pallas as pl
from jax.experimental.pallas import tpu as pltpu
from jax.sharding import PartitionSpec as P

WINDOW = 1024
EPSILON = 1e-06
GELU_COEF = 0.7978845608028654
BF16 = jnp.bfloat16
F32 = jnp.float32
NN = (((1,), (0,)), ((), ()))
NT = (((1,), (1,)), ((), ()))
TN = (((0,), (0,)), ((), ()))

RING = (0, 2, 4, 6, 7, 5, 3, 1)

ANY = pl.BlockSpec(memory_space=pl.ANY)
SMEM = pl.BlockSpec(memory_space=pltpu.SMEM)
VMEM = pl.BlockSpec(memory_space=pltpu.VMEM)
MIB = 2**20
COST = pl.CostEstimate(flops=0, bytes_accessed=0, transcendentals=0)

ORDER = " ".join(
    (
        "project attend0 attend1 dhidden0",
        "norm0 dhidden1 ffn0 dnsib0",
        "norm1 ffn1 wide dnown0",
        "down b a dnsib1",
        "a dnown1 b a",
        "nback0 a aback0 nback1",
        "b a aback1 a",
        "late b kv a",
        "fosib1 fosib0 b kvpart",
        "a dn11 E b",
        "e dn10 e b",
        "a e input1 foown0",
        "e a putdown0 b",
        "e input0 sums sums1",
        "e a b sums2",
        "e foown1 e sums4",
        "b out0 putwide0 e",
        "a sumscore e out1",
        "b sumschip e weave",
        "a b a e",
        "sumsend putdown1 e b",
        "putwide1 putlate0 e putlate1",
        "b putwide2",
    )
).split()


def dot(left, right, dims=NN):
    return lax.dot_general(left, right, dims, preferred_element_type=F32)


def swap_core(field):
    return lax.ppermute(field, "tensor", [(i, i ^ 1) for i in range(4)])


def swap_x(field):
    return lax.ppermute(field, "tensor", [(i, i ^ 2) for i in range(4)])


def shape(dims, dtype):
    return jax.ShapeDtypeStruct(dims, dtype)


def whole(array):
    rank = len(array.shape)
    return pl.BlockSpec(array.shape, lambda *_: (0,) * rank)


class Chain:
    def __init__(self):
        self.token = None

    def call(self, body, outs, ins, in_specs, out_specs, grid=(1,), scalars=(), vmem=16, scratch=(), aliases=None, far=(),
        far_ins=(), near=(),
    ):
        tokens = [] if self.token is None else [self.token]
        given, made = len(scalars) + len(ins), len(outs)

        def run(*refs):
            refs = refs[:given] + refs[given + len(tokens) :]
            body(*refs[: given + made], *refs[given + made + 1 :])

        outs = [pltpu.HBM(o.shape, o.dtype) if i in far else o for i, o in enumerate(outs)]
        outs = [pltpu.VMEM(o.shape, o.dtype) if i in near else o for i, o in enumerate(outs)]
        ins = [pltpu.with_memory_space_constraint(a, pltpu.HBM) if i in far_ins else a for i, a in enumerate(ins)]
        *results, self.token = pl.pallas_call(
            run,
            out_shape=outs + [shape((8, 128), F32)],
            grid_spec=pltpu.PrefetchScalarGridSpec(
                num_scalar_prefetch=len(scalars),
                grid=grid,
                in_specs=list(in_specs) + [ANY] * len(tokens),
                out_specs=list(out_specs) + [ANY],
                scratch_shapes=list(scratch),
            ),
            input_output_aliases=aliases or {},
            compiler_params=pltpu.CompilerParams(vmem_limit_bytes=vmem * MIB),
            cost_estimate=COST,
        )(*scalars, *ins, *tokens)
        return results

    def direct(self, body, outs, ins, scalars=(), far_ins=(), far=(), vmem=16, scratch=()):
        tokens = [] if self.token is None else [self.token]
        given, made = len(scalars) + len(ins), len(outs)

        def run(*refs):
            refs = refs[:given] + refs[given + len(tokens) :]
            body(*refs[: given + made], *refs[given + made + 1 :])

        ins = [pltpu.with_memory_space_constraint(a, pltpu.HBM) if i in far_ins else a for i, a in enumerate(ins)]
        in_specs = [SMEM] * len(scalars) + [ANY if i in far_ins else VMEM for i in range(len(ins))]
        *results, self.token = pl.pallas_call(
            run,
            out_shape=[pltpu.HBM(o.shape, o.dtype) if i in far else o for i, o in enumerate(outs)]
            + [shape((8, 128), F32)],
            in_specs=in_specs + [ANY] * len(tokens),
            out_specs=[ANY if i in far else VMEM for i in range(made)] + [ANY],
            scratch_shapes=list(scratch),
            compiler_params=pltpu.CompilerParams(vmem_limit_bytes=vmem * MIB),
            cost_estimate=COST,
        )(*scalars, *ins, *tokens)
        return results

    def after(self, *values):
        *values, self.token = lax.optimization_barrier((*values, self.token))
        return values


def rope(field, table, sign=1.0):
    half = field.shape[1] // 2
    other = pltpu.roll(table, half, 1)
    first = lax.broadcasted_iota(jnp.int32, table.shape, 1) < half
    cosine = jnp.where(first, table, other)
    sine = jnp.where(first, -other, table) * sign
    return field * cosine + pltpu.roll(field, half, 1) * sine


def rms_factor(field):
    return lax.rsqrt(jnp.mean(field * field, axis=1, keepdims=True) + EPSILON)


def start_all(sources, targets, done, first=0):
    copies = [pltpu.make_async_copy(s, t, done.at[first + i]) for i, (s, t) in enumerate(zip(sources, targets))]
    for copy in copies:
        copy.start()
    return copies


def project_kernel(
    core, gain, x, weight, table, keys, values, own0, own1, table0, table1, x_rows, weight_all, table_all, done
):
    quarter = own0.shape[0]
    head_dim = keys.shape[1]

    def rows(block):
        return pl.ds(block * quarter, quarter)

    copies = start_all([x.at[rows(i)] for i in range(4)], [x_rows.at[rows(i)] for i in range(4)], done)
    copies += start_all((weight, table), (weight_all, table_all), done, 4)
    for block in range(4):
        here = rows(block)
        copies[block].wait()
        field = x_rows[here, :].astype(F32)
        normed = (field * rms_factor(field) * gain[...]).astype(BF16)
        if block == 0:
            copies[4].wait()
            copies[5].wait()
        both = dot(normed, weight_all[...])
        keys[here, :] = rope(both[:, :head_dim], table_all[here, :]).astype(BF16)
        values[here, :] = both[:, head_dim:].astype(BF16)
        number, own, angles = (core[0], own0, table0) if block < 2 else (3 - core[0], own1, table1)

        @pl.when(number == block)
        def _():
            own[...] = normed
            angles[...] = table_all[here, :]


def causal(rows, columns, first_row):
    row = lax.broadcasted_iota(jnp.int32, (rows, columns), 0) + first_row
    column = lax.broadcasted_iota(jnp.int32, (rows, columns), 1)
    allowed = column <= row
    if columns > WINDOW:
        allowed = allowed & (row - column < WINDOW)
    return allowed


def attend(numbers, scale, block, normed, keys, values, table, query_w, out_w, part, rot_q, head_out, log_total, arriving):
    quarter = normed.shape[0]
    head_dim = keys.shape[1]
    heads = out_w.shape[0] // head_dim
    for side in range(2):
        arriving[side].wait()
        queries = dot(normed[...], query_w[side])
        for head in range(heads // 2):
            columns = slice(head * head_dim, (head + 1) * head_dim)
            place = side * (heads // 2) + head
            rot_q[:, place * head_dim : (place + 1) * head_dim] = (
                rope(queries[:, columns], table[...]) * scale
            ).astype(BF16)
    for number in numbers:

        @pl.when(block[0] == number)
        def _():
            span = (number + 1) * quarter
            allowed = causal(quarter, span, number * quarter)
            lane = lax.broadcasted_iota(jnp.int32, log_total.shape, 1)

            def two_heads(pair, _):
                for head in (2 * pair, 2 * pair + 1):
                    columns = pl.ds(pl.multiple_of(head * head_dim, head_dim), head_dim)
                    scores = dot(rot_q[:, columns], keys[:span, :], NT)
                    scores = jnp.where(allowed, scores, -1e30)
                    top = jnp.max(scores, axis=1, keepdims=True)
                    weights = jnp.exp(scores - top)
                    total = jnp.sum(weights, axis=1, keepdims=True)
                    probs = (weights * (1.0 / total)).astype(BF16)
                    head_out[:, columns] = dot(probs, values[:span, :]).astype(BF16)
                    log_total[...] = jnp.where(lane == head, top + jnp.log(total), log_total[...])
                return 0

            lax.fori_loop(0, heads // 2, two_heads, 0)

    arriving[2].wait()
    arriving[3].wait()
    part[...] = dot(head_out[...], out_w[...]).astype(BF16)


def attend_kernel(
    numbers, scale, gather, block, places, normed, keys, values, table, query_own, query_sib, out_own, out_sib, *refs
):
    *refs, query_w, out_w, done = refs
    columns = out_own.shape[0]
    weights = start_all(
        (query_own, query_sib, out_own, out_sib),
        (query_w.at[0], query_w.at[1], out_w.at[pl.ds(0, columns)], out_w.at[pl.ds(columns, columns)]),
        done,
    )
    if gather:
        cotangent, gate_up, part, rot_q, head_out, log_total, far_normed, far_keys, far_values, cot0, cot1, near_gate_up = refs
        quarter = normed.shape[0]
        rows = [cotangent.at[pl.ds(pl.multiple_of(places[i] * quarter, 16), quarter)] for i in range(4)]
        halves = [cot.at[pl.ds(i * quarter, quarter)] for cot in (cot0, cot1) for i in range(2)]
        sources, targets = (keys, values, *rows, gate_up), (far_keys, far_values, *halves, near_gate_up)
    else:
        down, part, rot_q, head_out, log_total, far_normed, near_down = refs
        sources, targets = (down,), (near_down,)
    kept = start_all((normed, *sources), (far_normed, *targets), done, 4)
    attend(numbers, scale, block, normed, keys, values, table, query_w, out_w, part, rot_q, head_out, log_total, weights)
    for copy in kept:
        copy.wait()


def attend_back_kernel(scale, order, core, rot_q, log_total, d_heads, keys, values, table, *refs):
    if order == 0:
        d_queries, wide_keys, wide_values = refs
        wide_keys[...] = jnp.zeros_like(wide_keys)
        wide_values[...] = jnp.zeros_like(wide_values)
    else:
        before_keys, before_values, d_queries, kv_own, kv_sib, d_keys, d_values, wide_keys, wide_values = refs
        wide_keys[...] = before_keys[...]
        wide_values[...] = before_values[...]
    quarter = rot_q.shape[0]
    head_dim = keys.shape[1]
    block = core[0] if order == 0 else 3 - core[0]
    for number in (0, 1) if order == 0 else (2, 3):

        @pl.when(block == number)
        def _():
            span = (number + 1) * quarter
            own_table = table[number * quarter : span, :]
            allowed = causal(quarter, span, number * quarter)
            for head in range(rot_q.shape[1] // head_dim):
                columns = slice(head * head_dim, (head + 1) * head_dim)
                query = rot_q[:, columns]
                d_out = d_heads[:, columns]
                scores = dot(query, keys[:span, :], NT) - log_total[:, head : head + 1]
                probs = jnp.exp(jnp.where(allowed, scores, -1e30))
                d_probs = dot(d_out, values[:span, :], NT)
                delta = jnp.sum(probs * d_probs, axis=1, keepdims=True)
                d_scores = (probs * (d_probs - delta)).astype(BF16)
                d_query = dot(d_scores, keys[:span, :]) * scale
                d_queries[:, columns] = rope(d_query, own_table, -1.0).astype(BF16)
                wide_keys[:, :span] += dot(query, d_scores, TN)
                wide_values[:, :span] += dot(d_out, probs.astype(BF16), TN)

    if order == 0:
        return

    def rows_of(number):
        return pl.ds(pl.multiple_of(number * quarter, 16), quarter)

    d_keys[...] = rope(wide_keys[...].T, table[...], -1.0)
    d_values[...] = wide_values[...].T
    for place in range(2):
        rows = slice(place * quarter, (place + 1) * quarter)
        own = rows_of(core[0] if place == 0 else 3 - core[0])
        sib = rows_of(1 - core[0] if place == 0 else 2 + core[0])
        kv_own[rows, :head_dim] = d_keys[own, :]
        kv_own[rows, head_dim:] = d_values[own, :]
        kv_sib[rows, :head_dim] = d_keys[sib, :].astype(BF16)
        kv_sib[rows, head_dim:] = d_values[sib, :].astype(BF16)


def d_hidden_kernel(cotangent, weight, d_hidden):
    d_hidden[...] = dot(cotangent[...], weight[...], NT).astype(BF16)


def norm_kernel(block, x, part, from_x, gain, upper, lower, residual, x_rows, done):
    quarter = part.shape[0]
    here = x.at[pl.ds(pl.multiple_of(block[0] * quarter, 16), quarter)]
    (copy,) = start_all((here,), (x_rows,), done)
    total = part[...].astype(F32) + from_x[...].astype(F32)
    copy.wait()
    value = x_rows[...].astype(F32) + total
    residual[...] = value
    normed = (value * rms_factor(value) * gain[...]).astype(BF16)
    cut = upper.shape[0]
    upper[...] = normed[:cut, :]
    lower[...] = normed[cut:, :]


def ffn_kernel(own0, own1, sib0, sib1, weight, d_hidden, hidden, d_gate, d_up, normed):
    first = 0
    for rows in (own0, own1, sib0, sib1):
        normed[first : first + rows.shape[0], :] = rows[...]
        first += rows.shape[0]
    gate = dot(normed[...], weight[0])
    up = dot(normed[...], weight[1])
    square = gate * gate
    inner = jnp.tanh(GELU_COEF * gate * (1.0 + 0.044715 * square))
    bell = 0.5 * (1.0 + inner)
    gelu = gate * bell
    slope = bell + 0.5 * gate * (1.0 - inner * inner) * (GELU_COEF * (1.0 + 3.0 * 0.044715 * square))
    change = d_hidden[...].astype(F32)
    hidden[...] = (gelu * up).astype(BF16)
    d_gate[...] = (change * up * slope).astype(BF16)
    d_up[...] = (change * gelu).astype(BF16)


def down_grad_kernel(place, left0, left1, right0, right1, out):
    rows, tile = out.shape[1], out.shape[2] // 2
    for i in range(2):
        here = slice(i * tile, (i + 1) * tile)
        total = dot(left0[...], right0[:, here], TN) + dot(left1[...], right1[:, here], TN)
        for number in range(8):
            out[turned(place, number), :, here] = total[number * rows : (number + 1) * rows, :].astype(BF16)


def turned(places, number, side=0):
    return (places[side] - number) & 7


def wide_grad_kernel(tiles, place, left0, left1, gate0, gate1, up0, up1, out):
    rows, columns, chunks = out.shape[1], gate0.shape[1], 8 // tiles
    for side, (right0, right1) in enumerate(((gate0, gate1), (up0, up1))):
        for i in range(tiles):
            here = slice(i * chunks * rows, (i + 1) * chunks * rows)
            total = dot(left0[:, here], right0[...], TN) + dot(left1[:, here], right1[...], TN)
            for chunk in range(chunks):
                part = total[chunk * rows : (chunk + 1) * rows, :].astype(BF16)
                out[turned(place, i * chunks + chunk), :, side * columns : (side + 1) * columns] = part


def rows_kernel(side, tiles, dims, count, *refs):
    refs, joined = refs[:-count], refs[-count:]
    chunks = joined[0].shape[0] * 2 // refs[0].shape[0]
    lefts, weight = refs[: chunks * count], refs[chunks * count]
    *extra, out = refs[chunks * count + 1 :]
    quarter = out.shape[0] // chunks
    own = slice(side * quarter, (side + 1) * quarter)
    for i, target in enumerate(joined):
        for chunk in range(chunks):
            target[chunk * quarter : (chunk + 1) * quarter, :] = lefts[chunks * i + chunk][own, :]
    tile = out.shape[1] // tiles
    for t in range(tiles):
        here = slice(t * tile, (t + 1) * tile)
        total = None
        for i, left in enumerate(joined):
            right = weight[:, here] if dims == NN else weight[i, here, :]
            term = dot(left[...], right, dims)
            total = term if total is None else total + term
        if extra:
            total = total + extra[0][:, here].astype(F32)
        out[:, here] = total.astype(BF16)


def d_normed1_kernel(d_queries, own, sibling, out):
    half = own.shape[1]
    out[...] = (dot(d_queries[:, :half], own[...], NT) + dot(d_queries[:, half:], sibling[...], NT)).astype(BF16)


def norm_back(field, gain, d_normed):
    factor = rms_factor(field)
    scaled = gain * d_normed
    d_gain = jnp.sum(d_normed * field * factor, axis=0, keepdims=True)
    return factor * scaled - field * (factor * factor * factor) * jnp.mean(scaled * field, axis=1, keepdims=True), d_gain


def norm2_back_kernel(
    residual, on_chip, from_x, cotangent, gain, out_own, out_sib, d_residual, d_res_low, d_heads, d_gain
):
    d_normed = on_chip[...].astype(F32) + from_x[...].astype(F32)
    change, d_gain[...] = norm_back(residual[...], gain[...], d_normed)
    total = cotangent[...].astype(F32) + change
    d_residual[...] = total
    low = total.astype(BF16)
    d_res_low[...] = low
    half = out_own.shape[0]
    d_heads[:, :half] = dot(low, out_own[...], NT).astype(BF16)
    d_heads[:, half:] = dot(low, out_sib[...], NT).astype(BF16)


def norm1_back_kernel(block, x, on_chip, from_x, d_kv, d_residual, kv_weight, gain, d_input, d_gain):
    d_normed = (on_chip[...].astype(F32) + from_x[...].astype(F32)) + dot(d_kv[...], kv_weight[...], NT)
    change, d_gain[...] = norm_back(x[...].astype(F32), gain[...], d_normed)
    d_input[...] = (d_residual[...] + change).astype(BF16)


def late_grad_kernel(
    columns, place, normed0, normed1, d_queries0, d_queries1, head_out0, head_out1, d_res_low0, d_res_low1, mine, other
):
    rows = mine.shape[1]
    for side, out in enumerate((mine, other)):
        part = slice(side * columns, (side + 1) * columns)
        query = dot(normed0[...], d_queries0[:, part], TN) + dot(normed1[...], d_queries1[:, part], TN)
        outer = dot(head_out0[:, part], d_res_low0[...], TN) + dot(head_out1[:, part], d_res_low1[...], TN)
        folds = outer.shape[1] // columns
        short = rows // folds
        for number in range(8):
            spot = turned(place, number, side)
            out[spot, :, :columns] = query[number * rows : (number + 1) * rows, :].astype(out.dtype)
            for fold in range(folds):
                out[spot, fold * short : (fold + 1) * short, columns:] = outer[
                    number * short : (number + 1) * short, fold * columns : (fold + 1) * columns
                ].astype(out.dtype)


def weave_kernel(places, *refs):
    *refs, first, second, done = refs
    quarter = refs[0].shape[0]
    copies = []
    for i, source in enumerate(refs):
        target = (first, second)[i // 4]
        rows = pl.ds(pl.multiple_of(places[i % 4] * quarter, 16), quarter)
        copies += start_all((source,), (target.at[rows],), done, i)
    for copy in copies:
        copy.wait()


def assemble_kernel(first, old, count, place, *refs):
    pieces, refs = refs[:count], refs[count + old :]
    *targets, stage, done = refs
    rows, width = pieces[0].shape
    flying = [None, None]
    for i, piece in enumerate(pieces):
        slot = i % 2
        k = (place[0] - first - i) & 7
        for copy in flying[slot] or ():
            copy.wait()
        stage[slot] = piece[...].astype(F32)
        if len(targets) == 1 and targets[0].shape[0] == 2:
            half = width // 2
            moves = [(stage.at[slot, :, n * half : (n + 1) * half], targets[0].at[n, k]) for n in range(2)]
        elif len(targets) == 1:
            moves = [(stage.at[slot], targets[0].at[k])]
        else:
            half = width // 2
            folds = targets[1].shape[2] // half
            short = rows // folds
            moves = [(stage.at[slot, :, :half], targets[0].at[k])]
            moves += [
                (stage.at[slot, n * short : (n + 1) * short, half:], targets[1].at[k, :, n * half : (n + 1) * half])
                for n in range(folds)
            ]
        flying[slot] = [pltpu.make_async_copy(s, t, done.at[slot, n]) for n, (s, t) in enumerate(moves)]
        for copy in flying[slot]:
            copy.start()
    for copies in flying:
        for copy in copies or ():
            copy.wait()


def ring_orders():
    return [RING if tensor % 2 == 0 else RING[::-1] for tensor in range(4)]


def ring_pairs():
    return [
        (order[i] * 4 + tensor, order[(i + 1) % 8] * 4 + tensor) for tensor, order in enumerate(ring_orders()) for i in range(8)
    ]


class Ring:
    def __init__(self, chain, place):
        self.chain, self.place, self.left = chain, place, 0

    def begin(self, field):
        self.field, self.travelling, self.pieces, self.left = field, field[1], [], 14
        self.send()

    def send(self):
        self.arrived = lax.ppermute(self.travelling, ("dp", "tensor"), ring_pairs())

    def step(self):
        if self.left == 0:
            raise ValueError("ring idle")
        self.left -= 1
        number = 14 - self.left
        (self.travelling,) = self.chain.after(self.arrived)
        if number <= 7:
            mine = self.field[(number + 1) % 8].astype(F32)
            (self.travelling,) = self.chain.after((self.travelling.astype(F32) + mine).astype(BF16))
        if number >= 7:
            self.pieces.append(self.travelling)
        if self.left:
            self.send()

    def assemble(self, targets, first, last):
        pieces = self.pieces[first:last]
        old = [t for t in targets if isinstance(t, jax.Array)]
        return self.chain.call(
            functools.partial(assemble_kernel, first, len(old), len(pieces)),
            [shape(t.shape, F32) for t in targets],
            [*pieces, *old],
            [whole(p) for p in pieces] + [ANY] * len(old),
            [ANY] * len(targets),
            scalars=[self.place],
            scratch=[pltpu.VMEM((2,) + pieces[0].shape, F32), pltpu.SemaphoreType.DMA((2, 8))],
            aliases={1 + len(pieces) + i: i for i in range(len(old))},
            vmem=16,
        )


class Whole:
    def __init__(self, chain, place):
        self.chain, self.place = chain, place

    def begin(self, field):
        total = lax.psum(field, "dp")
        self.pieces = [total[i] for i in range(8)]

    def step(self):
        pass

    assemble = Ring.assemble


def over_dp(field, step, n_dp):
    return field.astype(F32) + lax.ppermute(field, "dp", [(i, i ^ step) for i in range(n_dp)]).astype(F32)


class Block:
    def __init__(self, n_dp, args):
        (
            self.x, self.gain1, self.query_w, self.kv_w, self.out_w, self.gain2, self.gate_up_w, self.down_w, self.cot_in,
        ) = args
        self.gain1, self.gain2 = self.gain1[None], self.gain2[None]
        self.n_dp = n_dp
        self.length, self.width = self.x.shape
        self.quarter, self.half = self.length // 4, self.length // 2
        self.head_dim = self.kv_w.shape[1] // 2
        self.cols = self.query_w.shape[1]
        self.units = self.down_w.shape[0]
        self.middle = self.width // 2
        self.scale = 1.0 / math.sqrt(self.head_dim)
        tensor = lax.axis_index("tensor")
        self.core, self.chip = tensor & 1, tensor >> 1
        core = self.core
        self.own = jnp.stack([core, 3 - core])
        self.places = jnp.stack([core, 1 - core, 3 - core, 2 + core])
        self.weave_places = jnp.stack([core, 3 - core, 1 - core, 2 + core])
        self.chain = Chain()
        if n_dp == 8:
            dp = lax.axis_index("dp")
            z, y = dp >> 1, dp & 1
            forward = z + y * (7 - 2 * z)
            place = forward + core * (7 - 2 * forward)
            self.ring_place = jnp.stack([place, 7 - place])
        else:
            self.ring_place = jnp.zeros(2, jnp.int32)
        ring = Ring if n_dp == 8 else Whole
        self.ring_a, self.ring_b, self.ring_e = (ring(self.chain, self.ring_place) for _ in range(3))
        half_dim = self.head_dim // 2
        angle = np.arange(self.length)[:, None] * 10000.0 ** (-2.0 * np.arange(half_dim)[None, :] / self.head_dim)
        self.table = jnp.asarray(np.concatenate([np.cos(angle), np.sin(angle)], 1), F32)
        self.query_sib = swap_core(self.query_w)
        self.out_sib = swap_core(self.out_w)
    def rows(self, table=None):
        if table is None:
            return pl.BlockSpec((self.quarter, self.width), lambda i, *_: (i, 0))
        return pl.BlockSpec((self.quarter, self.width), lambda i, places: (places[i], 0))

    def project(self):
        q, d, w, n = self.quarter, self.head_dim, self.width, self.length
        outs = [shape((n, d), BF16)] * 2 + [shape((q, w), BF16)] * 2 + [shape((q, d), F32)] * 2
        self.keys, self.values, own0, own1, table0, table1 = self.chain.direct(
            project_kernel,
            outs,
            [self.gain1, self.x, self.kv_w, self.table],
            scalars=[self.core[None]],
            far_ins=(1, 2, 3),
            scratch=[
                pltpu.VMEM(self.x.shape, BF16), pltpu.VMEM(self.kv_w.shape, BF16), pltpu.VMEM(self.table.shape, F32),
                pltpu.SemaphoreType.DMA((6,)),
            ],
        )
        self.normed1, self.own_tables, self.far_normed1 = (own0, own1), (table0, table1), []

    def attend(self, j):
        q, w, c = self.quarter, self.width, 2 * self.cols
        ins = [
            self.normed1[j], self.keys, self.values, self.own_tables[j],
            self.query_w, self.query_sib, self.out_w, self.out_sib,
        ]
        blocks = [shape((q, w), BF16), shape((q, c), BF16), shape((q, c), BF16), shape((q, 8), F32)]
        outs = [shape((q, w), BF16)]
        if j == 1:
            more, narrow, rows = [self.cot_in, self.gate_up_w], shape(self.keys.shape, BF16), shape((self.half, w), BF16)
            outs += [narrow, narrow, rows, rows, shape(self.gate_up_w.shape, BF16)]
        else:
            more = [self.down_w]
            outs += [shape(self.down_w.shape, BF16)]
        part, rot_q, head_out, log_total, far_normed, *rest = self.chain.call(
            functools.partial(attend_kernel, (0, 1) if j == 0 else (2, 3), self.scale, j == 1),
            blocks + outs,
            ins + more,
            [whole(a) for a in ins[:4]] + [ANY] * (4 + len(more)),
            [whole(b) for b in blocks] + [ANY] * len(outs),
            scalars=[self.own[j : j + 1], self.places],
            scratch=[
                pltpu.VMEM((2,) + self.query_w.shape, BF16),
                pltpu.VMEM((c, w), BF16),
                pltpu.SemaphoreType.DMA((12,)),
            ],
            far=range(1, 7) if j == 1 else range(1, 5),
            near=range(7, 10) if j == 1 else (5,),
            far_ins=range(4, 10),
            vmem=20,
        )
        self.far_normed1.append(far_normed)
        return part, rot_q, head_out, log_total, rest

    def attend0(self):
        self.part0, self.rot_q0, self.head_out0, self.log0, (self.near_down,) = self.attend(0)
        self.from_x0 = swap_x(self.part0)

    def attend1(self):
        self.part1, self.rot_q1, self.head_out1, self.log1, rest = self.attend(1)
        self.far_keys, self.far_values, cot0, cot1, self.near_gate_up = rest
        self.cot = (cot0, cot1)
        self.from_x1 = swap_x(self.part1)

    def dhidden(self, j):
        return self.chain.direct(
            d_hidden_kernel, [shape((self.half, self.units), BF16)], [self.cot[j], self.near_down]
        )[0]

    def dhidden0(self):
        self.d_hidden0 = self.dhidden(0)

    def dhidden1(self):
        self.d_hidden1 = self.dhidden(1)

    def norm(self, j, part, from_x):
        upper = (self.quarter // 32 + 1) * 16
        outs = [shape((rows, self.width), BF16) for rows in (upper, self.quarter - upper)]
        outs.append(shape((self.quarter, self.width), F32))
        upper, lower, residual = self.chain.direct(
            norm_kernel,
            outs,
            [self.x, part, from_x, self.gain2],
            scalars=[self.own[j : j + 1]],
            far_ins=(0,),
            scratch=[pltpu.VMEM((self.quarter, self.width), BF16), pltpu.SemaphoreType.DMA((1,))],
        )
        return [upper, lower, swap_core(upper), swap_core(lower)], residual

    def norm0(self):
        self.normed2_0, self.residual0 = self.norm(0, self.part0, self.from_x0)

    def norm1(self):
        self.normed2_1, self.residual1 = self.norm(1, self.part1, self.from_x1)

    def ffn(self, normed, d_hidden):
        return self.chain.direct(
            ffn_kernel,
            [shape((self.half, self.units), BF16)] * 3 + [shape((self.half, self.width), BF16)],
            [*normed, self.near_gate_up, d_hidden],
        )

    def ffn0(self):
        self.wide0 = self.ffn(self.normed2_0, self.d_hidden0)

    def ffn1(self):
        self.wide1 = self.ffn(self.normed2_1, self.d_hidden1)
        self.hidden, self.d_gate, self.d_up, self.normed2 = zip(self.wide0, self.wide1)

    def down(self):
        (grad,) = self.chain.direct(
            down_grad_kernel,
            [shape((8, self.units // 8, self.width), BF16)],
            [*self.hidden, *self.cot],
            scalars=[self.ring_place],
        )
        self.ring_a.begin(grad)

    def wide(self):
        (grad,) = self.chain.direct(
            functools.partial(wide_grad_kernel, 2),
            [shape((8, self.width // 8, 2 * self.units), BF16)],
            [*self.normed2, *self.d_gate, *self.d_up],
            scalars=[self.ring_place],
        )
        self.ring_b.begin(grad)

    def put_down(self, first, last):
        target = shape((8, self.units // 8, self.width), F32) if first == 0 else self.down_sum
        (self.down_sum,) = self.ring_a.assemble([target], first, last)

    def putdown0(self):
        self.put_down(0, 4)

    def putdown1(self):
        self.put_down(4, 8)

    def put_wide(self, first, last):
        target = shape((2, 8, self.width // 8, self.units), F32) if first == 0 else self.gate_up_sum
        (self.gate_up_sum,) = self.ring_b.assemble([target], first, last)

    def putwide0(self):
        self.put_wide(0, 4)

    def putwide1(self):
        self.put_wide(4, 7)

    def putwide2(self):
        self.put_wide(7, 8)

    def put_late(self, first, last):
        targets = [shape((8, self.width // 8, self.cols), F32), shape((8, self.cols // 8, self.width), F32)]
        if first:
            targets = [self.query_sum, self.out_sum]
        self.query_sum, self.out_sum = self.ring_e.assemble(targets, first, last)

    def putlate0(self):
        self.put_late(0, 6)

    def putlate1(self):
        self.put_late(6, 8)

    def rows_back(self, side, chunks, lefts, weight, dims, extra):
        rows, count = chunks * self.quarter, len(lefts) // chunks
        return self.chain.direct(
            functools.partial(rows_kernel, side, 3, dims, count),
            [shape((rows, self.width), BF16)],
            [*lefts, weight, *extra],
            scratch=[pltpu.VMEM((rows, self.units), BF16)] * count,
        )[0]

    def dn(self, side, wide, extra=()):
        return self.rows_back(side, 1, wide[1:3], self.near_gate_up, NT, extra)

    def dnsib0(self):
        self.dn_from0 = swap_core(self.dn(1, self.wide0))

    def dnown0(self):
        self.dn_chip0 = self.dn(0, self.wide0, (self.dn_from0,))
        self.dn_x0 = swap_x(self.dn_chip0)

    def dnsib1(self):
        self.dn_from1 = swap_core(self.dn(1, self.wide1))

    def dnown1(self):
        self.dn_chip1 = self.dn(0, self.wide1, (self.dn_from1,))
        self.dn_x1 = swap_x(self.dn_chip1)

    def fo(self, side, wide, extra=()):
        return self.rows_back(side, 1, wide[:1], self.near_down, NN, extra)

    def fosib0(self):
        self.fo_from0 = swap_core(self.fo(1, self.wide0))

    def fosib1(self):
        self.fo_from1 = swap_core(self.fo(1, self.wide1))

    def foown0(self):
        self.fo_chip0 = self.fo(0, self.wide0, (self.fo_from0,))
        self.fo_x0 = swap_x(self.fo_chip0)

    def foown1(self):
        self.fo_chip1 = self.fo(0, self.wide1, (self.fo_from1,))
        self.fo_x1 = swap_x(self.fo_chip1)

    def nback(self, residual, on_chip, from_x, cot):
        q, w, c = self.quarter, self.width, 2 * self.cols
        outs = [shape((q, w), F32), shape((q, w), BF16), shape((q, c), BF16), shape((1, w), F32)]
        ins = [residual, on_chip, from_x, cot, self.gain2, self.out_w, self.out_sib]
        specs = [whole(a) for a in ins]
        specs[3] = pl.BlockSpec((q, w), lambda i: (0, 0))
        return self.chain.call(norm2_back_kernel, outs, ins, specs, [whole(o) for o in outs], far=(0, 1))

    def nback0(self):
        self.d_residual0, self.d_res_low0, self.d_heads0, self.norm2_part0 = self.nback(
            self.residual0, self.dn_chip0, self.dn_x0, self.cot[0]
        )

    def nback1(self):
        self.d_residual1, self.d_res_low1, self.d_heads1, self.norm2_part1 = self.nback(
            self.residual1, self.dn_chip1, self.dn_x1, self.cot[1]
        )

    def aback0(self):
        ins = [self.rot_q0, self.log0, self.d_heads0, self.far_keys, self.far_values, self.table]
        wide = shape((self.head_dim, self.length), F32)
        outs = [shape((self.quarter, 2 * self.cols), BF16), wide, wide]
        self.d_queries0, self.wide_keys, self.wide_values = self.chain.call(
            functools.partial(attend_back_kernel, self.scale, 0),
            outs,
            ins,
            [whole(a) for a in ins],
            [whole(a) for a in outs],
            scalars=[self.core[None]],
            far=(0,),
        )

    def aback1(self):
        ins = [self.rot_q1, self.log1, self.d_heads1, self.far_keys, self.far_values, self.table]
        ins += [self.wide_keys, self.wide_values]
        outs = [
            shape((self.quarter, 2 * self.cols), BF16),
            shape((self.half, 2 * self.head_dim), F32),
            shape((self.half, 2 * self.head_dim), BF16),
        ]
        self.d_queries1, self.kv_own, kv_sib = self.chain.call(
            functools.partial(attend_back_kernel, self.scale, 1),
            outs,
            ins,
            [whole(a) for a in ins],
            [whole(a) for a in outs],
            scalars=[self.core[None]],
            scratch=[pltpu.VMEM((self.length, self.head_dim), F32)] * 2
            + [pltpu.VMEM((self.head_dim, self.length), F32)] * 2,
        )
        self.d_queries = (self.d_queries0, self.d_queries1)
        self.kv_from = swap_core(kv_sib)

    def late(self):
        self.late_mine, other = self.chain.direct(
            functools.partial(late_grad_kernel, self.cols),
            [shape((8, self.width // 8, 2 * self.cols), BF16)] * 2,
            [
                *self.far_normed1, *self.d_queries, self.head_out0, self.head_out1, self.d_res_low0, self.d_res_low1,
            ],
            scalars=[self.ring_place],
        )
        self.late_from = swap_core(other)

    def dn1(self, d_queries):
        tile = pl.BlockSpec((self.width // 3, self.cols), lambda i: (i, 0))
        return self.chain.call(
            d_normed1_kernel,
            [shape((self.quarter, self.width), BF16)],
            [d_queries, self.query_w, self.query_sib],
            [whole(d_queries), tile, tile],
            [pl.BlockSpec((self.quarter, self.width // 3), lambda i: (0, i))],
            grid=(3,),
        )[0]

    def dn10(self):
        self.dn1_chip0 = self.dn1(self.d_queries0)
        self.dn1_x0 = swap_x(self.dn1_chip0)

    def dn11(self):
        self.dn1_chip1 = self.dn1(self.d_queries1)
        self.dn1_x1 = swap_x(self.dn1_chip1)

    def kv(self):
        own, sent = self.chain.after(self.kv_own, self.kv_from)
        self.kv_chip = (own + sent.astype(F32)).astype(BF16)
        self.kv_x = swap_x(self.kv_chip)

    def kvpart(self):
        chip, from_x = self.chain.after(self.kv_chip, self.kv_x)
        self.d_kv = (chip.astype(F32) + from_x.astype(F32)).astype(BF16)
        mine = lax.dynamic_slice_in_dim(self.d_kv, self.chip * self.head_dim, self.head_dim, 1)
        normed1 = jnp.concatenate(self.far_normed1, 0)
        part = dot(normed1, mine, TN)
        mine = lax.dynamic_slice_in_dim(part, self.core * self.middle, self.middle, 0)
        other = lax.dynamic_slice_in_dim(part, (1 - self.core) * self.middle, self.middle, 0).astype(BF16)
        self.kv_grad = (mine + swap_core(other).astype(F32)).astype(BF16)

    def out(self, residual, chip, from_x):
        chip, from_x = self.chain.after(chip, from_x)
        own = (residual + (chip.astype(F32) + from_x.astype(F32))).astype(BF16)
        return own, swap_core(own)

    def out0(self):
        self.output_own0, self.output_sib0 = self.out(self.residual0, self.fo_chip0, self.fo_x0)

    def out1(self):
        self.output_own1, self.output_sib1 = self.out(self.residual1, self.fo_chip1, self.fo_x1)

    def input(self, j, on_chip, from_x, d_residual):
        q, w, d = self.quarter, self.width, 2 * self.head_dim
        block = pl.BlockSpec((q, w), lambda i, _: (0, 0))
        own, part = self.chain.call(
            norm1_back_kernel,
            [shape((q, w), BF16), shape((1, w), F32)],
            [self.x, on_chip, from_x, self.d_kv, d_residual, self.kv_w, self.gain1],
            [
                self.rows(1), block, block, pl.BlockSpec((q, d), lambda i, _: (j, 0)), block, whole(self.kv_w),
                whole(self.gain1),
            ],
            [block, pl.BlockSpec((1, w), lambda i, _: (0, 0))],
            scalars=[self.own[j : j + 1]],
            far_ins=(0, 5),
        )
        return own, swap_core(own), part

    def input0(self):
        self.input_own0, self.input_sib0, self.norm1_part0 = self.input(0, self.dn1_chip0, self.dn1_x0, self.d_residual0)

    def input1(self):
        self.input_own1, self.input_sib1, self.norm1_part1 = self.input(1, self.dn1_chip1, self.dn1_x1, self.d_residual1)

    def weave(self):
        ins = [self.output_own0, self.output_own1, self.output_sib0, self.output_sib1]
        ins += [self.input_own0, self.input_own1, self.input_sib0, self.input_sib1]
        self.block_output, self.input_grad = self.chain.direct(
            weave_kernel,
            [shape((self.length, self.width), BF16)] * 2,
            ins,
            scalars=[self.weave_places],
            far=(0, 1),
            scratch=[pltpu.SemaphoreType.DMA((8,))],
        )

    def sums(self):
        d = self.head_dim
        gains = jnp.concatenate([self.norm1_part0 + self.norm1_part1, self.norm2_part0 + self.norm2_part1], 0).reshape(-1, d).astype(BF16)
        self.small = jnp.concatenate([self.kv_grad, gains], 0)
        if self.n_dp & (self.n_dp - 1):
            self.small = lax.psum(self.small, "dp")

    def small_step(self, step):
        if self.n_dp & (self.n_dp - 1):
            return
        while step < self.n_dp:
            (small,) = self.chain.after(self.small)
            self.small = over_dp(small, step, self.n_dp).astype(BF16)
            if step < 4:
                return
            step *= 2

    def sums1(self):
        self.small_step(1)

    def sums2(self):
        self.small_step(2)

    def sums4(self):
        self.small_step(4)

    def sumscore(self):
        (small,) = self.chain.after(self.small)
        self.from_core = swap_core(small)
        self.small = small

    def sumschip(self):
        d, rows = self.head_dim, self.middle
        mine, other = self.chain.after(self.small, self.from_core)
        total = mine[rows:].astype(F32) + other[rows:].astype(F32)
        self.norm_sums = total.reshape(2, self.width)
        halves = jnp.stack([mine[:rows], other[:rows]])
        self.kv_column = jnp.where(self.core == 0, halves, halves[::-1]).reshape(self.width, d)
        self.kv_other = swap_x(self.kv_column)

    def sumsend(self):
        mine, other = self.chain.after(self.kv_column, self.kv_other)
        columns = jnp.stack([mine, other])
        columns = jnp.where(self.chip == 0, columns, columns[::-1])
        self.kv_out = jnp.concatenate([columns[0], columns[1]], 1).astype(F32)

    def E(self):
        (grad,) = self.chain.after((self.late_mine.astype(F32) + self.late_from.astype(F32)).astype(BF16))
        self.ring_e.begin(grad)

    def e(self):
        self.ring_e.step()

    def a(self):
        self.ring_a.step()

    def b(self):
        self.ring_b.step()

    def results(self):
        return (
            self.block_output,
            self.input_grad,
            self.norm_sums[0],
            self.query_sum.reshape(self.width, self.cols),
            self.kv_out,
            self.out_sum.reshape(self.cols, self.width),
            self.norm_sums[1],
            self.gate_up_sum.reshape(2, self.width, self.units),
            self.down_sum.reshape(self.units, self.width),
        )


def solution(mesh):
    n_dp = mesh.shape["dp"]

    def local(*args):
        block = Block(n_dp, args)
        for name in ORDER:
            getattr(block, name)()
        return block.results()

    return jax.shard_map(
        local,
        mesh=mesh,
        in_specs=(
            P("dp", None),
            P(),
            P(None, "tensor"),
            P(),
            P("tensor", None),
            P(),
            P(None, None, "tensor"),
            P("tensor", None),
            P("dp", None),
        ),
        out_specs=(
            P("dp", None),
            P("dp", None),
            P(),
            P(None, "tensor"),
            P(),
            P("tensor", None),
            P(),
            P(None, None, "tensor"),
            P("tensor", None),
        ),
        check_vma=False,
    )
```
